32 devices in a mesh: dp: 8 (over z, x), expert: 4 (over y, core).
Axes of the slice: x: 2, y: 2, z: 4, core: 2. Of those that a mesh axis runs over, the one named last changes fastest.
Arguments:
- tokens: bfloat16 [4096, 2048], P(('dp', 'expert')), may hold values from -6 to 6
- expert_ids: int32 [4096, 2], P(('dp', 'expert')), may hold values from 0 to 3, all different within a row; in each aligned block of 128 rows (0 to 127, 128 to 255, ...) at most 72 rows name the same one
- gate_probs: float32 [4096, 2], P(('dp', 'expert')), may hold values from 0.2 to 1
- w_gate: bfloat16 [4, 2048, 768], P('expert', 'dp'), may hold values from -0.125 to 0.125
- w_up: bfloat16 [4, 2048, 768], P('expert', 'dp'), may hold values from -0.125 to 0.125
- w_down: bfloat16 [4, 768, 2048], P('expert', 'dp'), may hold values from -0.21875 to 0.21875
- d_out: bfloat16 [4096, 2048], P(('dp', 'expert')), may hold values from -6 to 6
Outputs:
- mixed: bfloat16 [4096, 2048], P(('dp', 'expert'))
- d_tokens: bfloat16 [4096, 2048], P(('dp', 'expert'))
- d_probs: float32 [4096, 2], P(('dp', 'expert'))
- d_w_gate: float32 [4, 2048, 768], P('expert', 'dp')
- d_w_up: float32 [4, 2048, 768], P('expert', 'dp')
- d_w_down: float32 [4, 768, 2048], P('expert', 'dp')
The draws below stay inside these ranges and needn't reach their ends.
Inputs may be any that keep to these rules, and one draw needn't show every extreme that they name: `expert_ids`: in the rows of one device no expert is named more than 72 times, a bound that some block reaches; the 2 ids of a token differ.
All inputs are finite; a program needn't handle non-finite values.
Results may differ from the reference program's by a relative error of at most 0.017.
Values may be sent and summed in bfloat16 or wider, within the bound.
No kernel may reach another device: no remote copies, remote signals or barrier semaphores. Data moves between devices by JAX's collectives and lax.ppermute only.
A program may use at most 128 MiB of HBM per device.

```python
import math
import jax
import jax.numpy as jnp
import numpy as np
from jax import lax

D = 2048
F = 768
TOPK = 2
TOK_DEV = 128
EXPERTS = 4
CAP = 72
TOKENS = 4096
N_EXPERT = 4


def spiked(result, own_key, source, target, shards_of, factor):
    def block_of(dim):
        return (jnp.arange(result.shape[dim]) // (result.shape[dim] // shards_of)).reshape((-1,) + (1,) * (result.ndim - 1 - dim))

    one_side = jax.random.permutation(own_key, shards_of)[block_of(target)]
    far = (block_of(target) + shards_of // 2) % shards_of
    return jnp.where((block_of(source) == one_side) | (block_of(source) == far), factor * result, result)


def level_of(key, shape, pieces, least, high):
    gain, own = 1.0, jax.random.fold_in(key, 6)
    for position, blocks in pieces:
        draws = jnp.exp(jax.random.uniform(jax.random.fold_in(own, position), (blocks,), jnp.float32, least / len(pieces), high / len(pieces)))
        gain = gain * jnp.repeat(draws, shape[position] // blocks).reshape([-1 if axis == position else 1 for axis in range(len(shape))])
    return gain


def assign_block(key, own, number, rows, number_of, top, reach, slope):
    order = jax.random.permutation(key, number_of)
    heavy_load, ordinary = portions_of(number_of, rows * top, reach, slope, True), portions_of(number_of, rows * top, reach, slope, False)
    places = jnp.arange(number_of)

    def named(tallies, turn):
        used = int((tallies > 0).sum())
        fixed = max(1, used // 4)
        shifted = fixed + (places - fixed + turn * (used - fixed)) % max(1, number_of - fixed)
        return jnp.zeros((number_of,), jnp.int32).at[order[jnp.where(places < fixed, places, shifted)]].set(jnp.asarray(tallies, jnp.int32))

    tallies = jnp.where(number % 4 == 0, named(heavy_load, number // 4), named(ordinary, number - number // 4 - 1))
    mixed = jax.random.permutation(jax.random.fold_in(own, 3), number_of)
    source_of, sink = mixed[0:number_of // 2 * 2:2], mixed[1:number_of // 2 * 2:2]
    margin = jnp.minimum(tallies[source_of] - 1, reach - tallies[sink]) // 2
    margin = jnp.where((source_of == order[0]) | (sink == order[0]) | (tallies[sink] == 0), 0, jnp.maximum(margin, 0))
    shifted = jax.random.randint(jax.random.fold_in(own, 4), (number_of // 2,), 0, 1 << 20) % (margin + 1)
    tallies = tallies.at[source_of].add(-shifted).at[sink].add(shifted)
    items = jnp.searchsorted(jnp.cumsum(tallies), jnp.arange(rows * top), side="right").astype(jnp.int32)
    table = items.reshape(top, rows).T
    table = table[jax.random.permutation(jax.random.fold_in(own, 1), rows)]
    turn = jax.random.randint(jax.random.fold_in(own, 2), (rows, 1), 0, top)
    return jnp.take_along_axis(table, (jnp.arange(top)[None, :] + turn) % top, axis=1)


def portions_of(amount, total, reach, skew, full):
    loads = [(1 << 20) // math.isqrt(grade ** skew) + 1 for grade in range(1, amount + 1)]
    largest = reach if full else min(reach, max(-(-total // amount), total * loads[0] // sum(loads)))
    least = 1 if total - largest >= amount - 1 else 0
    given, rest = [largest] + [least] * (amount - 1), total - largest - least * (amount - 1)
    while rest > 0:
        movable = [i for i in range(1, amount) if given[i] < largest] or [i for i in range(1, amount) if given[i] < reach]
        whole, budget = sum([loads[i] for i in movable]), rest
        for i in movable:
            extra = min(reach - given[i], max(1, budget * loads[i] // whole), rest)
            given[i] = given[i] + extra
            rest = rest - extra
    return np.array(given)


def normal_values(rng, dims, scale, bound, shards=(), held_as=jnp.bfloat16):
    result = scale * jax.random.normal(rng, dims, jnp.float32)
    if shards:
        result = result * level_of(rng, dims, shards, -0.22, 0.18)
    return jnp.clip(result, -bound, bound).astype(held_as)


def bell_draw_with(key, shape, spread, bound, split, heavy, held_as=jnp.bfloat16):
    result = spread * jax.random.normal(key, shape, jnp.float32)
    if split:
        result = result * level_of(key, shape, split, -0.22, 0.18)
    return jnp.clip(spiked(result, jax.random.fold_in(key, 3), *heavy), -bound, bound).astype(held_as)


def setup_inputs(seed: int = 0) -> dict:
    arg_keys = jax.random.split(jax.random.key(seed), 8)
    tokens = bell_draw_with(arg_keys[0], (TOKENS, D), 1.0, 6.0, ((0, 32),), (0, 1, 32, 2.75))
    expert_ids_keys = jax.random.split(jax.random.fold_in(arg_keys[1], 1), TOKENS // TOK_DEV)
    expert_ids_turns = jax.random.permutation(jax.random.fold_in(arg_keys[1], 3), TOKENS // TOK_DEV)
    expert_ids = jax.vmap(lambda own, number: assign_block(jax.random.fold_in(arg_keys[1], 2), own, number, TOK_DEV, EXPERTS, TOPK, CAP, 2))(expert_ids_keys, expert_ids_turns).reshape((TOKENS, TOPK))
    gate_probs = jnp.clip(0.2 + 0.8 * jax.random.uniform(arg_keys[2], (TOKENS, TOPK), jnp.float32) ** level_of(arg_keys[2], (TOKENS, TOPK), ((0, 32),), -0.2, 0.2), 0.2, 1.0)
    w_gate = normal_values(arg_keys[3], (EXPERTS, D, F), D ** -0.5, 0.125, ((0, 4), (1, 8)))
    w_up = normal_values(arg_keys[4], (EXPERTS, D, F), D ** -0.5, 0.125, ((0, 4), (1, 8)))
    w_down = normal_values(arg_keys[5], (EXPERTS, F, D), F ** -0.5, 0.21875, ((0, 4), (1, 8)))
    d_out = normal_values(arg_keys[6], (TOKENS, D), 1.0, 6.0, ((0, 32),))
    return {"tokens": tokens, "expert_ids": expert_ids, "gate_probs": gate_probs, "w_gate": w_gate, "w_up": w_up, "w_down": w_down, "d_out": d_out}


def destinations(ids, experts, cap):
    flat = ids.reshape(-1)
    onehot = (flat[:, None] == jnp.arange(experts, dtype=jnp.int32)[None, :]).astype(jnp.int32)
    before = jnp.cumsum(onehot, axis=0) - onehot
    return (flat * cap + jnp.sum(before * onehot, axis=1)).astype(jnp.int32)


def expert_pass(arrived, grad_rows, slot_probs, gate_w, up_w, down_w):
    gate_pre = jnp.dot(arrived, gate_w, preferred_element_type=jnp.float32)
    up_pre = jnp.dot(arrived, up_w, preferred_element_type=jnp.float32)
    sig = jax.nn.sigmoid(gate_pre)
    act = gate_pre * sig
    hidden = (act * up_pre).astype(jnp.bfloat16)
    produced = jnp.dot(hidden, down_w, preferred_element_type=jnp.float32).astype(jnp.bfloat16)
    d_produced = (slot_probs[:, None] * grad_rows.astype(jnp.float32)).astype(jnp.bfloat16)
    d_hidden = lax.dot_general(d_produced, down_w, (((1,), (1,)), ((), ())), preferred_element_type=jnp.float32)
    d_gate = (d_hidden * up_pre * sig * (1.0 + gate_pre * (1.0 - sig))).astype(jnp.bfloat16)
    d_up = (d_hidden * act).astype(jnp.bfloat16)
    d_arrived = (lax.dot_general(d_gate, gate_w, (((1,), (1,)), ((), ())), preferred_element_type=jnp.float32)
                 + lax.dot_general(d_up, up_w, (((1,), (1,)), ((), ())), preferred_element_type=jnp.float32)).astype(jnp.bfloat16)
    contract = (((0,), (0,)), ((), ()))
    part_gate = lax.dot_general(arrived, d_gate, contract, preferred_element_type=jnp.float32).astype(jnp.bfloat16)
    part_up = lax.dot_general(arrived, d_up, contract, preferred_element_type=jnp.float32).astype(jnp.bfloat16)
    part_down = lax.dot_general(hidden, d_produced, contract, preferred_element_type=jnp.float32).astype(jnp.bfloat16)
    return produced, d_arrived, part_gate, part_up, part_down


def reference(tokens, expert_ids, gate_probs, w_gate, w_up, w_down, d_out):
    members = N_EXPERT
    groups = TOKENS // (TOK_DEV * members)
    slots = EXPERTS * CAP
    x_all = tokens.reshape(groups, members, TOK_DEV, D)
    id_all = expert_ids.reshape(groups, members, TOK_DEV, TOPK)
    p_all = gate_probs.reshape(groups, members, TOK_DEV, TOPK)
    dy_all = d_out.reshape(groups, members, TOK_DEV, D)

    def place(rows, where):
        return jnp.zeros((slots, rows.shape[-1]), rows.dtype).at[where].set(rows)

    def place_flat(values, where):
        return jnp.zeros((slots,), values.dtype).at[where].set(values)

    def by_expert(sent):
        return sent.reshape(members, EXPERTS, CAP, D).transpose(1, 0, 2, 3).reshape(EXPERTS, members * CAP, D)

    def by_source(rows):
        return rows.reshape(EXPERTS, members, CAP, D).transpose(1, 0, 2, 3).reshape(members, slots, D)

    def group_step(carry, items):
        x_grp, id_grp, p_grp, dy_grp = items
        dest = jax.vmap(lambda ids: destinations(ids, EXPERTS, CAP))(id_grp)
        sent_x = jax.vmap(place)(jnp.repeat(x_grp, TOPK, axis=1), dest)
        sent_dy = jax.vmap(place)(jnp.repeat(dy_grp, TOPK, axis=1), dest)
        sent_p = jax.vmap(place_flat)(p_grp.reshape(members, TOK_DEV * TOPK), dest)
        probs_e = sent_p.reshape(members, EXPERTS, CAP).transpose(1, 0, 2).reshape(EXPERTS, members * CAP)
        produced, d_arrived, part_gate, part_up, part_down = lax.map(
            lambda a: expert_pass(*a), (by_expert(sent_x), by_expert(sent_dy), probs_e, w_gate, w_up, w_down))
        picked = jax.vmap(lambda r, w: r[w])(by_source(produced), dest)
        picked = picked.reshape(members, TOK_DEV, TOPK, D).astype(jnp.float32)
        mixed = jnp.sum(p_grp[..., None] * picked, axis=2).astype(jnp.bfloat16)
        d_probs = jnp.sum(dy_grp.astype(jnp.float32)[:, :, None, :] * picked, axis=3)
        back = jax.vmap(lambda r, w: r[w])(by_source(d_arrived), dest)
        d_tok = jnp.sum(back.reshape(members, TOK_DEV, TOPK, D).astype(jnp.float32), axis=2).astype(jnp.bfloat16)
        carry = (carry[0] + part_gate.astype(jnp.float32), carry[1] + part_up.astype(jnp.float32),
                 carry[2] + part_down.astype(jnp.float32))
        return carry, (mixed, d_tok, d_probs)

    init = (jnp.zeros((EXPERTS, D, F), jnp.float32), jnp.zeros((EXPERTS, D, F), jnp.float32),
            jnp.zeros((EXPERTS, F, D), jnp.float32))
    sums, outs = lax.scan(group_step, init, (x_all, id_all, p_all, dy_all))
    mixed = outs[0].reshape(TOKENS, D)
    d_tokens = outs[1].reshape(TOKENS, D)
    d_probs = outs[2].reshape(TOKENS, TOPK)
    return mixed, d_tokens, d_probs, sums[0], sums[1], sums[2]
```

```python
import jax
import jax.numpy as jnp
from jax import lax
from jax.sharding import PartitionSpec as P

BF = jnp.bfloat16
F32 = jnp.float32
BOTH = ("dp", "expert")


def dot(a, b, dims=((1,), (0,))):
    return lax.dot_general(a, b, (dims, ((), ())), preferred_element_type=F32)


class Grid:
    def __init__(self):
        self.dps, self.experts = lax.axis_size("dp"), lax.axis_size("expert")
        self.zs, self.qs = self.dps // 2, self.experts // 2
        dp, ex = lax.axis_index("dp"), lax.axis_index("expert")
        self.z, self.x, self.q, self.c = dp // 2, dp % 2, ex // 2, ex % 2
        self.z_groups = [[z * 2 + x for z in range(self.zs)] for x in range(2)]

    def send(self, value, move):
        pairs = []
        for z in range(self.zs):
            for x in range(2):
                for q in range(self.qs):
                    for c in range(2):
                        to = move(z, x, q, c)
                        if 0 <= to[0] < self.zs:
                            pairs.append((self.flat(z, x, q, c), self.flat(*to)))
        return lax.ppermute(value, BOTH, pairs)

    def flat(self, z, x, q, c):
        return (z * 2 + x) * self.experts + q * 2 + c


def local(tokens, expert_ids, gate_probs, w_gate, w_up, w_down, d_out):
    g = Grid()
    rows, topk = expert_ids.shape
    width = tokens.shape[1]
    hidden_width = w_gate.shape[2]
    half = hidden_width // 2
    experts = g.experts
    cap = rows * topk * 9 // (8 * experts)
    slots = experts * cap
    first = g.c == 0

    block = hidden_width // g.dps
    part = block // 2
    place = jnp.arange(hidden_width, dtype=jnp.int32)
    in_half = place % half
    source_col = (in_half // part) * block + ((place // half) ^ g.x) * part + in_half % part
    shuffle = (jnp.arange(hidden_width, dtype=jnp.int32)[:, None] == source_col[None, :]).astype(BF)

    def out_a(z, x, q, c):
        return z, c, q, x

    def out_b(z, x, q, c):
        return z, c, q, 1 - x

    def back_a(z, x, q, c):
        return z, c, q, x

    def back_b(z, x, q, c):
        return z, 1 - c, q, x

    def spread(part_a, part_b):
        got_a, got_b = g.send(part_a, out_a), g.send(part_b, out_b)
        return jnp.concatenate([jnp.where(first, got_a, got_b), jnp.where(first, got_b, got_a)], axis=0)

    def unspread(both):
        n = both.shape[0] // 2
        low, high = both[:n], both[n:]
        return g.send(jnp.where(first, low, high), back_a), g.send(jnp.where(first, high, low), back_b)

    gate_cols = dot(w_gate[0], shuffle).astype(BF)
    up_cols = dot(w_up[0], shuffle).astype(BF)
    gate_up_shard = spread(
        jnp.concatenate([gate_cols[:, :half], up_cols[:, :half]], axis=1),
        jnp.concatenate([gate_cols[:, half:], up_cols[:, half:]], axis=1),
    )
    down_low, down_high = w_down[0, :part], w_down[0, part:]
    even = g.x == 0
    down_shard = spread(jnp.where(even, down_low, down_high), jnp.where(even, down_high, down_low))
    gate_up = lax.all_gather(gate_up_shard, "dp", axis=0, tiled=True, axis_index_groups=g.z_groups)
    down = lax.all_gather(down_shard, "dp", axis=0, tiled=True, axis_index_groups=g.z_groups)

    expert_iota = jnp.arange(experts, dtype=jnp.int32)
    chosen = expert_ids[:, :, None] == expert_iota
    named = jnp.any(chosen, axis=1).astype(BF)
    token_iota = jnp.arange(rows, dtype=jnp.int32)
    earlier = (token_iota[:, None] > token_iota[None, :]).astype(BF)
    before = dot(earlier, named)
    slot = jnp.sum(jnp.where(chosen, before[:, None, :], 0.0), axis=2).astype(jnp.int32)
    relative = ((expert_ids // 2 - g.q + g.qs) % g.qs) * 2 + ((expert_ids % 2) ^ g.x)
    dest = relative * cap + slot
    slot_iota = jnp.arange(slots, dtype=jnp.int32)
    pair = dest[:, :, None] == slot_iota
    placing = jnp.any(pair, axis=1).astype(BF)
    weighted = jnp.sum(jnp.where(pair, gate_probs[:, :, None], 0.0), axis=1)
    slot_probs = jnp.sum(weighted, axis=0)

    def member(r, sign):
        def move(z, x, q, c):
            return z, x ^ (r % 2), (q + sign * (r // 2)) % g.qs, c

        return move

    def other_core(z, x, q, c):
        return z, x, q, 1 - c

    def dispatch(sent):
        got = [sent[:cap]] + [g.send(sent[r * cap:(r + 1) * cap], member(r, 1)) for r in range(1, experts)]
        mine = jnp.concatenate(got, axis=0)
        return jnp.concatenate([mine, g.send(mine, other_core)], axis=0)

    def give_back(partial):
        other = g.send(partial[slots:].astype(BF), other_core)
        mine = (partial[:slots] + other.astype(F32)).astype(BF)
        got = [mine[:cap]] + [g.send(mine[r * cap:(r + 1) * cap], member(r, -1)) for r in range(1, experts)]
        return jnp.concatenate(got, axis=0)

    arrived = dispatch(dot(placing, tokens, ((0,), (0,))).astype(BF))
    d_produced = dispatch((slot_probs[:, None] * dot(placing, d_out, ((0,), (0,)))).astype(BF))

    pre = dot(arrived, gate_up)
    gate_pre, up_pre = pre[:, :half], pre[:, half:]
    sig = jax.nn.sigmoid(gate_pre)
    act = gate_pre * sig
    hidden = (act * up_pre).astype(BF)

    def scatter(partial):
        return lax.psum_scatter(
            partial.astype(BF), "dp", scatter_dimension=0, tiled=True, axis_index_groups=g.z_groups
        ).astype(BF)

    down_grad = scatter(dot(hidden, d_produced, ((0,), (0,))))
    returned = give_back(dot(hidden, down))

    d_hidden = dot(d_produced, down, ((1,), (1,)))
    d_gate = (d_hidden * up_pre * sig * (1.0 + gate_pre * (1.0 - sig))).astype(BF)
    d_up = (d_hidden * act).astype(BF)
    d_both = jnp.concatenate([d_gate, d_up], axis=1)
    gate_up_grad = scatter(dot(arrived, d_both, ((0,), (0,))))
    back_rows = give_back(dot(d_both, gate_up, ((1,), (1,))))

    high = lax.reduce_precision(weighted, 8, 7)
    mixed = (dot(high.astype(BF), returned) + dot((weighted - high).astype(BF), returned)).astype(BF)
    products = dot(d_out, returned, ((1,), (1,)))
    d_probs = jnp.sum(jnp.where(pair, products[:, None, :], 0.0), axis=2)
    d_tokens = dot(placing, back_rows).astype(BF)

    down_a, down_b = unspread(down_grad)
    d_w_down = jnp.where(
        even, jnp.concatenate([down_a, down_b], axis=0), jnp.concatenate([down_b, down_a], axis=0)
    ).astype(F32)[None]
    both_a, both_b = unspread(gate_up_grad)
    d_w_gate = dot(jnp.concatenate([both_a[:, :half], both_b[:, :half]], axis=1), shuffle, ((1,), (1,)))[None]
    d_w_up = dot(jnp.concatenate([both_a[:, half:], both_b[:, half:]], axis=1), shuffle, ((1,), (1,)))[None]
    return (mixed, d_tokens, d_probs, d_w_gate, d_w_up, d_w_down)


def solution(mesh):
    rows = P(("dp", "expert"), None)
    weight = P("expert", "dp", None)
    return jax.shard_map(
        local,
        mesh=mesh,
        in_specs=(rows, rows, rows, weight, weight, weight, rows),
        out_specs=(rows, rows, rows, weight, weight, weight),
        check_vma=False,
    )
```

```python
import jax
import jax.numpy as jnp
from jax import lax
from jax.sharding import PartitionSpec as P

BF = jnp.bfloat16
F32 = jnp.float32
BOTH = ("dp", "expert")


def dot(a, b, dims=((1,), (0,))):
    return lax.dot_general(a, b, (dims, ((), ())), preferred_element_type=F32)


def added(*terms):
    return sum(t.astype(F32) for t in terms).astype(BF)


class Grid:
    def __init__(self):
        self.dps, self.experts = lax.axis_size("dp"), lax.axis_size("expert")
        self.zs, self.qs = self.dps // 2, self.experts // 2
        dp, ex = lax.axis_index("dp"), lax.axis_index("expert")
        self.z, self.x, self.q, self.c = dp // 2, dp % 2, ex // 2, ex % 2

    def send(self, value, move):
        pairs = []
        for z in range(self.zs):
            for x in range(2):
                for q in range(self.qs):
                    for c in range(2):
                        to = move(z, x, q, c)
                        if to is not None:
                            pairs.append((self.flat(z, x, q, c), self.flat(*to)))
        return lax.ppermute(value, BOTH, pairs)

    def flat(self, z, x, q, c):
        return (z * 2 + x) * self.experts + q * 2 + c

    def step(self, value, by, senders):
        return self.send(value, lambda z, x, q, c: (z + by, x, q, c) if z in senders else None)

    def gather(self, shard):
        up, down = [shard], [shard]
        for s in range(1, self.zs):
            up.append(self.step(up[-1], 1, range(s - 1, self.zs - 1)))
            down.append(self.step(down[-1], -1, range(1, self.zs - s + 1)))
        return up, down

    def rotated(self, shard):
        up, down = self.gather(shard)
        blocks = [shard]
        for s in range(1, self.zs):
            blocks.append(jnp.where(self.z + s < self.zs, down[s], up[self.zs - s]))
        return blocks

    def straight(self, shard):
        up, down = self.gather(shard)
        blocks = []
        for j in range(self.zs):
            block = shard
            for s in range(1, self.zs):
                if j + s < self.zs:
                    block = jnp.where(self.z == j + s, up[s], block)
                if j - s >= 0:
                    block = jnp.where(self.z == j - s, down[s], block)
            blocks.append(block)
        return blocks

    def scatter(self, block):
        n = self.zs
        up = self.step(block(n - 1), 1, range(0, 1))
        down = self.step(block(1 - n), -1, range(n - 1, n))
        for r in range(2, n):
            up = self.step(added(block(n - r), up), 1, range(0, r))
            down = self.step(added(block(r - n), down), -1, range(n - r, n))
        return added(block(0), up, down)


def local(tokens, expert_ids, gate_probs, w_gate, w_up, w_down, d_out):
    g = Grid()
    rows, topk = expert_ids.shape
    width = tokens.shape[1]
    hidden_width = w_gate.shape[2]
    half = hidden_width // 2
    experts = g.experts
    cap = rows * topk * 9 // (8 * experts)
    slots = experts * cap
    first = g.c == 0

    block = hidden_width // g.dps
    part = block // 2
    place = jnp.arange(hidden_width, dtype=jnp.int32)
    in_half = place % half
    source_col = (in_half // part) * block + ((place // half) ^ g.x) * part + in_half % part
    shuffle = (jnp.arange(hidden_width, dtype=jnp.int32)[:, None] == source_col[None, :]).astype(BF)

    def out_a(z, x, q, c):
        return z, c, q, x

    def out_b(z, x, q, c):
        return z, c, q, 1 - x

    def back_a(z, x, q, c):
        return z, c, q, x

    def back_b(z, x, q, c):
        return z, 1 - c, q, x

    def spread(part_a, part_b):
        got_a, got_b = g.send(part_a, out_a), g.send(part_b, out_b)
        return jnp.concatenate([jnp.where(first, got_a, got_b), jnp.where(first, got_b, got_a)], axis=0)

    def unspread(both):
        n = both.shape[0] // 2
        low, high = both[:n], both[n:]
        return g.send(jnp.where(first, low, high), back_a), g.send(jnp.where(first, high, low), back_b)

    gate_cols = dot(w_gate[0], shuffle).astype(BF)
    up_cols = dot(w_up[0], shuffle).astype(BF)
    gate_up_shard = spread(
        jnp.concatenate([gate_cols[:, :half], up_cols[:, :half]], axis=1),
        jnp.concatenate([gate_cols[:, half:], up_cols[:, half:]], axis=1),
    )
    down_low, down_high = w_down[0, :part], w_down[0, part:]
    even = g.x == 0
    down_shard = spread(jnp.where(even, down_low, down_high), jnp.where(even, down_high, down_low))
    gate_up = jnp.concatenate(g.rotated(gate_up_shard), axis=0)
    down = jnp.concatenate(g.straight(down_shard), axis=0)

    expert_iota = jnp.arange(experts, dtype=jnp.int32)
    chosen = expert_ids[:, :, None] == expert_iota
    named = jnp.any(chosen, axis=1).astype(BF)
    token_iota = jnp.arange(rows, dtype=jnp.int32)
    earlier = (token_iota[:, None] > token_iota[None, :]).astype(BF)
    before = dot(earlier, named)
    slot = jnp.sum(jnp.where(chosen, before[:, None, :], 0.0), axis=2).astype(jnp.int32)
    relative = ((expert_ids // 2 - g.q + g.qs) % g.qs) * 2 + ((expert_ids % 2) ^ g.x)
    dest = relative * cap + slot
    slot_iota = jnp.arange(slots, dtype=jnp.int32)
    pair = dest[:, :, None] == slot_iota
    placing = jnp.any(pair, axis=1).astype(BF)
    weighted = jnp.sum(jnp.where(pair, gate_probs[:, :, None], 0.0), axis=1)
    slot_probs = jnp.sum(weighted, axis=0)

    def member(r, sign):
        def move(z, x, q, c):
            return z, x ^ (r % 2), (q + sign * (r // 2)) % g.qs, c

        return move

    def other_core(z, x, q, c):
        return z, x, q, 1 - c

    def dispatch(sent):
        got = [sent[:cap]] + [g.send(sent[r * cap:(r + 1) * cap], member(r, 1)) for r in range(1, experts)]
        mine = jnp.concatenate(got, axis=0)
        return jnp.concatenate([mine, g.send(mine, other_core)], axis=0)

    def give_back(partial):
        other = g.send(partial[slots:].astype(BF), other_core)
        mine = (partial[:slots] + other.astype(F32)).astype(BF)
        got = [mine[:cap]] + [g.send(mine[r * cap:(r + 1) * cap], member(r, -1)) for r in range(1, experts)]
        return jnp.concatenate(got, axis=0)

    line_width = width // g.zs
    turned = lax.dynamic_slice(jnp.concatenate([tokens, tokens], axis=1), (0, g.z * line_width), (rows, width))
    arrived = dispatch(dot(placing, turned, ((0,), (0,))).astype(BF))
    d_produced = dispatch((slot_probs[:, None] * dot(placing, d_out, ((0,), (0,)))).astype(BF))

    pre = dot(arrived, gate_up)
    gate_pre, up_pre = pre[:, :half], pre[:, half:]
    sig = jax.nn.sigmoid(gate_pre)
    act = gate_pre * sig
    hidden = (act * up_pre).astype(BF)

    down_part = dot(hidden, d_produced, ((0,), (0,))).astype(BF)
    down_rows = 2 * part
    down_grad = g.scatter(lambda k: lax.dynamic_slice_in_dim(down_part, (g.z + k) * down_rows, down_rows))
    returned = give_back(dot(hidden, down))

    d_hidden = dot(d_produced, down, ((1,), (1,)))
    d_gate = (d_hidden * up_pre * sig * (1.0 + gate_pre * (1.0 - sig))).astype(BF)
    d_up = (d_hidden * act).astype(BF)
    d_both = jnp.concatenate([d_gate, d_up], axis=1)
    both_part = dot(arrived, d_both, ((0,), (0,))).astype(BF)
    gate_up_grad = g.scatter(lambda k: both_part[(k % g.zs) * line_width:(k % g.zs + 1) * line_width])
    back_rows = give_back(dot(d_both, gate_up, ((1,), (1,))))

    high = lax.reduce_precision(weighted, 8, 7)
    mixed = (dot(high.astype(BF), returned) + dot((weighted - high).astype(BF), returned)).astype(BF)
    products = dot(d_out, returned, ((1,), (1,)))
    d_probs = jnp.sum(jnp.where(pair, products[:, None, :], 0.0), axis=2)
    d_turned = dot(placing, back_rows).astype(BF)
    d_tokens = lax.dynamic_slice(
        jnp.concatenate([d_turned, d_turned], axis=1), (0, (g.zs - g.z) * line_width), (rows, width)
    )

    down_a, down_b = unspread(down_grad)
    d_w_down = jnp.where(
        even, jnp.concatenate([down_a, down_b], axis=0), jnp.concatenate([down_b, down_a], axis=0)
    ).astype(F32)[None]
    both_a, both_b = unspread(gate_up_grad)
    d_w_gate = dot(jnp.concatenate([both_a[:, :half], both_b[:, :half]], axis=1), shuffle, ((1,), (1,)))[None]
    d_w_up = dot(jnp.concatenate([both_a[:, half:], both_b[:, half:]], axis=1), shuffle, ((1,), (1,)))[None]
    return (mixed, d_tokens, d_probs, d_w_gate, d_w_up, d_w_down)


def solution(mesh):
    rows = P(("dp", "expert"), None)
    weight = P("expert", "dp", None)
    return jax.shard_map(
        local,
        mesh=mesh,
        in_specs=(rows, rows, rows, weight, weight, weight, rows),
        out_specs=(rows, rows, rows, weight, weight, weight),
        check_vma=False,
    )
```

```python
import jax
import jax.numpy as jnp
from jax import lax
from jax.sharding import PartitionSpec as P

BF = jnp.bfloat16
F32 = jnp.float32
BOTH = ("dp", "expert")


def dot(a, b, dims=((1,), (0,))):
    return lax.dot_general(a, b, (dims, ((), ())), preferred_element_type=F32)


def tie(value, *others):
    return lax.optimization_barrier((value,) + others)[0]


def added(*terms):
    return sum(t.astype(F32) for t in terms).astype(BF)


class Grid:
    def __init__(self):
        self.dps, self.experts = lax.axis_size("dp"), lax.axis_size("expert")
        self.zs, self.qs = self.dps // 2, self.experts // 2
        dp, ex = lax.axis_index("dp"), lax.axis_index("expert")
        self.z, self.x, self.q, self.c = dp // 2, dp % 2, ex // 2, ex % 2

    def send(self, value, move):
        pairs = []
        for z in range(self.zs):
            for x in range(2):
                for q in range(self.qs):
                    for c in range(2):
                        to = move(z, x, q, c)
                        if to is not None:
                            pairs.append((self.flat(z, x, q, c), self.flat(*to)))
        return lax.ppermute(value, BOTH, pairs)

    def flat(self, z, x, q, c):
        return (z * 2 + x) * self.experts + q * 2 + c

    def step(self, value, by, senders):
        return self.send(value, lambda z, x, q, c: (z + by, x, q, c) if z in senders else None)

    def gather(self, shard):
        up, down = [shard], [shard]
        for s in range(1, self.zs):
            up.append(self.step(up[-1], 1, range(s - 1, self.zs - 1)))
            down.append(self.step(down[-1], -1, range(1, self.zs - s + 1)))
        return up, down

    def rotated(self, shard, up, down):
        blocks = [shard]
        for s in range(1, self.zs):
            blocks.append(jnp.where(self.z + s < self.zs, down[s], up[self.zs - s]))
        return blocks

    def straight(self, shard, up, down):
        blocks = []
        for j in range(self.zs):
            block = shard
            for s in range(1, self.zs):
                if j + s < self.zs:
                    block = jnp.where(self.z == j + s, up[s], block)
                if j - s >= 0:
                    block = jnp.where(self.z == j - s, down[s], block)
            blocks.append(block)
        return blocks

    def scatter(self, block):
        n = self.zs
        up = self.step(block(n - 1), 1, range(0, 1))
        down = self.step(block(1 - n), -1, range(n - 1, n))
        for r in range(2, n):
            if r == 2:
                early = up, down
            up = self.step(added(block(n - r), up), 1, range(0, r))
            down = self.step(added(block(r - n), down), -1, range(n - r, n))
        return added(block(0), up, down), early


def local(tokens, expert_ids, gate_probs, w_gate, w_up, w_down, d_out):
    g = Grid()
    rows, topk = expert_ids.shape
    width = tokens.shape[1]
    hidden_width = w_gate.shape[2]
    half = hidden_width // 2
    experts = g.experts
    cap = rows * topk * 9 // (8 * experts)
    slots = experts * cap
    first = g.c == 0

    block = hidden_width // g.dps
    part = block // 2
    place = jnp.arange(hidden_width, dtype=jnp.int32)
    in_half = place % half
    source_col = (in_half // part) * block + ((place // half) ^ g.x) * part + in_half % part
    shuffle = (jnp.arange(hidden_width, dtype=jnp.int32)[:, None] == source_col[None, :]).astype(BF)

    def out_a(z, x, q, c):
        return z, c, q, x

    def out_b(z, x, q, c):
        return z, c, q, 1 - x

    def back_a(z, x, q, c):
        return z, c, q, x

    def back_b(z, x, q, c):
        return z, 1 - c, q, x

    def spread(part_a, part_b):
        got_a, got_b = g.send(part_a, out_a), g.send(part_b, out_b)
        return jnp.concatenate([jnp.where(first, got_a, got_b), jnp.where(first, got_b, got_a)], axis=0)

    def unspread(both):
        n = both.shape[0] // 2
        low, high = both[:n], both[n:]
        return g.send(jnp.where(first, low, high), back_a), g.send(jnp.where(first, high, low), back_b)

    gate_cols = dot(w_gate[0], shuffle).astype(BF)
    up_cols = dot(w_up[0], shuffle).astype(BF)
    part_a = jnp.concatenate([gate_cols[:, :half], up_cols[:, :half]], axis=1)
    part_b = jnp.concatenate([gate_cols[:, half:], up_cols[:, half:]], axis=1)
    gate_up_shard = spread(part_a, part_b)
    tokens, d_out = tie(tokens, part_a, part_b), tie(d_out, part_a, part_b)
    w_down_late = tie(w_down[0], gate_up_shard)
    down_low, down_high = w_down_late[:part], w_down_late[part:]
    even = g.x == 0
    down_shard = spread(jnp.where(even, down_low, down_high), jnp.where(even, down_high, down_low))
    up, dn = g.gather(gate_up_shard)
    gate_up = jnp.concatenate(g.rotated(gate_up_shard, up, dn), axis=0)
    down_shard = tie(down_shard, up[-2], dn[-2])
    down = jnp.concatenate(g.straight(down_shard, *g.gather(down_shard)), axis=0)

    expert_iota = jnp.arange(experts, dtype=jnp.int32)
    chosen = expert_ids[:, :, None] == expert_iota
    named = jnp.any(chosen, axis=1).astype(BF)
    token_iota = jnp.arange(rows, dtype=jnp.int32)
    earlier = (token_iota[:, None] > token_iota[None, :]).astype(BF)
    before = dot(earlier, named)
    slot = jnp.sum(jnp.where(chosen, before[:, None, :], 0.0), axis=2).astype(jnp.int32)
    relative = ((expert_ids // 2 - g.q + g.qs) % g.qs) * 2 + ((expert_ids % 2) ^ g.x)
    dest = relative * cap + slot
    slot_iota = jnp.arange(slots, dtype=jnp.int32)
    pair = dest[:, :, None] == slot_iota
    placing = jnp.any(pair, axis=1).astype(BF)
    weighted = jnp.sum(jnp.where(pair, gate_probs[:, :, None], 0.0), axis=1)
    slot_probs = jnp.sum(weighted, axis=0)

    def member(r, sign):
        def move(z, x, q, c):
            return z, x ^ (r % 2), (q + sign * (r // 2)) % g.qs, c

        return move

    def other_core(z, x, q, c):
        return z, x, q, 1 - c

    def dispatch(sent):
        got = [sent[:cap]] + [g.send(sent[r * cap:(r + 1) * cap], member(r, 1)) for r in range(1, experts)]
        mine = jnp.concatenate(got, axis=0)
        return jnp.concatenate([mine, g.send(mine, other_core)], axis=0)

    def give_back(partial):
        other = g.send(partial[slots:].astype(BF), other_core)
        mine = (partial[:slots] + other.astype(F32)).astype(BF)
        got = [mine[:cap]] + [g.send(mine[r * cap:(r + 1) * cap], member(r, -1)) for r in range(1, experts)]
        return jnp.concatenate(got, axis=0)

    line_width = width // g.zs
    turned = lax.dynamic_slice(jnp.concatenate([tokens, tokens], axis=1), (0, g.z * line_width), (rows, width))
    arrived = dispatch(dot(placing, turned, ((0,), (0,))).astype(BF))
    d_produced = dispatch((slot_probs[:, None] * dot(placing, d_out, ((0,), (0,)))).astype(BF))

    pre = dot(arrived, gate_up)
    gate_pre, up_pre = pre[:, :half], pre[:, half:]
    sig = jax.nn.sigmoid(gate_pre)
    act = gate_pre * sig
    hidden = (act * up_pre).astype(BF)

    down_part = dot(hidden, d_produced, ((0,), (0,))).astype(BF)
    down_rows = 2 * part
    down_grad, first_sums = g.scatter(lambda k: lax.dynamic_slice_in_dim(down_part, (g.z + k) * down_rows, down_rows))

    d_hidden = dot(tie(d_produced, *first_sums), down, ((1,), (1,)))
    d_gate = (d_hidden * up_pre * sig * (1.0 + gate_pre * (1.0 - sig))).astype(BF)
    d_up = (d_hidden * act).astype(BF)
    d_both = jnp.concatenate([d_gate, d_up], axis=1)
    both_part = dot(arrived, d_both, ((0,), (0,))).astype(BF)
    gate_up_grad, early = g.scatter(lambda k: both_part[(k % g.zs) * line_width:(k % g.zs + 1) * line_width])
    returned = give_back(dot(tie(hidden, both_part), down))
    back_rows = give_back(dot(tie(d_both, both_part), gate_up, ((1,), (1,))))
    returned, back_rows = tie(returned, *early), tie(back_rows, *early)

    high = lax.reduce_precision(weighted, 8, 7)
    mixed = (dot(high.astype(BF), returned) + dot((weighted - high).astype(BF), returned)).astype(BF)
    products = dot(d_out, returned, ((1,), (1,)))
    d_probs = jnp.sum(jnp.where(pair, products[:, None, :], 0.0), axis=2)
    d_turned = dot(placing, back_rows).astype(BF)
    d_tokens = lax.dynamic_slice(
        jnp.concatenate([d_turned, d_turned], axis=1), (0, (g.zs - g.z) * line_width), (rows, width)
    )

    down_a, down_b = unspread(down_grad)
    d_w_down = jnp.where(
        even, jnp.concatenate([down_a, down_b], axis=0), jnp.concatenate([down_b, down_a], axis=0)
    ).astype(F32)[None]
    both_a, both_b = unspread(gate_up_grad)
    d_w_gate = dot(jnp.concatenate([both_a[:, :half], both_b[:, :half]], axis=1), shuffle, ((1,), (1,)))[None]
    d_w_up = dot(jnp.concatenate([both_a[:, half:], both_b[:, half:]], axis=1), shuffle, ((1,), (1,)))[None]
    return (mixed, d_tokens, d_probs, d_w_gate, d_w_up, d_w_down)


def solution(mesh):
    rows = P(("dp", "expert"), None)
    weight = P("expert", "dp", None)
    return jax.shard_map(
        local,
        mesh=mesh,
        in_specs=(rows, rows, rows, weight, weight, weight, rows),
        out_specs=(rows, rows, rows, weight, weight, weight),
        check_vma=False,
    )
```

```python
import jax
import jax.numpy as jnp
from jax import lax
from jax.sharding import PartitionSpec as P

BF = jnp.bfloat16
F32 = jnp.float32
BOTH = ("dp", "expert")


def dot(a, b, dims=((1,), (0,))):
    return lax.dot_general(a, b, (dims, ((), ())), preferred_element_type=F32)


def tie(value, *others):
    return lax.optimization_barrier((value,) + others)[0]


def added(*terms):
    return sum(t.astype(F32) for t in terms).astype(BF)


class Grid:
    def __init__(self):
        self.dps, self.experts = lax.axis_size("dp"), lax.axis_size("expert")
        self.zs, self.qs = self.dps // 2, self.experts // 2
        dp, ex = lax.axis_index("dp"), lax.axis_index("expert")
        self.z, self.x, self.q, self.c = dp // 2, dp % 2, ex // 2, ex % 2

    def send(self, value, move):
        pairs = []
        for z in range(self.zs):
            for x in range(2):
                for q in range(self.qs):
                    for c in range(2):
                        to = move(z, x, q, c)
                        if to is not None:
                            pairs.append((self.flat(z, x, q, c), self.flat(*to)))
        return lax.ppermute(value, BOTH, pairs)

    def flat(self, z, x, q, c):
        return (z * 2 + x) * self.experts + q * 2 + c

    def hop(self, value, where):
        return self.send(value, lambda z, x, q, c: (where[z], x, q, c) if z in where else None)

    def gather(self, shard, *ahead):
        n, z = self.zs, self.z
        if n == 4:
            up = self.hop(shard, {0: 1, 1: 2, 2: 3})
            down = self.hop(shard, {1: 0, 2: 1, 3: 2})
            if ahead:
                up, down = tie(up, *ahead), tie(down, *ahead)
            passed = jnp.where(z == 1, up, down)
            far = self.hop(passed, {1: 3, 2: 0})
            up_2 = self.hop(up, {1: 2, 2: 3})
            down_2 = self.hop(down, {1: 0, 2: 1})
            blocks = [
                shard,
                jnp.where(z == 3, far, down),
                jnp.where(z < 2, down_2, up_2),
                jnp.where(z == 0, far, up),
            ]
            return blocks, (up, down, passed)
        ups, downs = [shard], [shard]
        for s in range(1, n):
            ups.append(self.hop(ups[-1], {i: i + 1 for i in range(s - 1, n - 1)}))
            downs.append(self.hop(downs[-1], {i: i - 1 for i in range(1, n - s + 1)}))
        blocks = [shard] + [jnp.where(z + s < n, downs[s], ups[n - s]) for s in range(1, n)]
        return blocks, (ups[1], downs[1])

    def straight(self, blocks):
        n = self.zs
        rows = []
        for j in range(n):
            row = blocks[j]
            for z in range(1, n):
                row = jnp.where(self.z == z, blocks[(j - z) % n], row)
            rows.append(row)
        return rows

    def scatter(self, block, *ahead):
        n, z = self.zs, self.z
        if n == 4:
            far = self.hop(jnp.where(z == 0, block(3), block(1)), {0: 2, 3: 1})
            middle = block(2)
            up = self.hop(middle, {0: 1, 1: 2})
            down = self.hop(middle, {3: 2, 2: 1})
            near = self.hop(jnp.where(z == 0, block(1), block(3)), {0: 1, 3: 2})
            is_low = z == 1
            to_end = added(jnp.where(is_low, block(3), block(1)), jnp.where(is_low, down, up), far)
            to_mid = added(jnp.where(is_low, block(1), block(3)), jnp.where(is_low, up, down))
            to_end, to_mid = tie(to_end, *ahead), tie(to_mid, *ahead)
            end = self.hop(to_end, {1: 0, 2: 3})
            mid = self.hop(to_mid, {1: 2, 2: 1})
            return added(block(0), near, mid, end), (to_end, to_mid)
        up = self.hop(block(n - 1), {0: 1})
        down = self.hop(block(1), {n - 1: n - 2})
        early = up, down
        for r in range(2, n):
            up = self.hop(added(block(n - r), up), {i: i + 1 for i in range(r)})
            down = self.hop(added(block(r), down), {i: i - 1 for i in range(n - r, n)})
        return added(block(0), up, down), early


def local(tokens, expert_ids, gate_probs, w_gate, w_up, w_down, d_out):
    g = Grid()
    rows, topk = expert_ids.shape
    width = tokens.shape[1]
    hidden_width = w_gate.shape[2]
    half = hidden_width // 2
    experts = g.experts
    cap = rows * topk * 9 // (8 * experts)
    slots = experts * cap
    first = g.c == 0
    even = g.x == 0

    block = hidden_width // g.dps
    part = block // 2
    place = jnp.arange(hidden_width, dtype=jnp.int32)
    in_half = place % half
    source_col = (in_half // part) * block + ((place // half) ^ g.x) * part + in_half % part
    shuffle = (jnp.arange(hidden_width, dtype=jnp.int32)[:, None] == source_col[None, :]).astype(BF)

    def out_a(z, x, q, c):
        return z, c, q, x

    def out_b(z, x, q, c):
        return z, c, q, 1 - x

    def back_a(z, x, q, c):
        return z, c, q, x

    def back_b(z, x, q, c):
        return z, 1 - c, q, x

    def spread(part_a, part_b):
        got_a, got_b = g.send(part_a, out_a), g.send(part_b, out_b)
        return jnp.concatenate([jnp.where(first, got_a, got_b), jnp.where(first, got_b, got_a)], axis=0)

    def unspread(both):
        n = both.shape[0] // 2
        low, high = both[:n], both[n:]
        return g.send(jnp.where(first, low, high), back_a), g.send(jnp.where(first, high, low), back_b)

    gate_cols = dot(w_gate[0], shuffle).astype(BF)
    up_cols = dot(w_up[0], shuffle).astype(BF)
    gate_up_shard = spread(
        jnp.concatenate([gate_cols[:, :half], up_cols[:, :half]], axis=1),
        jnp.concatenate([gate_cols[:, half:], up_cols[:, half:]], axis=1),
    )
    expert_iota = jnp.arange(experts, dtype=jnp.int32)
    chosen = expert_ids[:, :, None] == expert_iota
    named = jnp.any(chosen, axis=1).astype(BF)
    token_iota = jnp.arange(rows, dtype=jnp.int32)
    earlier = (token_iota[:, None] > token_iota[None, :]).astype(BF)
    before = dot(earlier, named)
    slot = jnp.sum(jnp.where(chosen, before[:, None, :], 0.0), axis=2).astype(jnp.int32)
    relative = ((expert_ids // 2 - g.q + g.qs) % g.qs) * 2 + ((expert_ids % 2) ^ g.x)
    dest = relative * cap + slot
    slot_iota = jnp.arange(slots, dtype=jnp.int32)
    pair = dest[:, :, None] == slot_iota
    placing = jnp.any(pair, axis=1).astype(BF)
    weighted = jnp.sum(jnp.where(pair, gate_probs[:, :, None], 0.0), axis=1)
    slot_probs = jnp.sum(weighted, axis=0)

    def member(r, sign):
        def move(z, x, q, c):
            return z, x ^ (r % 2), (q + sign * (r // 2)) % g.qs, c

        return move

    def other_core(z, x, q, c):
        return z, x, q, 1 - c

    def exchange(value, sign):
        got = [value[:cap]] + [g.send(value[r * cap:(r + 1) * cap], member(r, sign)) for r in range(1, experts)]
        return jnp.concatenate(got, axis=0)

    line_width = width // g.zs
    turned = lax.dynamic_slice(jnp.concatenate([tokens, tokens], axis=1), (0, g.z * line_width), (rows, width))
    sent = jnp.concatenate(
        [
            dot(placing, turned, ((0,), (0,))).astype(BF),
            (slot_probs[:, None] * dot(placing, d_out, ((0,), (0,)))).astype(BF),
        ],
        axis=1,
    )
    gate_up_blocks, gate_up_passed = g.gather(gate_up_shard)
    gate_up = jnp.concatenate(gate_up_blocks, axis=0)
    mine = tie(exchange(tie(sent, gate_up_shard), 1), *gate_up_passed)
    inputs = jnp.concatenate([mine, g.send(mine, other_core)], axis=0)
    arrived, d_produced = inputs[:, :width], inputs[:, width:]

    w_down_late = tie(w_down[0], *gate_up_passed)
    down_low, down_high = w_down_late[:part], w_down_late[part:]
    down_shard = spread(jnp.where(even, down_low, down_high), jnp.where(even, down_high, down_low))

    pre = dot(arrived, gate_up)
    gate_pre, up_pre = pre[:, :half], pre[:, half:]
    sig = jax.nn.sigmoid(gate_pre)
    act = gate_pre * sig
    hidden = (act * up_pre).astype(BF)
    down_part = dot(hidden, d_produced, ((0,), (0,))).astype(BF)
    down_rows = 2 * part
    down_blocks, _ = g.gather(down_shard, down_part)
    down = jnp.concatenate(g.straight(down_blocks), axis=0)

    d_hidden = dot(tie(d_produced, down_part), down, ((1,), (1,)))
    d_gate = (d_hidden * up_pre * sig * (1.0 + gate_pre * (1.0 - sig))).astype(BF)
    d_up = (d_hidden * act).astype(BF)
    d_both = jnp.concatenate([d_gate, d_up], axis=1)
    both_part = dot(arrived, d_both, ((0,), (0,))).astype(BF)

    produced = dot(tie(hidden, both_part), down)
    d_arrived = dot(tie(d_both, both_part), gate_up, ((1,), (1,)))
    theirs = jnp.concatenate([produced[slots:].astype(BF), d_arrived[slots:].astype(BF)], axis=1)
    other = g.send(theirs, other_core).astype(F32)
    sums = jnp.concatenate(
        [(produced[:slots] + other[:, :width]).astype(BF), (d_arrived[:slots] + other[:, width:]).astype(BF)], axis=1
    )
    down_grad, _ = g.scatter(
        lambda k: lax.dynamic_slice_in_dim(down_part, ((g.z + k) % g.zs) * down_rows, down_rows), sums
    )
    gate_up_grad, second = g.scatter(lambda k: both_part[k * line_width:(k + 1) * line_width], sums)
    got = tie(exchange(sums, -1), *second)
    returned, back_rows = got[:, :width], got[:, width:]
    gate_up_grad, down_grad = tie(gate_up_grad, got), tie(down_grad, *second)

    high = lax.reduce_precision(weighted, 8, 7)
    mixed = (dot(high.astype(BF), returned) + dot((weighted - high).astype(BF), returned)).astype(BF)
    products = dot(d_out, returned, ((1,), (1,)))
    d_probs = jnp.sum(jnp.where(pair, products[:, None, :], 0.0), axis=2)
    d_turned = dot(placing, back_rows).astype(BF)
    d_tokens = lax.dynamic_slice(
        jnp.concatenate([d_turned, d_turned], axis=1), (0, (g.zs - g.z) * line_width), (rows, width)
    )

    down_a, down_b = unspread(down_grad)
    d_w_down = jnp.where(
        even, jnp.concatenate([down_a, down_b], axis=0), jnp.concatenate([down_b, down_a], axis=0)
    ).astype(F32)[None]
    both_a, both_b = unspread(gate_up_grad)
    d_w_gate = dot(jnp.concatenate([both_a[:, :half], both_b[:, :half]], axis=1), shuffle, ((1,), (1,)))[None]
    d_w_up = dot(jnp.concatenate([both_a[:, half:], both_b[:, half:]], axis=1), shuffle, ((1,), (1,)))[None]
    return (mixed, d_tokens, d_probs, d_w_gate, d_w_up, d_w_down)


def solution(mesh):
    rows = P(("dp", "expert"), None)
    weight = P("expert", "dp", None)
    return jax.shard_map(
        local,
        mesh=mesh,
        in_specs=(rows, rows, rows, weight, weight, weight, rows),
        out_specs=(rows, rows, rows, weight, weight, weight),
        check_vma=False,
    )
```

```python
import jax
import jax.numpy as jnp
from jax import lax
from jax.sharding import PartitionSpec as P

BF = jnp.bfloat16
F32 = jnp.float32
BOTH = ("dp", "expert")


def dot(a, b, dims=((1,), (0,))):
    return lax.dot_general(a, b, (dims, ((), ())), preferred_element_type=F32)


def tie(value, *others):
    return lax.optimization_barrier((value,) + others)[0]


def added(*terms):
    return sum(t.astype(F32) for t in terms).astype(BF)


class Grid:
    def __init__(self):
        self.dps, self.experts = lax.axis_size("dp"), lax.axis_size("expert")
        self.zs, self.qs = self.dps // 2, self.experts // 2
        dp, ex = lax.axis_index("dp"), lax.axis_index("expert")
        self.z, self.x, self.q, self.c = dp // 2, dp % 2, ex // 2, ex % 2
        self.lines = [[z * 2 + x for z in range(self.zs)] for x in range(2)]

    def send(self, value, move):
        pairs = []
        for z in range(self.zs):
            for x in range(2):
                for q in range(self.qs):
                    for c in range(2):
                        to = move(z, x, q, c)
                        if to is not None:
                            pairs.append((self.flat(z, x, q, c), self.flat(*to)))
        return lax.ppermute(value, BOTH, pairs)

    def flat(self, z, x, q, c):
        return (z * 2 + x) * self.experts + q * 2 + c

    def hop(self, value, where):
        return self.send(value, lambda z, x, q, c: (where[z], x, q, c) if z in where else None)

    def gather(self, shard):
        n, z = self.zs, self.z
        if n == 4:
            up = self.hop(shard, {0: 1, 1: 2, 2: 3})
            down = self.hop(shard, {1: 0, 2: 1, 3: 2})
            passed = jnp.where(z == 1, up, down)
            far = self.hop(passed, {1: 3, 2: 0})
            up_2 = self.hop(up, {1: 2, 2: 3})
            down_2 = self.hop(down, {1: 0, 2: 1})
            blocks = [
                shard,
                jnp.where(z == 3, far, down),
                jnp.where(z < 2, down_2, up_2),
                jnp.where(z == 0, far, up),
            ]
            return blocks, (up, down, passed), (far, up_2, down_2)
        ups, downs = [shard], [shard]
        for s in range(1, n):
            ups.append(self.hop(ups[-1], {i: i + 1 for i in range(s - 1, n - 1)}))
            downs.append(self.hop(downs[-1], {i: i - 1 for i in range(1, n - s + 1)}))
        blocks = [shard] + [jnp.where(z + s < n, downs[s], ups[n - s]) for s in range(1, n)]
        return blocks, (ups[-2], downs[-2]), (ups[-1], downs[-1])

    def scatter(self, block):
        n, z = self.zs, self.z
        if n == 4:
            far = self.hop(jnp.where(z == 0, block(3), block(1)), {0: 2, 3: 1})
            middle = block(2)
            up = self.hop(middle, {0: 1, 1: 2})
            down = self.hop(middle, {3: 2, 2: 1})
            near = self.hop(jnp.where(z == 0, block(1), block(3)), {0: 1, 3: 2})
            is_low = z == 1
            to_end = added(jnp.where(is_low, block(3), block(1)), jnp.where(is_low, down, up), far)
            to_mid = added(jnp.where(is_low, block(1), block(3)), jnp.where(is_low, up, down))
            end = self.hop(to_end, {1: 0, 2: 3})
            mid = self.hop(to_mid, {1: 2, 2: 1})
            return added(block(0), near, mid, end), (to_end, to_mid)
        up = self.hop(block(n - 1), {0: 1})
        down = self.hop(block(1), {n - 1: n - 2})
        early = up, down
        for r in range(2, n):
            up = self.hop(added(block(n - r), up), {i: i + 1 for i in range(r)})
            down = self.hop(added(block(r), down), {i: i - 1 for i in range(n - r, n)})
        return added(block(0), up, down), early


def local(tokens, expert_ids, gate_probs, w_gate, w_up, w_down, d_out):
    g = Grid()
    rows, topk = expert_ids.shape
    width = tokens.shape[1]
    hidden_width = w_gate.shape[2]
    half = hidden_width // 2
    experts = g.experts
    cap = rows * topk * 9 // (8 * experts)
    slots = experts * cap
    first = g.c == 0
    even = g.x == 0

    block = hidden_width // g.dps
    part = block // 2
    place = jnp.arange(hidden_width, dtype=jnp.int32)
    in_half = place % half
    source_col = (in_half // part) * block + ((place // half) ^ g.x) * part + in_half % part
    shuffle = (jnp.arange(hidden_width, dtype=jnp.int32)[:, None] == source_col[None, :]).astype(BF)

    def out_a(z, x, q, c):
        return z, c, q, x

    def out_b(z, x, q, c):
        return z, c, q, 1 - x

    def back_a(z, x, q, c):
        return z, c, q, x

    def back_b(z, x, q, c):
        return z, 1 - c, q, x

    def spread(part_a, part_b):
        got_a, got_b = g.send(part_a, out_a), g.send(part_b, out_b)
        return jnp.concatenate([jnp.where(first, got_a, got_b), jnp.where(first, got_b, got_a)], axis=0)

    def unspread(both):
        n = both.shape[0] // 2
        low, high = both[:n], both[n:]
        return g.send(jnp.where(first, low, high), back_a), g.send(jnp.where(first, high, low), back_b)

    gate_cols = dot(w_gate[0], shuffle).astype(BF)
    up_cols = dot(w_up[0], shuffle).astype(BF)
    gate_up_shard = spread(
        jnp.concatenate([gate_cols[:, :half], up_cols[:, :half]], axis=1),
        jnp.concatenate([gate_cols[:, half:], up_cols[:, half:]], axis=1),
    )
    expert_iota = jnp.arange(experts, dtype=jnp.int32)
    chosen = expert_ids[:, :, None] == expert_iota
    named = jnp.any(chosen, axis=1).astype(BF)
    token_iota = jnp.arange(rows, dtype=jnp.int32)
    earlier = (token_iota[:, None] > token_iota[None, :]).astype(BF)
    before = dot(earlier, named)
    slot = jnp.sum(jnp.where(chosen, before[:, None, :], 0.0), axis=2).astype(jnp.int32)
    relative = ((expert_ids // 2 - g.q + g.qs) % g.qs) * 2 + ((expert_ids % 2) ^ g.x)
    dest = relative * cap + slot
    slot_iota = jnp.arange(slots, dtype=jnp.int32)
    pair = dest[:, :, None] == slot_iota
    placing = jnp.any(pair, axis=1).astype(BF)
    weighted = jnp.sum(jnp.where(pair, gate_probs[:, :, None], 0.0), axis=1)
    slot_probs = jnp.sum(weighted, axis=0)

    def member(r, sign):
        def move(z, x, q, c):
            return z, x ^ (r % 2), (q + sign * (r // 2)) % g.qs, c

        return move

    def other_core(z, x, q, c):
        return z, x, q, 1 - c

    def exchange(value, sign):
        got = [value[:cap]] + [g.send(value[r * cap:(r + 1) * cap], member(r, sign)) for r in range(1, experts)]
        return jnp.concatenate(got, axis=0)

    line_width = width // g.zs
    turned = lax.dynamic_slice(jnp.concatenate([tokens, tokens], axis=1), (0, g.z * line_width), (rows, width))
    gate_up_blocks, gate_up_passed, gate_up_last = g.gather(gate_up_shard)
    gate_up = jnp.concatenate(gate_up_blocks, axis=0)
    sent_rows = dot(placing, turned, ((0,), (0,))).astype(BF)
    sent_grads = (slot_probs[:, None] * dot(placing, d_out, ((0,), (0,)))).astype(BF)
    mine = exchange(tie(sent_rows, gate_up_shard), 1)
    arrived = jnp.concatenate([mine, g.send(mine, other_core)], axis=0)
    mine = tie(exchange(tie(sent_grads, *gate_up_passed), 1), *gate_up_last)
    d_produced = jnp.concatenate([mine, g.send(mine, other_core)], axis=0)

    w_down_late = tie(w_down[0], gate_up_shard)
    down_low, down_high = w_down_late[:part], w_down_late[part:]
    down_shard = spread(jnp.where(even, down_low, down_high), jnp.where(even, down_high, down_low))
    down = lax.all_gather(down_shard, "dp", axis=0, tiled=True, axis_index_groups=g.lines)

    pre = dot(arrived, gate_up)
    gate_pre, up_pre = pre[:, :half], pre[:, half:]
    sig = jax.nn.sigmoid(gate_pre)
    act = gate_pre * sig
    hidden = (act * up_pre).astype(BF)
    down_part = dot(hidden, d_produced, ((0,), (0,))).astype(BF)
    down_grad = lax.psum_scatter(down_part, "dp", scatter_dimension=0, tiled=True, axis_index_groups=g.lines)

    d_hidden = dot(tie(d_produced, down_part), down, ((1,), (1,)))
    d_gate = (d_hidden * up_pre * sig * (1.0 + gate_pre * (1.0 - sig))).astype(BF)
    d_up = (d_hidden * act).astype(BF)
    d_both = jnp.concatenate([d_gate, d_up], axis=1)
    both_part = dot(arrived, d_both, ((0,), (0,))).astype(BF)

    produced = dot(tie(hidden, both_part), down)
    d_arrived = dot(tie(d_both, both_part), gate_up, ((1,), (1,)))
    theirs = jnp.concatenate([produced[slots:].astype(BF), d_arrived[slots:].astype(BF)], axis=1)
    gate_up_grad, second = g.scatter(lambda k: both_part[k * line_width:(k + 1) * line_width])
    other = tie(g.send(theirs, other_core), *second).astype(F32)
    sums = jnp.concatenate(
        [(produced[:slots] + other[:, :width]).astype(BF), (d_arrived[:slots] + other[:, width:]).astype(BF)], axis=1
    )
    got = exchange(sums, -1)
    returned, back_rows = got[:, :width], got[:, width:]
    gate_up_grad, down_grad = tie(gate_up_grad, got), tie(down_grad, *second)

    high = lax.reduce_precision(weighted, 8, 7)
    mixed = (dot(high.astype(BF), returned) + dot((weighted - high).astype(BF), returned)).astype(BF)
    products = dot(d_out, returned, ((1,), (1,)))
    d_probs = jnp.sum(jnp.where(pair, products[:, None, :], 0.0), axis=2)
    d_turned = dot(placing, back_rows).astype(BF)
    d_tokens = lax.dynamic_slice(
        jnp.concatenate([d_turned, d_turned], axis=1), (0, (g.zs - g.z) * line_width), (rows, width)
    )

    down_a, down_b = unspread(down_grad)
    d_w_down = jnp.where(
        even, jnp.concatenate([down_a, down_b], axis=0), jnp.concatenate([down_b, down_a], axis=0)
    ).astype(F32)[None]
    both_a, both_b = unspread(gate_up_grad)
    d_w_gate = dot(jnp.concatenate([both_a[:, :half], both_b[:, :half]], axis=1), shuffle, ((1,), (1,)))[None]
    d_w_up = dot(jnp.concatenate([both_a[:, half:], both_b[:, half:]], axis=1), shuffle, ((1,), (1,)))[None]
    return (mixed, d_tokens, d_probs, d_w_gate, d_w_up, d_w_down)


def solution(mesh):
    rows = P(("dp", "expert"), None)
    weight = P("expert", "dp", None)
    return jax.shard_map(
        local,
        mesh=mesh,
        in_specs=(rows, rows, rows, weight, weight, weight, rows),
        out_specs=(rows, rows, rows, weight, weight, weight),
        check_vma=False,
    )
```

```python
import jax
import jax.numpy as jnp
from jax import lax
from jax.experimental import pallas as pl
from jax.experimental.pallas import tpu as pltpu
from jax.sharding import PartitionSpec as P

BF = jnp.bfloat16
F32 = jnp.float32
BOTH = ("dp", "expert")


def dot(a, b, dims=((1,), (0,))):
    return lax.dot_general(a, b, (dims, ((), ())), preferred_element_type=F32)


def added(*terms):
    return sum(t.astype(F32) for t in terms).astype(BF)


class Grid:
    def __init__(self):
        self.dps, self.experts = lax.axis_size("dp"), lax.axis_size("expert")
        self.zs, self.qs = self.dps // 2, self.experts // 2
        dp, ex = lax.axis_index("dp"), lax.axis_index("expert")
        self.z, self.x, self.q, self.c = dp // 2, dp % 2, ex // 2, ex % 2

    def send(self, value, move):
        pairs = []
        for z in range(self.zs):
            for x in range(2):
                for q in range(self.qs):
                    for c in range(2):
                        to = move(z, x, q, c)
                        if to is not None:
                            pairs.append((self.flat(z, x, q, c), self.flat(*to)))
        return lax.ppermute(value, BOTH, pairs)

    def flat(self, z, x, q, c):
        return (z * 2 + x) * self.experts + q * 2 + c

    def hop(self, value, where):
        return self.send(value, lambda z, x, q, c: (where[z], x, q, c) if z in where else None)

    def line(self, shard):
        n = self.zs
        ups, downs = [shard], [shard]
        for s in range(1, n):
            ups.append(self.hop(ups[-1], {i: i + 1 for i in range(s - 1, n - 1)}))
            downs.append(self.hop(downs[-1], {i: i - 1 for i in range(1, n - s + 1)}))
        return [shard] + [jnp.where(self.z + s < n, downs[s], ups[n - s]) for s in range(1, n)]

    def straight(self, blocks):
        n = self.zs
        rows = []
        for j in range(n):
            row = blocks[j]
            for z in range(1, n):
                row = jnp.where(self.z == z, blocks[(j - z) % n], row)
            rows.append(row)
        return rows

    def line_sum(self, block):
        n = self.zs
        up, down = self.hop(block(n - 1), {0: 1}), self.hop(block(1), {n - 1: n - 2})
        for r in range(2, n):
            up = self.hop(added(block(n - r), up), {i: i + 1 for i in range(r)})
            down = self.hop(added(block(r), down), {i: i - 1 for i in range(n - r, n)})
        return added(block(0), up, down)


LANES = 256
VMEM_BYTES = 48 * 2**20


def pack_kernel(x_ref, gate_ref, up_ref, down_ref, shuffle_ref, a_ref, b_ref):
    rows, hidden_width = gate_ref.shape
    half, part = hidden_width // 2, down_ref.shape[0] // 2
    shuffle = shuffle_ref[...]
    gate, up = dot(gate_ref[...], shuffle).astype(BF), dot(up_ref[...], shuffle).astype(BF)
    x = x_ref[0]
    for ref, at, start in ((a_ref, 0, x), (b_ref, half, 1 - x)):
        both = jnp.concatenate([gate[:, at:at + half], up[:, at:at + half]], axis=1)
        count = hidden_width // LANES
        for i in range(count):
            ref[i * rows:(i + 1) * rows, :] = both[:, i * LANES:(i + 1) * LANES]
        source = pl.ds(pl.multiple_of(start * part, 16), part)
        for j in range(down_ref.shape[1] // LANES):
            to = count * rows + j * part
            ref[to:to + part, :] = down_ref[source, j * LANES:(j + 1) * LANES]


def unpack_kernel(x_ref, a_ref, b_ref, shuffle_ref, gate_ref, up_ref, down_ref):
    rows, hidden_width = gate_ref.shape
    half, part = hidden_width // 2, down_ref.shape[0] // 2
    count = hidden_width // LANES
    x = x_ref[0]
    a, b = (
        jnp.concatenate([ref[i * rows:(i + 1) * rows, :] for i in range(count)], axis=1) for ref in (a_ref, b_ref)
    )
    shuffle = shuffle_ref[...]
    gate_ref[...] = dot(jnp.concatenate([a[:, :half], b[:, :half]], axis=1), shuffle, ((1,), (1,)))
    up_ref[...] = dot(jnp.concatenate([a[:, half:], b[:, half:]], axis=1), shuffle, ((1,), (1,)))
    for ref, start in ((a_ref, x), (b_ref, 1 - x)):
        to = pl.ds(pl.multiple_of(start * part, 16), part)
        for j in range(down_ref.shape[1] // LANES):
            at = count * rows + j * part
            down_ref[to, j * LANES:(j + 1) * LANES] = ref[at:at + part, :].astype(F32)


def expert_kernel(
    z_ref, own, up, down, far, up_2, down_2, mine, theirs,
    keep_out, give_out, outer_out, inner_out, middle_out, own_out,
    packed, x, grads, gate_up, w_down, pre, d_hidden, hidden, d_both, d_down, keep, give, terms, load, store,
):
    places, size, _ = packed.shape
    rows, width = x.shape
    slots = rows // 2
    line = width // places
    part_rows = line // 2
    hidden_width = gate_up.shape[1]
    half = hidden_width // 2
    part = half // places // 2
    count, columns = hidden_width // LANES, width // LANES
    size_half = size // 2
    z = z_ref[0]

    for number, (source, target) in enumerate(
        (
            (mine.at[:, :width], x.at[:slots]),
            (theirs.at[:, :width], x.at[slots:]),
            (mine.at[:, width:], grads.at[:slots]),
            (theirs.at[:, width:], grads.at[slots:]),
        )
    ):
        pltpu.make_async_copy(source, target, load.at[number]).start()
    pltpu.make_async_copy(own, packed.at[0], load.at[4]).start()
    for s, is_one, one, other in (
        (1, z == places - 1, far, down),
        (2, z < 2, down_2, up_2),
        (3, z == 0, far, up),
    ):
        @pl.when(is_one)
        def _():
            pltpu.make_async_copy(one, packed.at[s], load.at[4 + s]).start()

        @pl.when(jnp.logical_not(is_one))
        def _():
            pltpu.make_async_copy(other, packed.at[s], load.at[4 + s]).start()

    def down_rows(k, h):
        return pl.ds(pl.multiple_of(lax.rem(z + k, places) * (2 * part) + h * part, 16), part)

    pltpu.make_async_copy(mine.at[:, :width], x.at[:slots], load.at[0]).wait()
    pltpu.make_async_copy(theirs.at[:, :width], x.at[slots:], load.at[1]).wait()
    for s in range(places):
        pltpu.make_async_copy(own, packed.at[s], load.at[4 + s]).wait()
        for h in range(2):
            for i in range(count):
                at = h * size_half + i * part_rows
                to = s * line + h * part_rows
                gate_up[to:to + part_rows, i * LANES:(i + 1) * LANES] = packed[s, at:at + part_rows, :]
            for j in range(columns):
                at = h * size_half + count * part_rows + j * part
                w_down[down_rows(s, h), j * LANES:(j + 1) * LANES] = packed[s, at:at + part, :]
        block = slice(s * line, (s + 1) * line)
        for i in range(count):
            cols = slice(i * LANES, (i + 1) * LANES)
            product = dot(x[:, block], gate_up[block, cols])
            pre[:, cols] = product if s == 0 else pre[:, cols] + product

    step = 64 if rows % 64 == 0 else 16

    def activate(r, _):
        at = pl.ds(pl.multiple_of(r * step, 16), step)
        gate_pre, up_pre = pre[at, :half], pre[at, half:]
        sig = 1.0 / (1.0 + jnp.exp(-gate_pre))
        act = gate_pre * sig
        hidden[at, :] = (act * up_pre).astype(BF)
        pre[at, :half] = up_pre * sig * (1.0 + gate_pre * (1.0 - sig))
        pre[at, half:] = act
        return 0

    lax.fori_loop(0, rows // step, activate, 0)

    pltpu.make_async_copy(mine.at[:, width:], grads.at[:slots], load.at[2]).wait()
    pltpu.make_async_copy(theirs.at[:, width:], grads.at[slots:], load.at[3]).wait()
    d_hidden[...] = dot(grads[...], w_down[...], ((1,), (1,)))

    def differentiate(r, _):
        at = pl.ds(pl.multiple_of(r * step, 16), step)
        d_h = d_hidden[at, :]
        d_both[at, :half] = (d_h * pre[at, :half]).astype(BF)
        d_both[at, half:] = (d_h * pre[at, half:]).astype(BF)
        return 0

    lax.fori_loop(0, rows // step, differentiate, 0)

    def to_tokens(n, _):
        at = pl.multiple_of(n * LANES, LANES)
        cols, beyond = pl.ds(at, LANES), pl.ds(at + width, LANES)
        produced = dot(hidden[...], w_down[:, cols]).astype(BF)
        keep[:, cols], give[:, cols] = produced[:slots], produced[slots:]
        d_arrived = dot(d_both[...], gate_up[cols, :], ((1,), (1,))).astype(BF)
        keep[:, beyond], give[:, beyond] = d_arrived[:slots], d_arrived[slots:]
        d_down[:, cols] = dot(hidden[...], grads[:, cols], ((0,), (0,))).astype(BF)
        return 0

    lax.fori_loop(0, columns, to_tokens, 0)
    pltpu.make_async_copy(keep, keep_out, store.at[4]).start()
    pltpu.make_async_copy(give, give_out, store.at[5]).start()

    outer_k = jnp.where(z < places // 2, places - 1, 1)
    roles = ((0, outer_k, outer_out), (1, 2, middle_out), (2, places - outer_k, inner_out), (3, 0, own_out))
    for r, k, out in roles:
        for h in range(2):
            from_cols = pl.ds(pl.multiple_of(k * line + h * part_rows, LANES), part_rows)
            weights = dot(x[:, from_cols], d_both[...], ((0,), (0,))).astype(BF)
            for i in range(count):
                to = h * size_half + i * part_rows
                terms[r, to:to + part_rows, :] = weights[:, i * LANES:(i + 1) * LANES]
            for j in range(columns):
                to = h * size_half + count * part_rows + j * part
                terms[r, to:to + part, :] = d_down[down_rows(k, h), j * LANES:(j + 1) * LANES]
        pltpu.make_async_copy(terms.at[r], out, store.at[r]).start()
    for r, k, out in roles:
        pltpu.make_async_copy(terms.at[r], out, store.at[r]).wait()
    pltpu.make_async_copy(keep, keep_out, store.at[4]).wait()
    pltpu.make_async_copy(give, give_out, store.at[5]).wait()


def in_vmem(count):
    return [pl.BlockSpec(memory_space=pltpu.VMEM)] * count


IN_SMEM = pl.BlockSpec(memory_space=pltpu.SMEM)


def pack(x, gate, up, down, shuffle):
    rows, hidden_width = gate.shape
    size = (rows * hidden_width + down.size // 2) // LANES
    return pl.pallas_call(
        pack_kernel,
        out_shape=[jax.ShapeDtypeStruct((size, LANES), BF)] * 2,
        in_specs=[IN_SMEM] + in_vmem(4),
        out_specs=in_vmem(2),
        compiler_params=pltpu.CompilerParams(vmem_limit_bytes=VMEM_BYTES // 2),
    )(x, gate, up, down, shuffle)


def unpack(x, a, b, shuffle, gate_shape, down_shape):
    return pl.pallas_call(
        unpack_kernel,
        out_shape=[jax.ShapeDtypeStruct(shape, F32) for shape in (gate_shape, gate_shape, down_shape)],
        in_specs=[IN_SMEM] + in_vmem(3),
        out_specs=in_vmem(3),
        compiler_params=pltpu.CompilerParams(vmem_limit_bytes=VMEM_BYTES // 2),
    )(x, a, b, shuffle)


def expert(z, places, half, weights, mine, theirs):
    size = weights[0].shape[0]
    slots, width = mine.shape[0], mine.shape[1] // 2
    rows = 2 * slots
    row_shape, term_shape = jax.ShapeDtypeStruct(mine.shape, BF), jax.ShapeDtypeStruct((size, LANES), BF)
    return pl.pallas_call(
        expert_kernel,
        out_shape=[row_shape] * 2 + [term_shape] * 4,
        in_specs=[IN_SMEM] + [pl.BlockSpec(memory_space=pl.ANY)] * 8,
        out_specs=[pl.BlockSpec(memory_space=pl.ANY)] * 6,
        scratch_shapes=[
            pltpu.VMEM((places, size, LANES), BF),
            pltpu.VMEM((rows, width), BF),
            pltpu.VMEM((rows, width), BF),
            pltpu.VMEM((width, 2 * half), BF),
            pltpu.VMEM((half, width), BF),
            pltpu.VMEM((rows, 2 * half), F32),
            pltpu.VMEM((rows, half), F32),
            pltpu.VMEM((rows, half), BF),
            pltpu.VMEM((rows, 2 * half), BF),
            pltpu.VMEM((half, width), BF),
            pltpu.VMEM((slots, 2 * width), BF),
            pltpu.VMEM((slots, 2 * width), BF),
            pltpu.VMEM((places, size, LANES), BF),
            pltpu.SemaphoreType.DMA((4 + places,)),
            pltpu.SemaphoreType.DMA((6,)),
        ],
        compiler_params=pltpu.CompilerParams(vmem_limit_bytes=VMEM_BYTES),
        cost_estimate=pl.CostEstimate(
            flops=18 * rows * width * half, bytes_accessed=20 * 2**20, transcendentals=rows * half
        ),
    )(z, *weights, mine, theirs)


def local(tokens, expert_ids, gate_probs, w_gate, w_up, w_down, d_out):
    g = Grid()
    rows, topk = expert_ids.shape
    width = tokens.shape[1]
    hidden_width = w_gate.shape[2]
    half = hidden_width // 2
    experts = g.experts
    cap = rows * topk * 9 // (8 * experts)
    slots = experts * cap
    first = g.c == 0
    even = g.x == 0

    block = hidden_width // g.dps
    part = block // 2
    place = jnp.arange(hidden_width, dtype=jnp.int32)
    in_half = place % half
    source_col = (in_half // part) * block + ((place // half) ^ g.x) * part + in_half % part
    shuffle = (jnp.arange(hidden_width, dtype=jnp.int32)[:, None] == source_col[None, :]).astype(BF)

    def out_a(z, x, q, c):
        return z, c, q, x

    def out_b(z, x, q, c):
        return z, c, q, 1 - x

    def back_a(z, x, q, c):
        return z, c, q, x

    def back_b(z, x, q, c):
        return z, 1 - c, q, x

    def spread(part_a, part_b):
        got_a, got_b = g.send(part_a, out_a), g.send(part_b, out_b)
        return jnp.concatenate([jnp.where(first, got_a, got_b), jnp.where(first, got_b, got_a)], axis=0)

    def unspread(both):
        n = both.shape[0] // 2
        low, high = both[:n], both[n:]
        return g.send(jnp.where(first, low, high), back_a), g.send(jnp.where(first, high, low), back_b)

    expert_iota = jnp.arange(experts, dtype=jnp.int32)
    chosen = expert_ids[:, :, None] == expert_iota
    named = jnp.any(chosen, axis=1).astype(BF)
    token_iota = jnp.arange(rows, dtype=jnp.int32)
    earlier = (token_iota[:, None] > token_iota[None, :]).astype(BF)
    before = dot(earlier, named)
    slot = jnp.sum(jnp.where(chosen, before[:, None, :], 0.0), axis=2).astype(jnp.int32)
    relative = ((expert_ids // 2 - g.q + g.qs) % g.qs) * 2 + ((expert_ids % 2) ^ g.x)
    dest = relative * cap + slot
    slot_iota = jnp.arange(slots, dtype=jnp.int32)
    pair = dest[:, :, None] == slot_iota
    placing = jnp.any(pair, axis=1).astype(BF)
    weighted = jnp.sum(jnp.where(pair, gate_probs[:, :, None], 0.0), axis=1)
    slot_probs = jnp.sum(weighted, axis=0)

    def member(r, sign):
        def move(z, x, q, c):
            return z, x ^ (r % 2), (q + sign * (r // 2)) % g.qs, c

        return move

    def other_core(z, x, q, c):
        return z, x, q, 1 - c

    def exchange(value, sign):
        got = [value[:cap]] + [g.send(value[r * cap:(r + 1) * cap], member(r, sign)) for r in range(1, experts)]
        return jnp.concatenate(got, axis=0)

    line_width = width // g.zs
    turned = lax.dynamic_slice(jnp.concatenate([tokens, tokens], axis=1), (0, g.z * line_width), (rows, width))
    sent = jnp.concatenate(
        [
            dot(placing, turned, ((0,), (0,))).astype(BF),
            (slot_probs[:, None] * dot(placing, d_out, ((0,), (0,)))).astype(BF),
        ],
        axis=1,
    )
    shapes = w_gate.shape[1:], w_down.shape[1:]
    if g.zs == 4 and cap % 8 == 0 and slots % 16 == 0 and part % 16 == 0:
        place_x, place_z = g.x.reshape(1).astype(jnp.int32), g.z.reshape(1).astype(jnp.int32)
        shard = spread(*pack(place_x, w_gate[0], w_up[0], w_down[0], shuffle))
        shard, sent = lax.optimization_barrier((shard, sent))
        up, down = g.hop(shard, {0: 1, 1: 2, 2: 3}), g.hop(shard, {1: 0, 2: 1, 3: 2})
        up, down, mine = lax.optimization_barrier((up, down, exchange(sent, 1)))
        passed, mine = lax.optimization_barrier((jnp.where(g.z == 1, up, down), mine))
        far = g.hop(passed, {1: 3, 2: 0})
        up_2, down_2 = g.hop(up, {1: 2, 2: 3}), g.hop(down, {1: 0, 2: 1})
        theirs = g.send(mine, other_core)
        keep, give, outer, inner, middle, own = expert(
            place_z, g.zs, half, (shard, up, down, far, up_2, down_2), mine, theirs
        )
        far = g.hop(outer, {0: 2, 3: 1})
        up, down = g.hop(middle, {0: 1, 1: 2}), g.hop(middle, {3: 2, 2: 1})
        near = g.hop(inner, {0: 1, 3: 2})
        far, up, down, near, given = lax.optimization_barrier((far, up, down, near, g.send(give, other_core)))
        is_low = g.z == 1
        to_end = added(outer, jnp.where(is_low, down, up), far)
        to_mid = added(inner, jnp.where(is_low, up, down))
        to_end, to_mid, sums = lax.optimization_barrier((to_end, to_mid, added(keep, given)))
        end, mid = g.hop(to_end, {1: 0, 2: 3}), g.hop(to_mid, {1: 2, 2: 1})
        end, mid, got = lax.optimization_barrier((end, mid, exchange(sums, -1)))
        grad = added(own, near, end, mid)
        d_w_gate, d_w_up, d_w_down = unpack(place_x, *unspread(grad), shuffle, *shapes)
    else:
        gate_cols, up_cols = dot(w_gate[0], shuffle).astype(BF), dot(w_up[0], shuffle).astype(BF)
        gate_up_shard = spread(
            jnp.concatenate([gate_cols[:, :half], up_cols[:, :half]], axis=1),
            jnp.concatenate([gate_cols[:, half:], up_cols[:, half:]], axis=1),
        )
        down_low, down_high = w_down[0, :part], w_down[0, part:]
        down_shard = spread(jnp.where(even, down_low, down_high), jnp.where(even, down_high, down_low))
        gate_up = jnp.concatenate(g.line(gate_up_shard), axis=0)
        down = jnp.concatenate(g.straight(g.line(down_shard)), axis=0)
        mine = exchange(sent, 1)
        inputs = jnp.concatenate([mine, g.send(mine, other_core)], axis=0)
        arrived, d_produced = inputs[:, :width], inputs[:, width:]
        pre = dot(arrived, gate_up)
        gate_pre, up_pre = pre[:, :half], pre[:, half:]
        sig = jax.nn.sigmoid(gate_pre)
        act = gate_pre * sig
        hidden = (act * up_pre).astype(BF)
        d_hidden = dot(d_produced, down, ((1,), (1,)))
        d_gate = (d_hidden * up_pre * sig * (1.0 + gate_pre * (1.0 - sig))).astype(BF)
        d_up = (d_hidden * act).astype(BF)
        d_both = jnp.concatenate([d_gate, d_up], axis=1)
        down_part = dot(hidden, d_produced, ((0,), (0,))).astype(BF)
        both_part = dot(arrived, d_both, ((0,), (0,))).astype(BF)
        partial = jnp.concatenate([dot(hidden, down), dot(d_both, gate_up, ((1,), (1,)))], axis=1).astype(BF)
        got = exchange(added(partial[:slots], g.send(partial[slots:], other_core)), -1)
        down_a, down_b = unspread(
            g.line_sum(
                lambda k: lax.dynamic_slice_in_dim(down_part, ((g.z + k) % g.zs) * (2 * part), 2 * part)
            )
        )
        d_w_down = jnp.where(
            even, jnp.concatenate([down_a, down_b], axis=0), jnp.concatenate([down_b, down_a], axis=0)
        ).astype(F32)
        both_a, both_b = unspread(g.line_sum(lambda k: both_part[k * line_width:(k + 1) * line_width]))
        d_w_gate, d_w_up = (
            dot(jnp.concatenate([both_a[:, cols], both_b[:, cols]], axis=1), shuffle, ((1,), (1,)))
            for cols in (slice(0, half), slice(half, None))
        )
    returned, back_rows = got[:, :width], got[:, width:]

    high = lax.reduce_precision(weighted, 8, 7)
    mixed = (dot(high.astype(BF), returned) + dot((weighted - high).astype(BF), returned)).astype(BF)
    products = dot(d_out, returned, ((1,), (1,)))
    d_probs = jnp.sum(jnp.where(pair, products[:, None, :], 0.0), axis=2)
    d_turned = dot(placing, back_rows).astype(BF)
    d_tokens = lax.dynamic_slice(
        jnp.concatenate([d_turned, d_turned], axis=1), (0, (g.zs - g.z) * line_width), (rows, width)
    )

    return (mixed, d_tokens, d_probs, d_w_gate[None], d_w_up[None], d_w_down[None])


def solution(mesh):
    rows = P(("dp", "expert"), None)
    weight = P("expert", "dp", None)
    return jax.shard_map(
        local,
        mesh=mesh,
        in_specs=(rows, rows, rows, weight, weight, weight, rows),
        out_specs=(rows, rows, rows, weight, weight, weight),
        check_vma=False,
    )
```

```python
import functools

import jax
import jax.numpy as jnp
from jax import lax
from jax.experimental import pallas as pl
from jax.experimental.pallas import tpu as pltpu
from jax.sharding import PartitionSpec as P

BF = jnp.bfloat16
F32 = jnp.float32
BOTH = ("dp", "expert")


def dot(a, b, dims=((1,), (0,))):
    return lax.dot_general(a, b, (dims, ((), ())), preferred_element_type=F32)


def added(*terms):
    return sum(t.astype(F32) for t in terms).astype(BF)


class Grid:
    def __init__(self):
        self.dps, self.experts = lax.axis_size("dp"), lax.axis_size("expert")
        self.zs, self.qs = self.dps // 2, self.experts // 2
        dp, ex = lax.axis_index("dp"), lax.axis_index("expert")
        self.z, self.x, self.q, self.c = dp // 2, dp % 2, ex // 2, ex % 2

    def send(self, value, move):
        pairs = []
        for z in range(self.zs):
            for x in range(2):
                for q in range(self.qs):
                    for c in range(2):
                        to = move(z, x, q, c)
                        if to is not None:
                            pairs.append((self.flat(z, x, q, c), self.flat(*to)))
        return lax.ppermute(value, BOTH, pairs)

    def flat(self, z, x, q, c):
        return (z * 2 + x) * self.experts + q * 2 + c

    def hop(self, value, where):
        return self.send(value, lambda z, x, q, c: (where[z], x, q, c) if z in where else None)

    def line(self, shard):
        n = self.zs
        ups, downs = [shard], [shard]
        for s in range(1, n):
            ups.append(self.hop(ups[-1], {i: i + 1 for i in range(s - 1, n - 1)}))
            downs.append(self.hop(downs[-1], {i: i - 1 for i in range(1, n - s + 1)}))
        return [shard] + [jnp.where(self.z + s < n, downs[s], ups[n - s]) for s in range(1, n)]

    def straight(self, blocks):
        n = self.zs
        rows = []
        for j in range(n):
            row = blocks[j]
            for z in range(1, n):
                row = jnp.where(self.z == z, blocks[(j - z) % n], row)
            rows.append(row)
        return rows

    def line_sum(self, block):
        n = self.zs
        up, down = self.hop(block(n - 1), {0: 1}), self.hop(block(1), {n - 1: n - 2})
        for r in range(2, n):
            up = self.hop(added(block(n - r), up), {i: i + 1 for i in range(r)})
            down = self.hop(added(block(r), down), {i: i - 1 for i in range(n - r, n)})
        return added(block(0), up, down)


LANES = 256
VMEM_BYTES = 48 * 2**20


def shuffle_matrix(x, dps, hidden_width, pieces):
    block, half = hidden_width // dps, hidden_width // 2
    sources, start = [], 0
    for piece in pieces:
        unit = jnp.arange(piece * dps, dtype=jnp.int32)
        sources.append((unit // piece) * block + start + unit % piece)
        start += piece
    low = jnp.concatenate(sources)
    source = jnp.concatenate([low + x * (block // 2), low + (1 - x) * (block // 2)])
    return (jnp.arange(hidden_width, dtype=jnp.int32)[:, None] == source[None, :]).astype(BF)


def pack_kernel(pieces, x_ref, gate_ref, up_ref, down_ref, shuffle_ref, *outs):
    rows, hidden_width = gate_ref.shape
    half, block = hidden_width // 2, down_ref.shape[0]
    shuffle = shuffle_ref[...]
    gate, up = dot(gate_ref[...], shuffle).astype(BF), dot(up_ref[...], shuffle).astype(BF)
    x = x_ref[0]
    done = 0
    for number, piece in enumerate(pieces):
        units = piece * half // sum(pieces)
        count = 2 * units // LANES
        for side, start in ((0, x), (1, 1 - x)):
            ref = outs[2 * number + side]
            at = side * half + done * units // piece
            both = jnp.concatenate([gate[:, at:at + units], up[:, at:at + units]], axis=1)
            for i in range(count):
                ref[i * rows:(i + 1) * rows, :] = both[:, i * LANES:(i + 1) * LANES]
            source = pl.ds(pl.multiple_of(start * (block // 2) + done, 16), piece)
            for j in range(down_ref.shape[1] // LANES):
                to = count * rows + j * piece
                ref[to:to + piece, :] = down_ref[source, j * LANES:(j + 1) * LANES]
        done += piece


def unpack_kernel(pieces, x_ref, *refs):
    packed, (shuffle_ref, gate_ref, up_ref, down_ref) = refs[:-4], refs[-4:]
    rows, hidden_width = gate_ref.shape
    half, block = hidden_width // 2, down_ref.shape[0]
    x = x_ref[0]
    gates, ups = [[], []], [[], []]
    done = 0
    for number, piece in enumerate(pieces):
        units = piece * half // sum(pieces)
        count = 2 * units // LANES
        for side, start in ((0, x), (1, 1 - x)):
            ref = packed[2 * number + side]
            both = jnp.concatenate([ref[i * rows:(i + 1) * rows, :] for i in range(count)], axis=1)
            gates[side].append(both[:, :units])
            ups[side].append(both[:, units:])
            to = pl.ds(pl.multiple_of(start * (block // 2) + done, 16), piece)
            for j in range(down_ref.shape[1] // LANES):
                at = count * rows + j * piece
                down_ref[to, j * LANES:(j + 1) * LANES] = ref[at:at + piece, :].astype(F32)
        done += piece
    shuffle = shuffle_ref[...]
    gate_ref[...] = dot(jnp.concatenate(gates[0] + gates[1], axis=1), shuffle, ((1,), (1,)))
    up_ref[...] = dot(jnp.concatenate(ups[0] + ups[1], axis=1), shuffle, ((1,), (1,)))


def expert_kernel(
    adds, z_ref, own, up, down, up_2, down_2, last, mine, theirs, *refs
):
    earlier, refs = refs[:2 * adds], refs[2 * adds:]
    keep_out, give_out, outer_out, *refs = refs
    outs, refs = refs[:4], refs[4:]
    packed, x, grads, gate_up, w_down, pre, d_hidden, hidden, d_both, d_down, keep, give, terms, load, store = refs
    places, size, _ = packed.shape
    rows, width = x.shape
    slots = rows // 2
    line = width // places
    part_rows = line // 2
    units = w_down.shape[0]
    piece = units // places // 2
    count, columns = 2 * units // LANES, width // LANES
    size_half = size // 2
    z = z_ref[0]

    loads = [
        (mine.at[:, :width], x.at[:slots]),
        (theirs.at[:, :width], x.at[slots:]),
        (mine.at[:, width:], grads.at[:slots]),
        (theirs.at[:, width:], grads.at[slots:]),
    ]
    if adds:
        loads += [(earlier[0], keep), (earlier[1], give)]
    loads = [pltpu.make_async_copy(a, b, load.at[places + n]) for n, (a, b) in enumerate(loads)]
    for copy in loads[:2]:
        copy.start()
    pltpu.make_async_copy(own, packed.at[0], load.at[0]).start()
    for s, is_one, one, other in (
        (1, z == places - 1, last, down),
        (2, z < 2, down_2, up_2),
        (3, z == 0, last, up),
    ):
        @pl.when(is_one)
        def _():
            pltpu.make_async_copy(one, packed.at[s], load.at[s]).start()

        @pl.when(jnp.logical_not(is_one))
        def _():
            pltpu.make_async_copy(other, packed.at[s], load.at[s]).start()

    for copy in loads[2:]:
        copy.start()

    def down_rows(k, h):
        return pl.ds(pl.multiple_of(lax.rem(z + k, places) * (2 * piece) + h * piece, 16), piece)

    for copy in loads[:2]:
        copy.wait()
    for s in range(places):
        pltpu.make_async_copy(own, packed.at[s], load.at[s]).wait()
        for h in range(2):
            for i in range(count):
                at = h * size_half + i * part_rows
                to = s * line + h * part_rows
                gate_up[to:to + part_rows, i * LANES:(i + 1) * LANES] = packed[s, at:at + part_rows, :]
            for j in range(columns):
                at = h * size_half + count * part_rows + j * piece
                w_down[down_rows(s, h), j * LANES:(j + 1) * LANES] = packed[s, at:at + piece, :]
        block = slice(s * line, (s + 1) * line)
        for i in range(count):
            cols = slice(i * LANES, (i + 1) * LANES)
            product = dot(x[:, block], gate_up[block, cols])
            pre[:, cols] = product if s == 0 else pre[:, cols] + product

    step = 64 if rows % 64 == 0 else 16

    def activate(r, _):
        at = pl.ds(pl.multiple_of(r * step, 16), step)
        gate_pre, up_pre = pre[at, :units], pre[at, units:]
        sig = 1.0 / (1.0 + jnp.exp(-gate_pre))
        act = gate_pre * sig
        hidden[at, :] = (act * up_pre).astype(BF)
        pre[at, :units] = up_pre * sig * (1.0 + gate_pre * (1.0 - sig))
        pre[at, units:] = act
        return 0

    lax.fori_loop(0, rows // step, activate, 0)
    for copy in loads[2:]:
        copy.wait()
    d_hidden[...] = dot(grads[...], w_down[...], ((1,), (1,)))

    def differentiate(r, _):
        at = pl.ds(pl.multiple_of(r * step, 16), step)
        d_h = d_hidden[at, :]
        d_both[at, :units] = (d_h * pre[at, :units]).astype(BF)
        d_both[at, units:] = (d_h * pre[at, units:]).astype(BF)
        return 0

    lax.fori_loop(0, rows // step, differentiate, 0)

    def to_tokens(n, _):
        at = pl.multiple_of(n * LANES, LANES)
        cols, beyond = pl.ds(at, LANES), pl.ds(at + width, LANES)
        for to, value in (
            (cols, dot(hidden[...], w_down[:, cols])),
            (beyond, dot(d_both[...], gate_up[cols, :], ((1,), (1,)))),
        ):
            for ref, part in ((keep, value[:slots]), (give, value[slots:])):
                ref[:, to] = (part + ref[:, to].astype(F32) if adds else part).astype(BF)
        d_down[:, cols] = dot(hidden[...], grads[:, cols], ((0,), (0,))).astype(BF)
        return 0

    lax.fori_loop(0, columns, to_tokens, 0)
    stores = [pltpu.make_async_copy(keep, keep_out, store.at[0]), pltpu.make_async_copy(give, give_out, store.at[1])]
    for copy in stores:
        copy.start()

    def term(k, _):
        for h in range(2):
            from_cols = pl.ds(pl.multiple_of(k * line + h * part_rows, LANES), part_rows)
            weights = dot(x[:, from_cols], d_both[...], ((0,), (0,))).astype(BF)
            for i in range(count):
                to = h * size_half + i * part_rows
                terms[k, to:to + part_rows, :] = weights[:, i * LANES:(i + 1) * LANES]
            for j in range(columns):
                to = h * size_half + count * part_rows + j * piece
                terms[k, to:to + piece, :] = d_down[down_rows(k, h), j * LANES:(j + 1) * LANES]
        return 0

    lax.fori_loop(0, places, term, 0)
    outer_k = jnp.where(z == 0, places - 1, 1)
    stores.append(pltpu.make_async_copy(terms.at[outer_k], outer_out, store.at[2]))
    stores += [pltpu.make_async_copy(terms.at[k], out, store.at[3 + k]) for k, out in enumerate(outs)]
    for copy in stores[2:]:
        copy.start()
    for copy in stores:
        copy.wait()


def in_vmem(count):
    return [pl.BlockSpec(memory_space=pltpu.VMEM)] * count


IN_SMEM = pl.BlockSpec(memory_space=pltpu.SMEM)


def pack(pieces, x, gate, up, down, shuffle):
    rows, hidden_width = gate.shape
    sizes = [(rows * hidden_width + down.size // 2) * piece // sum(pieces) // LANES for piece in pieces]
    return pl.pallas_call(
        functools.partial(pack_kernel, pieces),
        out_shape=[jax.ShapeDtypeStruct((size, LANES), BF) for size in sizes for _ in range(2)],
        in_specs=[IN_SMEM] + in_vmem(4),
        out_specs=in_vmem(2 * len(pieces)),
        compiler_params=pltpu.CompilerParams(vmem_limit_bytes=VMEM_BYTES // 2),
    )(x, gate, up, down, shuffle)


def unpack(pieces, x, packed, shuffle, gate_shape, down_shape):
    return pl.pallas_call(
        functools.partial(unpack_kernel, pieces),
        out_shape=[jax.ShapeDtypeStruct(shape, F32) for shape in (gate_shape, gate_shape, down_shape)],
        in_specs=[IN_SMEM] + in_vmem(len(packed) + 1),
        out_specs=in_vmem(3),
        compiler_params=pltpu.CompilerParams(vmem_limit_bytes=VMEM_BYTES // 2),
    )(x, *packed, shuffle)


def expert(z, places, units, weights, mine, theirs, earlier=()):
    size = weights[0].shape[0]
    slots, width = mine.shape[0], mine.shape[1] // 2
    rows = 2 * slots
    row_shape, term_shape = jax.ShapeDtypeStruct(mine.shape, BF), jax.ShapeDtypeStruct((size, LANES), BF)
    return pl.pallas_call(
        functools.partial(expert_kernel, len(earlier) // 2),
        out_shape=[row_shape] * 2 + [term_shape] * 5,
        in_specs=[IN_SMEM] + [pl.BlockSpec(memory_space=pl.ANY)] * (8 + len(earlier)),
        out_specs=[pl.BlockSpec(memory_space=pl.ANY)] * 7,
        scratch_shapes=[
            pltpu.VMEM((places, size, LANES), BF),
            pltpu.VMEM((rows, width), BF),
            pltpu.VMEM((rows, width), BF),
            pltpu.VMEM((width, 2 * units), BF),
            pltpu.VMEM((units, width), BF),
            pltpu.VMEM((rows, 2 * units), F32),
            pltpu.VMEM((rows, units), F32),
            pltpu.VMEM((rows, units), BF),
            pltpu.VMEM((rows, 2 * units), BF),
            pltpu.VMEM((units, width), BF),
            pltpu.VMEM((slots, 2 * width), BF),
            pltpu.VMEM((slots, 2 * width), BF),
            pltpu.VMEM((places, size, LANES), BF),
            pltpu.SemaphoreType.DMA((places + 6,)),
            pltpu.SemaphoreType.DMA((7,)),
        ],
        compiler_params=pltpu.CompilerParams(vmem_limit_bytes=VMEM_BYTES),
        cost_estimate=pl.CostEstimate(
            flops=18 * rows * width * units, bytes_accessed=16 * 2**20, transcendentals=rows * units
        ),
    )(z, *weights, mine, theirs, *earlier)


def local(tokens, expert_ids, gate_probs, w_gate, w_up, w_down, d_out):
    g = Grid()
    rows, topk = expert_ids.shape
    width = tokens.shape[1]
    hidden_width = w_gate.shape[2]
    half = hidden_width // 2
    experts = g.experts
    cap = rows * topk * 9 // (8 * experts)
    slots = experts * cap
    first = g.c == 0
    even = g.x == 0

    block = hidden_width // g.dps
    part = block // 2
    pieces = (2 * part // 3, part // 3)
    in_kernels = g.zs == 4 and slots % 16 == 0 and part % 48 == 0 and all(2 * p * g.dps % LANES == 0 for p in pieces)
    if not in_kernels:
        pieces = (part,)
    shuffle = shuffle_matrix(g.x, g.dps, hidden_width, pieces)

    def out_a(z, x, q, c):
        return z, c, q, x

    def out_b(z, x, q, c):
        return z, c, q, 1 - x

    def back_a(z, x, q, c):
        return z, c, q, x

    def back_b(z, x, q, c):
        return z, 1 - c, q, x

    def spread(part_a, part_b):
        got_a, got_b = g.send(part_a, out_a), g.send(part_b, out_b)
        return jnp.concatenate([jnp.where(first, got_a, got_b), jnp.where(first, got_b, got_a)], axis=0)

    def unspread(both):
        n = both.shape[0] // 2
        low, high = both[:n], both[n:]
        return g.send(jnp.where(first, low, high), back_a), g.send(jnp.where(first, high, low), back_b)

    expert_iota = jnp.arange(experts, dtype=jnp.int32)
    chosen = expert_ids[:, :, None] == expert_iota
    named = jnp.any(chosen, axis=1).astype(BF)
    token_iota = jnp.arange(rows, dtype=jnp.int32)
    earlier = (token_iota[:, None] > token_iota[None, :]).astype(BF)
    before = dot(earlier, named)
    slot = jnp.sum(jnp.where(chosen, before[:, None, :], 0.0), axis=2).astype(jnp.int32)
    relative = ((expert_ids // 2 - g.q + g.qs) % g.qs) * 2 + ((expert_ids % 2) ^ g.x)
    dest = relative * cap + slot
    slot_iota = jnp.arange(slots, dtype=jnp.int32)
    pair = dest[:, :, None] == slot_iota
    placing = jnp.any(pair, axis=1).astype(BF)
    weighted = jnp.sum(jnp.where(pair, gate_probs[:, :, None], 0.0), axis=1)
    slot_probs = jnp.sum(weighted, axis=0)

    def member(r, sign):
        def move(z, x, q, c):
            return z, x ^ (r % 2), (q + sign * (r // 2)) % g.qs, c

        return move

    def other_core(z, x, q, c):
        return z, x, q, 1 - c

    def exchange(value, sign):
        got = [value[:cap]] + [g.send(value[r * cap:(r + 1) * cap], member(r, sign)) for r in range(1, experts)]
        return jnp.concatenate(got, axis=0)

    line_width = width // g.zs
    turned = lax.dynamic_slice(jnp.concatenate([tokens, tokens], axis=1), (0, g.z * line_width), (rows, width))
    sent = jnp.concatenate(
        [
            dot(placing, turned, ((0,), (0,))).astype(BF),
            (slot_probs[:, None] * dot(placing, d_out, ((0,), (0,)))).astype(BF),
        ],
        axis=1,
    )
    shapes = w_gate.shape[1:], w_down.shape[1:]
    together = lax.optimization_barrier
    if in_kernels:
        place_x, place_z = g.x.reshape(1).astype(jnp.int32), g.z.reshape(1).astype(jnp.int32)
        units = [piece * g.dps for piece in pieces]
        a, b, a2, b2 = pack(pieces, place_x, w_gate[0], w_up[0], w_down[0], shuffle)
        ups, downs, passing = {0: 1, 1: 2, 2: 3}, {1: 0, 2: 1, 3: 2}, {2: 3, 1: 0}
        outward, inward_up, inward_down = {0: 1, 3: 2}, {0: 1, 1: 2}, {3: 2, 2: 1}
        to_last = g.z == 2

        shard, a2, b2 = together((spread(a, b), a2, b2))
        up, down = g.hop(shard, ups), g.hop(shard, downs)
        shard2, sent = together((spread(a2, b2), sent))
        up, down, shard2 = together((up, down, shard2))
        up_2, down_2 = g.hop(up, {1: 2, 2: 3}), g.hop(down, {1: 0, 2: 1})
        up2, down2 = g.hop(shard2, ups), g.hop(shard2, downs)
        up_2, down_2, mine = together((up_2, down_2, exchange(sent, 1)))
        theirs = g.send(mine, other_core)
        last = g.hop(jnp.where(to_last, up_2, down_2), passing)
        up2, down2, up_2, down_2 = together((up2, down2, up_2, down_2))
        up2_2, down2_2 = g.hop(up2, {1: 2, 2: 3}), g.hop(down2, {1: 0, 2: 1})
        keep, give, outer, *terms = expert(
            place_z, g.zs, units[0], (shard, up, down, up_2, down_2, last), mine, theirs
        )
        up2_2, down2_2, outer, keep, give = together((up2_2, down2_2, outer, keep, give))
        last2 = g.hop(jnp.where(to_last, up2_2, down2_2), passing)
        begun = g.hop(outer, outward)
        keep, give, outer2, *terms2 = expert(
            place_z, g.zs, units[1], (shard2, up2, down2, up2_2, down2_2, last2), mine, theirs, (keep, give)
        )
        begun, give, outer2 = together((begun, give, outer2))
        middle = added(terms[2], begun)
        sum_up, sum_down = g.hop(middle, inward_up), g.hop(middle, inward_down)
        given = g.send(give, other_core)
        begun2 = g.hop(outer2, outward)
        sum_up, sum_down, keep = together((sum_up, sum_down, keep))
        sum_up, sum_down = g.hop(added(terms[1], sum_up), ups), g.hop(added(terms[3], sum_down), downs)
        begun2, given, keep = together((begun2, given, keep))
        middle2, sums = together((added(terms2[2], begun2), added(keep, given)))
        sum_up2, sum_down2 = g.hop(middle2, inward_up), g.hop(middle2, inward_down)
        sums = sums.reshape(g.qs, 2, cap, 2 * width)
        near = jnp.stack([sums[:, 0], g.send(sums[:, 1], lambda z, x, q, c: (z, 1 - x, q, c))], axis=1)
        sum_up, sum_down = together((sum_up, sum_down))
        grad = added(terms[0], sum_up, sum_down)
        sum_up2, sum_down2, near = together((sum_up2, sum_down2, near))
        sum_up2, sum_down2 = g.hop(added(terms2[1], sum_up2), ups), g.hop(added(terms2[3], sum_down2), downs)
        got = jnp.concatenate(
            [near[0]] + [g.send(near[d], lambda z, x, q, c, d=d: (z, x, (q - d) % g.qs, c)) for d in range(1, g.qs)]
        ).reshape(slots, 2 * width)
        grads = unspread(grad)
        sum_up2, sum_down2, got, grads = together((sum_up2, sum_down2, got, grads))
        grads += unspread(added(terms2[0], sum_up2, sum_down2))
        d_w_gate, d_w_up, d_w_down = unpack(pieces, place_x, grads, shuffle, *shapes)
    else:
        gate_cols, up_cols = dot(w_gate[0], shuffle).astype(BF), dot(w_up[0], shuffle).astype(BF)
        gate_up_shard = spread(
            jnp.concatenate([gate_cols[:, :half], up_cols[:, :half]], axis=1),
            jnp.concatenate([gate_cols[:, half:], up_cols[:, half:]], axis=1),
        )
        down_low, down_high = w_down[0, :part], w_down[0, part:]
        down_shard = spread(jnp.where(even, down_low, down_high), jnp.where(even, down_high, down_low))
        gate_up = jnp.concatenate(g.line(gate_up_shard), axis=0)
        down = jnp.concatenate(g.straight(g.line(down_shard)), axis=0)
        mine = exchange(sent, 1)
        inputs = jnp.concatenate([mine, g.send(mine, other_core)], axis=0)
        arrived, d_produced = inputs[:, :width], inputs[:, width:]
        pre = dot(arrived, gate_up)
        gate_pre, up_pre = pre[:, :half], pre[:, half:]
        sig = jax.nn.sigmoid(gate_pre)
        act = gate_pre * sig
        hidden = (act * up_pre).astype(BF)
        d_hidden = dot(d_produced, down, ((1,), (1,)))
        d_gate = (d_hidden * up_pre * sig * (1.0 + gate_pre * (1.0 - sig))).astype(BF)
        d_up = (d_hidden * act).astype(BF)
        d_both = jnp.concatenate([d_gate, d_up], axis=1)
        down_part = dot(hidden, d_produced, ((0,), (0,))).astype(BF)
        both_part = dot(arrived, d_both, ((0,), (0,))).astype(BF)
        partial = jnp.concatenate([dot(hidden, down), dot(d_both, gate_up, ((1,), (1,)))], axis=1).astype(BF)
        got = exchange(added(partial[:slots], g.send(partial[slots:], other_core)), -1)
        down_a, down_b = unspread(
            g.line_sum(
                lambda k: lax.dynamic_slice_in_dim(down_part, ((g.z + k) % g.zs) * (2 * part), 2 * part)
            )
        )
        d_w_down = jnp.where(
            even, jnp.concatenate([down_a, down_b], axis=0), jnp.concatenate([down_b, down_a], axis=0)
        ).astype(F32)
        both_a, both_b = unspread(g.line_sum(lambda k: both_part[k * line_width:(k + 1) * line_width]))
        d_w_gate, d_w_up = (
            dot(jnp.concatenate([both_a[:, cols], both_b[:, cols]], axis=1), shuffle, ((1,), (1,)))
            for cols in (slice(0, half), slice(half, None))
        )
    returned, back_rows = got[:, :width], got[:, width:]

    high = lax.reduce_precision(weighted, 8, 7)
    mixed = (dot(high.astype(BF), returned) + dot((weighted - high).astype(BF), returned)).astype(BF)
    products = dot(d_out, returned, ((1,), (1,)))
    d_probs = jnp.sum(jnp.where(pair, products[:, None, :], 0.0), axis=2)
    d_turned = dot(placing, back_rows).astype(BF)
    d_tokens = lax.dynamic_slice(
        jnp.concatenate([d_turned, d_turned], axis=1), (0, (g.zs - g.z) * line_width), (rows, width)
    )

    return (mixed, d_tokens, d_probs, d_w_gate[None], d_w_up[None], d_w_down[None])


def solution(mesh):
    rows = P(("dp", "expert"), None)
    weight = P("expert", "dp", None)
    return jax.shard_map(
        local,
        mesh=mesh,
        in_specs=(rows, rows, rows, weight, weight, weight, rows),
        out_specs=(rows, rows, rows, weight, weight, weight),
        check_vma=False,
    )
```

```python
import functools

import jax
import jax.numpy as jnp
from jax import lax
from jax.experimental import pallas as pl
from jax.experimental.pallas import tpu as pltpu
from jax.sharding import PartitionSpec as P

BF = jnp.bfloat16
F32 = jnp.float32
BOTH = ("dp", "expert")


def dot(a, b, dims=((1,), (0,))):
    return lax.dot_general(a, b, (dims, ((), ())), preferred_element_type=F32)


def tie(value, *others):
    return lax.optimization_barrier((value,) + others)[0]


def added(*terms):
    return sum(t.astype(F32) for t in terms).astype(BF)


class Grid:
    def __init__(self):
        self.dps, self.experts = lax.axis_size("dp"), lax.axis_size("expert")
        self.zs, self.qs = self.dps // 2, self.experts // 2
        dp, ex = lax.axis_index("dp"), lax.axis_index("expert")
        self.z, self.x, self.q, self.c = dp // 2, dp % 2, ex // 2, ex % 2

    def send(self, value, move):
        pairs = []
        for z in range(self.zs):
            for x in range(2):
                for q in range(self.qs):
                    for c in range(2):
                        to = move(z, x, q, c)
                        if to is not None:
                            pairs.append((self.flat(z, x, q, c), self.flat(*to)))
        return lax.ppermute(value, BOTH, pairs)

    def flat(self, z, x, q, c):
        return (z * 2 + x) * self.experts + q * 2 + c

    def hop(self, value, where):
        return self.send(value, lambda z, x, q, c: (where[z], x, q, c) if z in where else None)

    def line(self, shard):
        n = self.zs
        ups, downs = [shard], [shard]
        for s in range(1, n):
            ups.append(self.hop(ups[-1], {i: i + 1 for i in range(s - 1, n - 1)}))
            downs.append(self.hop(downs[-1], {i: i - 1 for i in range(1, n - s + 1)}))
        return [shard] + [jnp.where(self.z + s < n, downs[s], ups[n - s]) for s in range(1, n)]

    def straight(self, blocks):
        n = self.zs
        rows = []
        for j in range(n):
            row = blocks[j]
            for z in range(1, n):
                row = jnp.where(self.z == z, blocks[(j - z) % n], row)
            rows.append(row)
        return rows

    def line_sum(self, block):
        n = self.zs
        up, down = self.hop(block(n - 1), {0: 1}), self.hop(block(1), {n - 1: n - 2})
        for r in range(2, n):
            up = self.hop(added(block(n - r), up), {i: i + 1 for i in range(r)})
            down = self.hop(added(block(r), down), {i: i - 1 for i in range(n - r, n)})
        return added(block(0), up, down)


LANES = 256
VMEM_BYTES = 48 * 2**20


def shuffle_matrix(x, dps, hidden_width, pieces):
    block, half = hidden_width // dps, hidden_width // 2
    sources, start = [], 0
    for piece in pieces:
        unit = jnp.arange(piece * dps, dtype=jnp.int32)
        sources.append((unit // piece) * block + start + unit % piece)
        start += piece
    low = jnp.concatenate(sources)
    source = jnp.concatenate([low + x * (block // 2), low + (1 - x) * (block // 2)])
    return (jnp.arange(hidden_width, dtype=jnp.int32)[:, None] == source[None, :]).astype(BF)


def pack_kernel(pieces, x_ref, gate_ref, up_ref, down_ref, shuffle_ref, *outs):
    rows, hidden_width = gate_ref.shape
    half, block = hidden_width // 2, down_ref.shape[0]
    shuffle = shuffle_ref[...]
    gate, up = dot(gate_ref[...], shuffle).astype(BF), dot(up_ref[...], shuffle).astype(BF)
    x = x_ref[0]
    done = 0
    for number, piece in enumerate(pieces):
        units = piece * half // sum(pieces)
        count = 2 * units // LANES
        for side, start in ((0, x), (1, 1 - x)):
            ref = outs[2 * number + side]
            at = side * half + done * units // piece
            both = jnp.concatenate([gate[:, at:at + units], up[:, at:at + units]], axis=1)
            for i in range(count):
                ref[i * rows:(i + 1) * rows, :] = both[:, i * LANES:(i + 1) * LANES]
            source = pl.ds(pl.multiple_of(start * (block // 2) + done, 16), piece)
            for j in range(down_ref.shape[1] // LANES):
                to = count * rows + j * piece
                ref[to:to + piece, :] = down_ref[source, j * LANES:(j + 1) * LANES]
        done += piece


def unpack_kernel(pieces, x_ref, *refs):
    packed, (shuffle_ref, gate_ref, up_ref, down_ref) = refs[:-4], refs[-4:]
    rows, hidden_width = gate_ref.shape
    half, block = hidden_width // 2, down_ref.shape[0]
    x = x_ref[0]
    gates, ups = [[], []], [[], []]
    done = 0
    for number, piece in enumerate(pieces):
        units = piece * half // sum(pieces)
        count = 2 * units // LANES
        for side, start in ((0, x), (1, 1 - x)):
            ref = packed[2 * number + side]
            both = jnp.concatenate([ref[i * rows:(i + 1) * rows, :] for i in range(count)], axis=1)
            gates[side].append(both[:, :units])
            ups[side].append(both[:, units:])
            to = pl.ds(pl.multiple_of(start * (block // 2) + done, 16), piece)
            for j in range(down_ref.shape[1] // LANES):
                at = count * rows + j * piece
                down_ref[to, j * LANES:(j + 1) * LANES] = ref[at:at + piece, :].astype(F32)
        done += piece
    shuffle = shuffle_ref[...]
    gate_ref[...] = dot(jnp.concatenate(gates[0] + gates[1], axis=1), shuffle, ((1,), (1,)))
    up_ref[...] = dot(jnp.concatenate(ups[0] + ups[1], axis=1), shuffle, ((1,), (1,)))


def expert_kernel(z_ref, own, up, down, up_2, down_2, last, mine, theirs, *refs):
    weight_outs, (hidden_out, d_both_out, outer_out), outs, refs = refs[:2], refs[2:5], refs[5:9], refs[9:]
    packed, x, grads, gate_up, w_down, pre, d_hidden, hidden, d_both, d_down, terms, load, store = refs
    places, size, _ = packed.shape
    rows, width = x.shape
    slots = rows // 2
    line = width // places
    part_rows = line // 2
    units = w_down.shape[0]
    piece = units // places // 2
    count, columns = 2 * units // LANES, width // LANES
    size_half = size // 2
    z = z_ref[0]

    loads = [
        pltpu.make_async_copy(a, b, load.at[places + n])
        for n, (a, b) in enumerate(
            (
                (mine.at[:, :width], x.at[:slots]),
                (theirs.at[:, :width], x.at[slots:]),
                (mine.at[:, width:], grads.at[:slots]),
                (theirs.at[:, width:], grads.at[slots:]),
            )
        )
    ]
    for copy in loads[:2]:
        copy.start()
    pltpu.make_async_copy(own, packed.at[0], load.at[0]).start()
    for s, is_one, one, other in (
        (1, z == places - 1, last, down),
        (2, z < 2, down_2, up_2),
        (3, z == 0, last, up),
    ):
        @pl.when(is_one)
        def _():
            pltpu.make_async_copy(one, packed.at[s], load.at[s]).start()

        @pl.when(jnp.logical_not(is_one))
        def _():
            pltpu.make_async_copy(other, packed.at[s], load.at[s]).start()

    for copy in loads[2:]:
        copy.start()

    def down_rows(k, h):
        return pl.ds(pl.multiple_of(lax.rem(z + k, places) * (2 * piece) + h * piece, 16), piece)

    for copy in loads[:2]:
        copy.wait()
    for s in range(places):
        pltpu.make_async_copy(own, packed.at[s], load.at[s]).wait()
        for h in range(2):
            for i in range(count):
                at = h * size_half + i * part_rows
                to = s * line + h * part_rows
                gate_up[to:to + part_rows, i * LANES:(i + 1) * LANES] = packed[s, at:at + part_rows, :]
            for j in range(columns):
                at = h * size_half + count * part_rows + j * piece
                w_down[down_rows(s, h), j * LANES:(j + 1) * LANES] = packed[s, at:at + piece, :]
        block = slice(s * line, (s + 1) * line)
        for i in range(count):
            cols = slice(i * LANES, (i + 1) * LANES)
            product = dot(x[:, block], gate_up[block, cols])
            pre[:, cols] = product if s == 0 else pre[:, cols] + product

    stores = []

    def store_to(out, value):
        stores.append(pltpu.make_async_copy(value, out, store.at[len(stores)]))
        stores[-1].start()

    store_to(weight_outs[0], gate_up)
    store_to(weight_outs[1], w_down)
    step = 64 if rows % 64 == 0 else 16

    def activate(r, _):
        at = pl.ds(pl.multiple_of(r * step, 16), step)
        gate_pre, up_pre = pre[at, :units], pre[at, units:]
        sig = 1.0 / (1.0 + jnp.exp(-gate_pre))
        act = gate_pre * sig
        hidden[at, :] = (act * up_pre).astype(BF)
        pre[at, :units] = up_pre * sig * (1.0 + gate_pre * (1.0 - sig))
        pre[at, units:] = act
        return 0

    lax.fori_loop(0, rows // step, activate, 0)
    store_to(hidden_out, hidden)
    for copy in loads[2:]:
        copy.wait()
    d_hidden[...] = dot(grads[...], w_down[...], ((1,), (1,)))

    def differentiate(r, _):
        at = pl.ds(pl.multiple_of(r * step, 16), step)
        d_h = d_hidden[at, :]
        d_both[at, :units] = (d_h * pre[at, :units]).astype(BF)
        d_both[at, units:] = (d_h * pre[at, units:]).astype(BF)
        return 0

    lax.fori_loop(0, rows // step, differentiate, 0)
    store_to(d_both_out, d_both)
    d_down[...] = dot(hidden[...], grads[...], ((0,), (0,))).astype(BF)

    for k in (places - 1, 1, 2, 0):
        for h in range(2):
            from_cols = slice(k * line + h * part_rows, k * line + (h + 1) * part_rows)
            weights = dot(x[:, from_cols], d_both[...], ((0,), (0,))).astype(BF)
            for i in range(count):
                to = h * size_half + i * part_rows
                terms[k, to:to + part_rows, :] = weights[:, i * LANES:(i + 1) * LANES]
            for j in range(columns):
                to = h * size_half + count * part_rows + j * piece
                terms[k, to:to + piece, :] = d_down[down_rows(k, h), j * LANES:(j + 1) * LANES]
        store_to(outs[k], terms.at[k])
        if k == 1:
            store_to(outer_out, terms.at[jnp.where(z == 0, places - 1, 1)])
    for copy in stores:
        copy.wait()


def rows_kernel(chunks, *refs):
    keep, give = refs[-2:]
    slots = keep.shape[0]

    def add(pairs, dims):
        total = sum(dot(a[...], b[...], dims) for a, b in pairs).astype(BF)
        keep[...], give[...] = total[:slots], total[slots:]

    chunked = [refs[4 * n:4 * n + 4] for n in range(chunks)]

    @pl.when(pl.program_id(0) < pl.num_programs(0) // 2)
    def _():
        add([(hidden, w_down) for _, w_down, hidden, _ in chunked], ((1,), (0,)))

    @pl.when(pl.program_id(0) >= pl.num_programs(0) // 2)
    def _():
        add([(d_both, gate_up) for gate_up, _, _, d_both in chunked], ((1,), (1,)))


def in_vmem(count):
    return [pl.BlockSpec(memory_space=pltpu.VMEM)] * count


IN_SMEM = pl.BlockSpec(memory_space=pltpu.SMEM)


def pack(pieces, x, gate, up, down, shuffle):
    rows, hidden_width = gate.shape
    sizes = [(rows * hidden_width + down.size // 2) * piece // sum(pieces) // LANES for piece in pieces]
    return pl.pallas_call(
        functools.partial(pack_kernel, pieces),
        out_shape=[jax.ShapeDtypeStruct((size, LANES), BF) for size in sizes for _ in range(2)],
        in_specs=[IN_SMEM] + in_vmem(4),
        out_specs=in_vmem(2 * len(pieces)),
        compiler_params=pltpu.CompilerParams(vmem_limit_bytes=VMEM_BYTES // 2),
    )(x, gate, up, down, shuffle)


def unpack(pieces, x, packed, shuffle, gate_shape, down_shape):
    return pl.pallas_call(
        functools.partial(unpack_kernel, pieces),
        out_shape=[jax.ShapeDtypeStruct(shape, F32) for shape in (gate_shape, gate_shape, down_shape)],
        in_specs=[IN_SMEM] + in_vmem(len(packed) + 1),
        out_specs=in_vmem(3),
        compiler_params=pltpu.CompilerParams(vmem_limit_bytes=VMEM_BYTES // 2),
    )(x, *packed, shuffle)


def expert(z, places, units, weights, mine, theirs):
    size = weights[0].shape[0]
    slots, width = mine.shape[0], mine.shape[1] // 2
    rows = 2 * slots
    for_rows = [
        jax.ShapeDtypeStruct(shape, BF) for shape in ((width, 2 * units), (units, width), (rows, units), (rows, 2 * units))
    ]
    outs = pl.pallas_call(
        expert_kernel,
        out_shape=for_rows + [jax.ShapeDtypeStruct((size, LANES), BF)] * 5,
        in_specs=[IN_SMEM] + [pl.BlockSpec(memory_space=pl.ANY)] * 8,
        out_specs=[pl.BlockSpec(memory_space=pl.ANY)] * 9,
        scratch_shapes=[
            pltpu.VMEM((places, size, LANES), BF),
            pltpu.VMEM((rows, width), BF),
            pltpu.VMEM((rows, width), BF),
            pltpu.VMEM((width, 2 * units), BF),
            pltpu.VMEM((units, width), BF),
            pltpu.VMEM((rows, 2 * units), F32),
            pltpu.VMEM((rows, units), F32),
            pltpu.VMEM((rows, units), BF),
            pltpu.VMEM((rows, 2 * units), BF),
            pltpu.VMEM((units, width), BF),
            pltpu.VMEM((places, size, LANES), BF),
            pltpu.SemaphoreType.DMA((places + 4,)),
            pltpu.SemaphoreType.DMA((9,)),
        ],
        compiler_params=pltpu.CompilerParams(vmem_limit_bytes=VMEM_BYTES),
        cost_estimate=pl.CostEstimate(
            flops=12 * rows * width * units, bytes_accessed=16 * 2**20, transcendentals=rows * units
        ),
    )(z, *weights, mine, theirs)
    return outs[:4], outs[4], outs[5:]


def token_rows(chunks, slots, width):
    tile = 2 * LANES
    tiles = width // tile
    in_specs = []
    for gate_up, w_down, hidden, d_both in chunks:
        in_specs += [
            pl.BlockSpec((tile, gate_up.shape[1]), lambda n: (jnp.maximum(n - tiles, 0), 0)),
            pl.BlockSpec((w_down.shape[0], tile), lambda n: (0, jnp.minimum(n, tiles - 1))),
            pl.BlockSpec(hidden.shape, lambda n: (0, 0)),
            pl.BlockSpec(d_both.shape, lambda n: (0, 0)),
        ]
    units = sum(chunk[1].shape[0] for chunk in chunks)
    return pl.pallas_call(
        functools.partial(rows_kernel, len(chunks)),
        grid=(2 * tiles,),
        out_shape=[jax.ShapeDtypeStruct((slots, 2 * width), BF)] * 2,
        in_specs=in_specs,
        out_specs=[pl.BlockSpec((slots, tile), lambda n: (0, n))] * 2,
        compiler_params=pltpu.CompilerParams(vmem_limit_bytes=VMEM_BYTES // 2),
        cost_estimate=pl.CostEstimate(
            flops=12 * slots * width * units, bytes_accessed=12 * 2**20, transcendentals=0
        ),
    )(*(array for chunk in chunks for array in chunk))


def local(tokens, expert_ids, gate_probs, w_gate, w_up, w_down, d_out):
    g = Grid()
    rows, topk = expert_ids.shape
    width = tokens.shape[1]
    hidden_width = w_gate.shape[2]
    half = hidden_width // 2
    experts = g.experts
    cap = rows * topk * 9 // (8 * experts)
    slots = experts * cap
    first = g.c == 0
    even = g.x == 0

    block = hidden_width // g.dps
    part = block // 2
    pieces = (2 * part // 3, part // 3)
    in_kernels = g.zs == 4 and slots % 16 == 0 and part % 48 == 0 and all(2 * p * g.dps % LANES == 0 for p in pieces)
    if not in_kernels:
        pieces = (part,)
    shuffle = shuffle_matrix(g.x, g.dps, hidden_width, pieces)

    def out_a(z, x, q, c):
        return z, c, q, x

    def out_b(z, x, q, c):
        return z, c, q, 1 - x

    def back_a(z, x, q, c):
        return z, c, q, x

    def back_b(z, x, q, c):
        return z, 1 - c, q, x

    def spread(part_a, part_b):
        got_a, got_b = g.send(part_a, out_a), g.send(part_b, out_b)
        return jnp.concatenate([jnp.where(first, got_a, got_b), jnp.where(first, got_b, got_a)], axis=0)

    def unspread(both):
        n = both.shape[0] // 2
        low, high = both[:n], both[n:]
        return g.send(jnp.where(first, low, high), back_a), g.send(jnp.where(first, high, low), back_b)

    expert_iota = jnp.arange(experts, dtype=jnp.int32)
    chosen = expert_ids[:, :, None] == expert_iota
    named = jnp.any(chosen, axis=1).astype(BF)
    token_iota = jnp.arange(rows, dtype=jnp.int32)
    earlier = (token_iota[:, None] > token_iota[None, :]).astype(BF)
    before = dot(earlier, named)
    slot = jnp.sum(jnp.where(chosen, before[:, None, :], 0.0), axis=2).astype(jnp.int32)
    relative = ((expert_ids // 2 - g.q + g.qs) % g.qs) * 2 + ((expert_ids % 2) ^ g.x)
    dest = relative * cap + slot
    slot_iota = jnp.arange(slots, dtype=jnp.int32)
    pair = dest[:, :, None] == slot_iota
    placing = jnp.any(pair, axis=1).astype(BF)
    weighted = jnp.sum(jnp.where(pair, gate_probs[:, :, None], 0.0), axis=1)
    slot_probs = jnp.sum(weighted, axis=0)

    def member(r, sign):
        def move(z, x, q, c):
            return z, x ^ (r % 2), (q + sign * (r // 2)) % g.qs, c

        return move

    def other_core(z, x, q, c):
        return z, x, q, 1 - c

    def exchange(value, sign):
        got = [value[:cap]] + [g.send(value[r * cap:(r + 1) * cap], member(r, sign)) for r in range(1, experts)]
        return jnp.concatenate(got, axis=0)

    line_width = width // g.zs
    turned = lax.dynamic_slice(jnp.concatenate([tokens, tokens], axis=1), (0, g.z * line_width), (rows, width))
    sent = jnp.concatenate(
        [
            dot(placing, turned, ((0,), (0,))).astype(BF),
            (slot_probs[:, None] * dot(placing, d_out, ((0,), (0,)))).astype(BF),
        ],
        axis=1,
    )
    shapes = w_gate.shape[1:], w_down.shape[1:]
    together = lax.optimization_barrier
    if in_kernels:
        place_x, place_z = g.x.reshape(1).astype(jnp.int32), g.z.reshape(1).astype(jnp.int32)
        units = [piece * g.dps for piece in pieces]
        a, b, a2, b2 = pack(pieces, place_x, w_gate[0], w_up[0], w_down[0], shuffle)
        ups, downs, passing = {0: 1, 1: 2, 2: 3}, {1: 0, 2: 1, 3: 2}, {2: 3, 1: 0}
        outward, inward_up, inward_down = {0: 1, 3: 2}, {0: 1, 1: 2}, {3: 2, 2: 1}
        to_last = g.z == 2

        shard, a2, b2 = together((spread(a, b), a2, b2))
        up, down = g.hop(shard, ups), g.hop(shard, downs)
        shard2, sent = together((spread(a2, b2), sent))
        up, down = together((up, down))
        up_2, down_2 = g.hop(up, {1: 2, 2: 3}), g.hop(down, {1: 0, 2: 1})
        shard2, mine = together((shard2, exchange(sent, 1)))
        up2, down2 = g.hop(shard2, ups), g.hop(shard2, downs)
        up_2, down_2, up2, down2, mine = together((up_2, down_2, up2, down2, mine))
        last = g.hop(jnp.where(to_last, up_2, down_2), passing)
        up2_2, down2_2 = g.hop(up2, {1: 2, 2: 3}), g.hop(down2, {1: 0, 2: 1})
        theirs = g.send(mine, other_core)
        chunk, outer, terms = expert(
            place_z, g.zs, units[0], (shard, up, down, up_2, down_2, last), mine, theirs
        )
        up2_2, down2_2, outer = together((up2_2, down2_2, outer))
        last2 = g.hop(jnp.where(to_last, up2_2, down2_2), passing)
        begun = g.hop(outer, outward)
        chunk2, outer2, terms2 = expert(
            place_z, g.zs, units[1], (shard2, up2, down2, up2_2, down2_2, last2), mine, theirs
        )
        begun, outer2, chunk2 = together((begun, outer2, chunk2))
        middle, outer2, chunk2 = together((added(terms[2], begun), outer2, chunk2))
        sum_up, sum_down = g.hop(middle, inward_up), g.hop(middle, inward_down)
        begun2 = g.hop(outer2, outward)
        keep, give = token_rows((chunk, chunk2), slots, width)
        sums = added(keep, g.send(give, other_core)).reshape(g.qs, 2, cap, 2 * width)
        sum_up, sum_down, sums = together((sum_up, sum_down, sums))
        far_rows = g.send(sums[:, 1], lambda z, x, q, c: (z, 1 - x, q, c))
        sum_up, sum_down = g.hop(added(terms[1], sum_up), ups), g.hop(added(terms[3], sum_down), downs)
        middle2 = added(terms2[2], begun2)
        sum_up2, sum_down2 = g.hop(middle2, inward_up), g.hop(middle2, inward_down)
        grad = added(terms[0], sum_up, sum_down)
        far_rows = tie(far_rows, grad)
        near = jnp.stack([sums[:, 0], far_rows], axis=1)
        got = jnp.concatenate(
            [near[0]] + [g.send(near[d], lambda z, x, q, c, d=d: (z, x, (q - d) % g.qs, c)) for d in range(1, g.qs)]
        ).reshape(slots, 2 * width)
        sum_up2, sum_down2 = tie(sum_up2, near), tie(sum_down2, near)
        grads = unspread(grad)
        sum_up2, sum_down2 = g.hop(added(terms2[1], sum_up2), ups), g.hop(added(terms2[3], sum_down2), downs)
        sum_up2, sum_down2, grads = together((sum_up2, sum_down2, grads))
        grad2 = added(terms2[0], sum_up2, sum_down2)
        got = tie(got, grad2)
        grads += unspread(grad2)
        d_w_gate, d_w_up, d_w_down = unpack(pieces, place_x, grads, shuffle, *shapes)
    else:
        gate_cols, up_cols = dot(w_gate[0], shuffle).astype(BF), dot(w_up[0], shuffle).astype(BF)
        gate_up_shard = spread(
            jnp.concatenate([gate_cols[:, :half], up_cols[:, :half]], axis=1),
            jnp.concatenate([gate_cols[:, half:], up_cols[:, half:]], axis=1),
        )
        down_low, down_high = w_down[0, :part], w_down[0, part:]
        down_shard = spread(jnp.where(even, down_low, down_high), jnp.where(even, down_high, down_low))
        gate_up = jnp.concatenate(g.line(gate_up_shard), axis=0)
        down = jnp.concatenate(g.straight(g.line(down_shard)), axis=0)
        mine = exchange(sent, 1)
        inputs = jnp.concatenate([mine, g.send(mine, other_core)], axis=0)
        arrived, d_produced = inputs[:, :width], inputs[:, width:]
        pre = dot(arrived, gate_up)
        gate_pre, up_pre = pre[:, :half], pre[:, half:]
        sig = jax.nn.sigmoid(gate_pre)
        act = gate_pre * sig
        hidden = (act * up_pre).astype(BF)
        d_hidden = dot(d_produced, down, ((1,), (1,)))
        d_gate = (d_hidden * up_pre * sig * (1.0 + gate_pre * (1.0 - sig))).astype(BF)
        d_up = (d_hidden * act).astype(BF)
        d_both = jnp.concatenate([d_gate, d_up], axis=1)
        down_part = dot(hidden, d_produced, ((0,), (0,))).astype(BF)
        both_part = dot(arrived, d_both, ((0,), (0,))).astype(BF)
        partial = jnp.concatenate([dot(hidden, down), dot(d_both, gate_up, ((1,), (1,)))], axis=1).astype(BF)
        got = exchange(added(partial[:slots], g.send(partial[slots:], other_core)), -1)
        down_a, down_b = unspread(
            g.line_sum(
                lambda k: lax.dynamic_slice_in_dim(down_part, ((g.z + k) % g.zs) * (2 * part), 2 * part)
            )
        )
        d_w_down = jnp.where(
            even, jnp.concatenate([down_a, down_b], axis=0), jnp.concatenate([down_b, down_a], axis=0)
        ).astype(F32)
        both_a, both_b = unspread(g.line_sum(lambda k: both_part[k * line_width:(k + 1) * line_width]))
        d_w_gate, d_w_up = (
            dot(jnp.concatenate([both_a[:, cols], both_b[:, cols]], axis=1), shuffle, ((1,), (1,)))
            for cols in (slice(0, half), slice(half, None))
        )
    returned, back_rows = got[:, :width], got[:, width:]

    high = lax.reduce_precision(weighted, 8, 7)
    mixed = (dot(high.astype(BF), returned) + dot((weighted - high).astype(BF), returned)).astype(BF)
    products = dot(d_out, returned, ((1,), (1,)))
    d_probs = jnp.sum(jnp.where(pair, products[:, None, :], 0.0), axis=2)
    d_turned = dot(placing, back_rows).astype(BF)
    d_tokens = lax.dynamic_slice(
        jnp.concatenate([d_turned, d_turned], axis=1), (0, (g.zs - g.z) * line_width), (rows, width)
    )

    return (mixed, d_tokens, d_probs, d_w_gate[None], d_w_up[None], d_w_down[None])


def solution(mesh):
    rows = P(("dp", "expert"), None)
    weight = P("expert", "dp", None)
    return jax.shard_map(
        local,
        mesh=mesh,
        in_specs=(rows, rows, rows, weight, weight, weight, rows),
        out_specs=(rows, rows, rows, weight, weight, weight),
        check_vma=False,
    )
```

```python
import functools

import jax
import jax.numpy as jnp
from jax import lax
from jax.experimental import pallas as pl
from jax.experimental.pallas import tpu as pltpu
from jax.sharding import PartitionSpec as P

BF = jnp.bfloat16
F32 = jnp.float32
BOTH = ("dp", "expert")


def dot(a, b, dims=((1,), (0,))):
    return lax.dot_general(a, b, (dims, ((), ())), preferred_element_type=F32)


def tie(value, *others):
    return lax.optimization_barrier((value,) + others)[0]


def tie_all(values, *others):
    return [tie(value, *others) for value in values]


def added(*terms):
    return sum(t.astype(F32) for t in terms).astype(BF)


class Grid:
    def __init__(self):
        self.dps, self.experts = lax.axis_size("dp"), lax.axis_size("expert")
        self.zs, self.qs = self.dps // 2, self.experts // 2
        dp, ex = lax.axis_index("dp"), lax.axis_index("expert")
        self.z, self.x, self.q, self.c = dp // 2, dp % 2, ex // 2, ex % 2

    def send(self, value, move):
        pairs = []
        for z in range(self.zs):
            for x in range(2):
                for q in range(self.qs):
                    for c in range(2):
                        to = move(z, x, q, c)
                        if to is not None:
                            pairs.append((self.flat(z, x, q, c), self.flat(*to)))
        return lax.ppermute(value, BOTH, pairs)

    def flat(self, z, x, q, c):
        return (z * 2 + x) * self.experts + q * 2 + c

    def hop(self, value, where):
        return self.send(value, lambda z, x, q, c: (where[z], x, q, c) if z in where else None)

    def line(self, shard):
        n = self.zs
        ups, downs = [shard], [shard]
        for s in range(1, n):
            ups.append(self.hop(ups[-1], {i: i + 1 for i in range(s - 1, n - 1)}))
            downs.append(self.hop(downs[-1], {i: i - 1 for i in range(1, n - s + 1)}))
        return [shard] + [jnp.where(self.z + s < n, downs[s], ups[n - s]) for s in range(1, n)]

    def straight(self, blocks):
        n = self.zs
        rows = []
        for j in range(n):
            row = blocks[j]
            for z in range(1, n):
                row = jnp.where(self.z == z, blocks[(j - z) % n], row)
            rows.append(row)
        return rows

    def line_sum(self, block):
        n = self.zs
        up, down = self.hop(block(n - 1), {0: 1}), self.hop(block(1), {n - 1: n - 2})
        for r in range(2, n):
            up = self.hop(added(block(n - r), up), {i: i + 1 for i in range(r)})
            down = self.hop(added(block(r), down), {i: i - 1 for i in range(n - r, n)})
        return added(block(0), up, down)


LANES = 256
VMEM_BYTES = 48 * 2**20


def shuffle_matrix(x, dps, hidden_width, pieces):
    block, half = hidden_width // dps, hidden_width // 2
    sources, start = [], 0
    for piece in pieces:
        unit = jnp.arange(piece * dps, dtype=jnp.int32)
        sources.append((unit // piece) * block + start + unit % piece)
        start += piece
    low = jnp.concatenate(sources)
    source = jnp.concatenate([low + x * (block // 2), low + (1 - x) * (block // 2)])
    return (jnp.arange(hidden_width, dtype=jnp.int32)[:, None] == source[None, :]).astype(BF)


def pack_kernel(pieces, x_ref, gate_in, up_in, down_in, shuffle_ref, a_ref, b_ref, gate_ref, up_ref, down_ref, load):
    loads = [
        pltpu.make_async_copy(source, target, load.at[n])
        for n, (source, target) in enumerate(((gate_in, gate_ref), (up_in, up_ref), (down_in, down_ref)))
    ]
    for copy in loads:
        copy.start()
    rows, hidden_width = gate_ref.shape
    half, block = hidden_width // 2, down_ref.shape[0]
    shuffle = shuffle_ref[...]
    loads[0].wait()
    gate = dot(gate_ref[...], shuffle).astype(BF)
    loads[1].wait()
    up = dot(up_ref[...], shuffle).astype(BF)
    loads[2].wait()
    x = x_ref[0]
    done = base = 0
    for piece in pieces:
        units = piece * half // sum(pieces)
        count, columns = 2 * units // LANES, down_ref.shape[1] // LANES
        for side, (ref, start) in enumerate(((a_ref, x), (b_ref, 1 - x))):
            at = side * half + done * units // piece
            both = jnp.concatenate([gate[:, at:at + units], up[:, at:at + units]], axis=1)
            for i in range(count):
                ref[base + i * rows:base + (i + 1) * rows, :] = both[:, i * LANES:(i + 1) * LANES]
            source = pl.ds(pl.multiple_of(start * (block // 2) + done, 16), piece)
            for j in range(columns):
                to = base + count * rows + j * piece
                ref[to:to + piece, :] = down_ref[source, j * LANES:(j + 1) * LANES]
        done += piece
        base += count * rows + columns * piece


def unpack_kernel(pieces, x_ref, *refs):
    packed, (shuffle_ref, gate_ref, up_ref, down_ref) = refs[:-4], refs[-4:]
    rows, hidden_width = gate_ref.shape
    half, block = hidden_width // 2, down_ref.shape[0]
    x = x_ref[0]
    gates, ups = [[], []], [[], []]
    done = 0
    for number, piece in enumerate(pieces):
        units = piece * half // sum(pieces)
        count = 2 * units // LANES
        for side, start in ((0, x), (1, 1 - x)):
            ref = packed[2 * number + side]
            both = jnp.concatenate([ref[i * rows:(i + 1) * rows, :] for i in range(count)], axis=1)
            gates[side].append(both[:, :units])
            ups[side].append(both[:, units:])
            to = pl.ds(pl.multiple_of(start * (block // 2) + done, 16), piece)
            for j in range(down_ref.shape[1] // LANES):
                at = count * rows + j * piece
                down_ref[to, j * LANES:(j + 1) * LANES] = ref[at:at + piece, :].astype(F32)
        done += piece
    shuffle = shuffle_ref[...]
    gate_ref[...] = dot(jnp.concatenate(gates[0] + gates[1], axis=1), shuffle, ((1,), (1,)))
    up_ref[...] = dot(jnp.concatenate(ups[0] + ups[1], axis=1), shuffle, ((1,), (1,)))


def expert_kernel(offset, z_ref, own, up, down, far, up_2, down_2, mine, theirs, *refs):
    weight_outs, (hidden_out, d_both_out), term_outs, refs = refs[:2], refs[2:4], refs[4:8], refs[8:]
    packed, x, grads, gate_up, w_down, pre, d_hidden, hidden, d_both, d_down, terms, load, store = refs
    places, size, _ = packed.shape
    rows, width = x.shape
    slots = rows // 2
    line = width // places
    part_rows = line // 2
    units = w_down.shape[0]
    piece = units // places // 2
    count, columns = 2 * units // LANES, width // LANES
    size_half = size // 2
    z = z_ref[0]
    own, up, down = (ref.at[offset:offset + size] for ref in (own, up, down))

    loads = [
        pltpu.make_async_copy(a, b, load.at[places + n])
        for n, (a, b) in enumerate(
            (
                (mine.at[:, :width], x.at[:slots]),
                (theirs.at[:, :width], x.at[slots:]),
                (mine.at[:, width:], grads.at[:slots]),
                (theirs.at[:, width:], grads.at[slots:]),
            )
        )
    ]
    for copy in loads[:2]:
        copy.start()
    pltpu.make_async_copy(own, packed.at[0], load.at[0]).start()
    for s, is_one, one, other in (
        (1, z == places - 1, far, down),
        (2, z < 2, down_2, up_2),
        (3, z == 0, far, up),
    ):
        @pl.when(is_one)
        def _():
            pltpu.make_async_copy(one, packed.at[s], load.at[s]).start()

        @pl.when(jnp.logical_not(is_one))
        def _():
            pltpu.make_async_copy(other, packed.at[s], load.at[s]).start()

    for copy in loads[2:]:
        copy.start()

    def down_rows(k, h):
        return pl.ds(pl.multiple_of(lax.rem(z + k, places) * (2 * piece) + h * piece, 16), piece)

    for copy in loads[:2]:
        copy.wait()
    for s in range(places):
        pltpu.make_async_copy(own, packed.at[s], load.at[s]).wait()
        for h in range(2):
            for i in range(count):
                at = h * size_half + i * part_rows
                to = s * line + h * part_rows
                gate_up[to:to + part_rows, i * LANES:(i + 1) * LANES] = packed[s, at:at + part_rows, :]
            for j in range(columns):
                at = h * size_half + count * part_rows + j * piece
                w_down[down_rows(s, h), j * LANES:(j + 1) * LANES] = packed[s, at:at + piece, :]
        block = slice(s * line, (s + 1) * line)
        for i in range(count):
            cols = slice(i * LANES, (i + 1) * LANES)
            product = dot(x[:, block], gate_up[block, cols])
            pre[:, cols] = product if s == 0 else pre[:, cols] + product

    stores = []

    def store_to(out, value):
        stores.append(pltpu.make_async_copy(value, out, store.at[len(stores)]))
        stores[-1].start()

    store_to(weight_outs[0], gate_up)
    store_to(weight_outs[1], w_down)
    step = 64 if rows % 64 == 0 else 16

    def activate(r, _):
        at = pl.ds(pl.multiple_of(r * step, 16), step)
        gate_pre, up_pre = pre[at, :units], pre[at, units:]
        sig = 1.0 / (1.0 + jnp.exp(-gate_pre))
        act = gate_pre * sig
        hidden[at, :] = (act * up_pre).astype(BF)
        pre[at, :units] = up_pre * sig * (1.0 + gate_pre * (1.0 - sig))
        pre[at, units:] = act
        return 0

    lax.fori_loop(0, rows // step, activate, 0)
    store_to(hidden_out, hidden)
    for copy in loads[2:]:
        copy.wait()
    d_hidden[...] = dot(grads[...], w_down[...], ((1,), (1,)))

    def differentiate(r, _):
        at = pl.ds(pl.multiple_of(r * step, 16), step)
        d_h = d_hidden[at, :]
        d_both[at, :units] = (d_h * pre[at, :units]).astype(BF)
        d_both[at, units:] = (d_h * pre[at, units:]).astype(BF)
        return 0

    lax.fori_loop(0, rows // step, differentiate, 0)
    store_to(d_both_out, d_both)
    d_down[...] = dot(hidden[...], grads[...], ((0,), (0,))).astype(BF)

    for k in (places - 1, 1, 2, 0):
        for h in range(2):
            from_cols = slice(k * line + h * part_rows, k * line + (h + 1) * part_rows)
            weights = dot(x[:, from_cols], d_both[...], ((0,), (0,))).astype(BF)
            for i in range(count):
                to = h * size_half + i * part_rows
                terms[k, to:to + part_rows, :] = weights[:, i * LANES:(i + 1) * LANES]
            for j in range(columns):
                to = h * size_half + count * part_rows + j * piece
                terms[k, to:to + piece, :] = d_down[down_rows(k, h), j * LANES:(j + 1) * LANES]
        if k == 1:
            outer = jnp.where(z < 2, places - 1, 1)
            store_to(term_outs[0], terms.at[outer])
            store_to(term_outs[1], terms.at[places - outer])
        elif k != places - 1:
            store_to(term_outs[2 if k else 3], terms.at[k])
    for copy in stores:
        copy.wait()


def rows_kernel(chunks, *refs):
    keep, give = refs[-2:]
    slots = keep.shape[0]

    def add(pairs, dims):
        total = sum(dot(a[...], b[...], dims) for a, b in pairs).astype(BF)
        keep[...], give[...] = total[:slots], total[slots:]

    chunked = [refs[4 * n:4 * n + 4] for n in range(chunks)]

    @pl.when(pl.program_id(0) < pl.num_programs(0) // 2)
    def _():
        add([(hidden, w_down) for _, w_down, hidden, _ in chunked], ((1,), (0,)))

    @pl.when(pl.program_id(0) >= pl.num_programs(0) // 2)
    def _():
        add([(d_both, gate_up) for gate_up, _, _, d_both in chunked], ((1,), (1,)))


def in_vmem(count):
    return [pl.BlockSpec(memory_space=pltpu.VMEM)] * count


IN_SMEM = pl.BlockSpec(memory_space=pltpu.SMEM)


def pack(pieces, x, gate, up, down, shuffle):
    size = (gate.size + down.size // 2) // LANES
    anywhere = pl.BlockSpec(memory_space=pl.ANY)
    return pl.pallas_call(
        functools.partial(pack_kernel, pieces),
        out_shape=[jax.ShapeDtypeStruct((size, LANES), BF)] * 2,
        in_specs=[IN_SMEM] + [anywhere] * 3 + in_vmem(1),
        out_specs=in_vmem(2),
        scratch_shapes=[pltpu.VMEM(w.shape, BF) for w in (gate, up, down)] + [pltpu.SemaphoreType.DMA((3,))],
        compiler_params=pltpu.CompilerParams(vmem_limit_bytes=VMEM_BYTES // 2),
    )(x, gate, up, down, shuffle)


def unpack(pieces, x, packed, shuffle, gate_shape, down_shape):
    return pl.pallas_call(
        functools.partial(unpack_kernel, pieces),
        out_shape=[jax.ShapeDtypeStruct(shape, F32) for shape in (gate_shape, gate_shape, down_shape)],
        in_specs=[IN_SMEM] + in_vmem(len(packed) + 1),
        out_specs=in_vmem(3),
        compiler_params=pltpu.CompilerParams(vmem_limit_bytes=VMEM_BYTES // 2),
    )(x, *packed, shuffle)


def expert(z, places, units, offset, weights, mine, theirs):
    size = weights[-1].shape[0]
    slots, width = mine.shape[0], mine.shape[1] // 2
    rows = 2 * slots
    for_rows = [
        jax.ShapeDtypeStruct(shape, BF) for shape in ((width, 2 * units), (units, width), (rows, units), (rows, 2 * units))
    ]
    outs = pl.pallas_call(
        functools.partial(expert_kernel, offset),
        out_shape=for_rows + [jax.ShapeDtypeStruct((size, LANES), BF)] * 4,
        in_specs=[IN_SMEM] + [pl.BlockSpec(memory_space=pl.ANY)] * 8,
        out_specs=[pl.BlockSpec(memory_space=pl.ANY)] * 8,
        scratch_shapes=[
            pltpu.VMEM((places, size, LANES), BF),
            pltpu.VMEM((rows, width), BF),
            pltpu.VMEM((rows, width), BF),
            pltpu.VMEM((width, 2 * units), BF),
            pltpu.VMEM((units, width), BF),
            pltpu.VMEM((rows, 2 * units), F32),
            pltpu.VMEM((rows, units), F32),
            pltpu.VMEM((rows, units), BF),
            pltpu.VMEM((rows, 2 * units), BF),
            pltpu.VMEM((units, width), BF),
            pltpu.VMEM((places, size, LANES), BF),
            pltpu.SemaphoreType.DMA((places + 4,)),
            pltpu.SemaphoreType.DMA((8,)),
        ],
        compiler_params=pltpu.CompilerParams(vmem_limit_bytes=VMEM_BYTES),
        cost_estimate=pl.CostEstimate(
            flops=12 * rows * width * units, bytes_accessed=16 * 2**20, transcendentals=rows * units
        ),
    )(z, *weights, mine, theirs)
    return outs[:4], outs[4:]


def token_rows(chunks, slots, width):
    tile = 2 * LANES
    tiles = width // tile
    in_specs = []
    for gate_up, w_down, hidden, d_both in chunks:
        in_specs += [
            pl.BlockSpec((tile, gate_up.shape[1]), lambda n: (jnp.maximum(n - tiles, 0), 0)),
            pl.BlockSpec((w_down.shape[0], tile), lambda n: (0, jnp.minimum(n, tiles - 1))),
            pl.BlockSpec(hidden.shape, lambda n: (0, 0)),
            pl.BlockSpec(d_both.shape, lambda n: (0, 0)),
        ]
    units = sum(chunk[1].shape[0] for chunk in chunks)
    return pl.pallas_call(
        functools.partial(rows_kernel, len(chunks)),
        grid=(2 * tiles,),
        out_shape=[jax.ShapeDtypeStruct((slots, 2 * width), BF)] * 2,
        in_specs=in_specs,
        out_specs=[pl.BlockSpec((slots, tile), lambda n: (0, n))] * 2,
        compiler_params=pltpu.CompilerParams(vmem_limit_bytes=VMEM_BYTES // 2),
        cost_estimate=pl.CostEstimate(
            flops=12 * slots * width * units, bytes_accessed=12 * 2**20, transcendentals=0
        ),
    )(*(array for chunk in chunks for array in chunk))


def local(tokens, expert_ids, gate_probs, w_gate, w_up, w_down, d_out):
    g = Grid()
    rows, topk = expert_ids.shape
    width = tokens.shape[1]
    hidden_width = w_gate.shape[2]
    half = hidden_width // 2
    experts = g.experts
    cap = rows * topk * 9 // (8 * experts)
    slots = experts * cap
    first = g.c == 0
    even = g.x == 0

    block = hidden_width // g.dps
    part = block // 2
    pieces = (2 * part // 3, part // 3)
    in_kernels = g.zs == 4 and slots % 16 == 0 and part % 48 == 0 and all(2 * p * g.dps % LANES == 0 for p in pieces)
    if not in_kernels:
        pieces = (part,)
    shuffle = shuffle_matrix(g.x, g.dps, hidden_width, pieces)

    def out_a(z, x, q, c):
        return z, c, q, x

    def out_b(z, x, q, c):
        return z, c, q, 1 - x

    def back_a(z, x, q, c):
        return z, c, q, x

    def back_b(z, x, q, c):
        return z, 1 - c, q, x

    def spread_halves(part_a, part_b):
        got_a, got_b = g.send(part_a, out_a), g.send(part_b, out_b)
        return jnp.where(first, got_a, got_b), jnp.where(first, got_b, got_a)

    def spread(part_a, part_b):
        return jnp.concatenate(spread_halves(part_a, part_b), axis=0)

    def unspread(both):
        n = both.shape[0] // 2
        low, high = both[:n], both[n:]
        return g.send(jnp.where(first, low, high), back_a), g.send(jnp.where(first, high, low), back_b)

    expert_iota = jnp.arange(experts, dtype=jnp.int32)
    chosen = expert_ids[:, :, None] == expert_iota
    named = jnp.any(chosen, axis=1).astype(BF)
    token_iota = jnp.arange(rows, dtype=jnp.int32)
    earlier = (token_iota[:, None] > token_iota[None, :]).astype(BF)
    before = dot(earlier, named)
    slot = jnp.sum(jnp.where(chosen, before[:, None, :], 0.0), axis=2).astype(jnp.int32)
    relative = ((expert_ids // 2 - g.q + g.qs) % g.qs) * 2 + ((expert_ids % 2) ^ g.x)
    dest = relative * cap + slot
    slot_iota = jnp.arange(slots, dtype=jnp.int32)
    pair = dest[:, :, None] == slot_iota
    placing = jnp.any(pair, axis=1).astype(BF)
    weighted = jnp.sum(jnp.where(pair, gate_probs[:, :, None], 0.0), axis=1)
    slot_probs = jnp.sum(weighted, axis=0)

    def member(r, sign):
        def move(z, x, q, c):
            return z, x ^ (r % 2), (q + sign * (r // 2)) % g.qs, c

        return move

    def other_core(z, x, q, c):
        return z, x, q, 1 - c

    def exchange(value, sign):
        got = [value[:cap]] + [g.send(value[r * cap:(r + 1) * cap], member(r, sign)) for r in range(1, experts)]
        return jnp.concatenate(got, axis=0)

    line_width = width // g.zs
    turned = lax.dynamic_slice(jnp.concatenate([tokens, tokens], axis=1), (0, g.z * line_width), (rows, width))
    sent = jnp.concatenate(
        [
            dot(placing, turned, ((0,), (0,))).astype(BF),
            (slot_probs[:, None] * dot(placing, d_out, ((0,), (0,)))).astype(BF),
        ],
        axis=1,
    )
    shapes = w_gate.shape[1:], w_down.shape[1:]
    together = lax.optimization_barrier
    if in_kernels:
        place_x, place_z = g.x.reshape(1).astype(jnp.int32), g.z.reshape(1).astype(jnp.int32)
        units = [piece * g.dps for piece in pieces]
        a, b = pack(pieces, place_x, w_gate[0], w_up[0], w_down[0], shuffle)
        ups, downs = {0: 1, 1: 2, 2: 3}, {1: 0, 2: 1, 3: 2}
        split = a.shape[0] * pieces[0] // part

        def forward(up, down):
            far = g.hop(jnp.where(g.z == 1, up, down), {1: 3, 2: 0})
            return far, g.hop(up, {1: 2, 2: 3}), g.hop(down, {1: 0, 2: 1})

        def inner_sums(terms, far, from_low, from_high):
            outer, inner, _, own = terms
            is_low, is_end = g.z == 1, (g.z == 0) | (g.z == 3)
            to_end = added(outer, jnp.where(is_low, from_high, from_low), far)
            to_mid = added(inner, jnp.where(is_low, from_low, from_high))
            return own, jnp.where(is_end, inner, to_end), to_mid

        def cross(to_end, to_mid):
            return g.hop(to_end, {0: 1, 1: 0, 2: 3, 3: 2}), g.hop(to_mid, {1: 2, 2: 1})

        outward, inward_up, inward_down = {0: 2, 3: 1}, {0: 1, 1: 2}, {3: 2, 2: 1}

        a, b = spread_halves(a, b)
        shard = jnp.concatenate([a[:split], b[:split], a[split:], b[split:]], axis=0)
        shard, sent = together((shard, sent))
        up, down = g.hop(shard, ups), g.hop(shard, downs)
        up, down, mine = together((up, down, exchange(sent, 1)))
        offset = 2 * split
        passed = forward(up[:offset], down[:offset])
        theirs = g.send(mine, other_core)
        up2, down2 = tie(up[offset:], *passed), tie(down[offset:], *passed)
        passed2 = forward(up2, down2)
        chunk, terms = expert(place_z, g.zs, units[0], 0, (shard, up, down, *passed), mine, theirs)
        far, from_low = g.hop(terms[0], outward), g.hop(terms[2], inward_up)
        passed2 = tie_all(passed2, terms[0], terms[2])
        from_high = g.hop(tie(terms[2], *passed2), inward_down)
        chunk2, terms2 = expert(place_z, g.zs, units[1], offset, (shard, up, down, *passed2), mine, theirs)
        far2, from_low2 = g.hop(terms2[0], outward), g.hop(terms2[2], inward_up)
        far, from_low, from_high, far2, from_low2 = together((far, from_low, from_high, far2, from_low2))
        own, to_end, to_mid = inner_sums(terms, far, from_low, from_high)
        middle2, to_end, to_mid = together((terms2[2], to_end, to_mid))
        end, mid = cross(to_end, to_mid)
        from_high2 = g.hop(middle2, inward_down)
        keep, give = token_rows([tie_all(parts, to_end, to_mid) for parts in (chunk, chunk2)], slots, width)
        sums = added(keep, g.send(give, other_core)).reshape(g.qs, 2, cap, 2 * width)
        sums = tie(sums, from_high2)
        own2, to_end2, to_mid2 = inner_sums(terms2, far2, from_low2, from_high2)
        end2, mid2 = cross(to_end2, to_mid2)

        def along_x(rows):
            return jnp.stack([rows[:, 0], g.send(rows[:, 1], lambda z, x, q, c: (z, 1 - x, q, c))], axis=1)

        def along_q(rows):
            return jnp.stack(
                [rows[0]] + [g.send(rows[d], lambda z, x, q, c, d=d: (z, x, (q - d) % g.qs, c)) for d in range(1, g.qs)]
            )

        returned, back_rows = together((along_x(sums[..., :width]), along_q(sums[..., width:])))
        grads = unspread(tie(added(own, end, mid), returned, back_rows))
        returned, back_rows = along_q(returned), along_x(back_rows)
        end2, mid2, grads = together((end2, mid2, grads))
        grad2 = added(own2, end2, mid2)
        returned, back_rows = tie(returned, grad2), tie(back_rows, grad2)
        returned, back_rows = returned.reshape(slots, width), back_rows.reshape(slots, width)
        grads += unspread(grad2)
        d_w_gate, d_w_up, d_w_down = unpack(pieces, place_x, grads, shuffle, *shapes)
    else:
        gate_cols, up_cols = dot(w_gate[0], shuffle).astype(BF), dot(w_up[0], shuffle).astype(BF)
        gate_up_shard = spread(
            jnp.concatenate([gate_cols[:, :half], up_cols[:, :half]], axis=1),
            jnp.concatenate([gate_cols[:, half:], up_cols[:, half:]], axis=1),
        )
        down_low, down_high = w_down[0, :part], w_down[0, part:]
        down_shard = spread(jnp.where(even, down_low, down_high), jnp.where(even, down_high, down_low))
        gate_up = jnp.concatenate(g.line(gate_up_shard), axis=0)
        down = jnp.concatenate(g.straight(g.line(down_shard)), axis=0)
        mine = exchange(sent, 1)
        inputs = jnp.concatenate([mine, g.send(mine, other_core)], axis=0)
        arrived, d_produced = inputs[:, :width], inputs[:, width:]
        pre = dot(arrived, gate_up)
        gate_pre, up_pre = pre[:, :half], pre[:, half:]
        sig = jax.nn.sigmoid(gate_pre)
        act = gate_pre * sig
        hidden = (act * up_pre).astype(BF)
        d_hidden = dot(d_produced, down, ((1,), (1,)))
        d_gate = (d_hidden * up_pre * sig * (1.0 + gate_pre * (1.0 - sig))).astype(BF)
        d_up = (d_hidden * act).astype(BF)
        d_both = jnp.concatenate([d_gate, d_up], axis=1)
        down_part = dot(hidden, d_produced, ((0,), (0,))).astype(BF)
        both_part = dot(arrived, d_both, ((0,), (0,))).astype(BF)
        partial = jnp.concatenate([dot(hidden, down), dot(d_both, gate_up, ((1,), (1,)))], axis=1).astype(BF)
        got = exchange(added(partial[:slots], g.send(partial[slots:], other_core)), -1)
        down_a, down_b = unspread(
            g.line_sum(
                lambda k: lax.dynamic_slice_in_dim(down_part, ((g.z + k) % g.zs) * (2 * part), 2 * part)
            )
        )
        d_w_down = jnp.where(
            even, jnp.concatenate([down_a, down_b], axis=0), jnp.concatenate([down_b, down_a], axis=0)
        ).astype(F32)
        both_a, both_b = unspread(g.line_sum(lambda k: both_part[k * line_width:(k + 1) * line_width]))
        d_w_gate, d_w_up = (
            dot(jnp.concatenate([both_a[:, cols], both_b[:, cols]], axis=1), shuffle, ((1,), (1,)))
            for cols in (slice(0, half), slice(half, None))
        )
        returned, back_rows = got[:, :width], got[:, width:]

    high = lax.reduce_precision(weighted, 8, 7)
    mixed = (dot(high.astype(BF), returned) + dot((weighted - high).astype(BF), returned)).astype(BF)
    products = dot(d_out, returned, ((1,), (1,)))
    d_probs = jnp.sum(jnp.where(pair, products[:, None, :], 0.0), axis=2)
    d_turned = dot(placing, back_rows).astype(BF)
    d_tokens = lax.dynamic_slice(
        jnp.concatenate([d_turned, d_turned], axis=1), (0, (g.zs - g.z) * line_width), (rows, width)
    )

    return (mixed, d_tokens, d_probs, d_w_gate[None], d_w_up[None], d_w_down[None])


def solution(mesh):
    rows = P(("dp", "expert"), None)
    weight = P("expert", "dp", None)
    return jax.shard_map(
        local,
        mesh=mesh,
        in_specs=(rows, rows, rows, weight, weight, weight, rows),
        out_specs=(rows, rows, rows, weight, weight, weight),
        check_vma=False,
    )
```

```python
import functools

import jax
import jax.numpy as jnp
from jax import lax
from jax.experimental import pallas as pl
from jax.experimental.pallas import tpu as pltpu
from jax.sharding import PartitionSpec as P

BF = jnp.bfloat16
F32 = jnp.float32
BOTH = ("dp", "expert")


def dot(a, b, dims=((1,), (0,))):
    return lax.dot_general(a, b, (dims, ((), ())), preferred_element_type=F32)


def tie(value, *others):
    return lax.optimization_barrier((value,) + others)[0]


def added(*terms):
    return sum(t.astype(F32) for t in terms).astype(BF)


class Grid:
    def __init__(self):
        self.dps, self.experts = lax.axis_size("dp"), lax.axis_size("expert")
        self.zs, self.qs = self.dps // 2, self.experts // 2
        dp, ex = lax.axis_index("dp"), lax.axis_index("expert")
        self.z, self.x, self.q, self.c = dp // 2, dp % 2, ex // 2, ex % 2

    def send(self, value, move):
        pairs = []
        for z in range(self.zs):
            for x in range(2):
                for q in range(self.qs):
                    for c in range(2):
                        to = move(z, x, q, c)
                        if to is not None:
                            pairs.append((self.flat(z, x, q, c), self.flat(*to)))
        return lax.ppermute(value, BOTH, pairs)

    def flat(self, z, x, q, c):
        return (z * 2 + x) * self.experts + q * 2 + c

    def hop(self, value, where):
        return self.send(value, lambda z, x, q, c: (where[z], x, q, c) if z in where else None)

    def line(self, shard):
        n = self.zs
        ups, downs = [shard], [shard]
        for s in range(1, n):
            ups.append(self.hop(ups[-1], {i: i + 1 for i in range(s - 1, n - 1)}))
            downs.append(self.hop(downs[-1], {i: i - 1 for i in range(1, n - s + 1)}))
        return [shard] + [jnp.where(self.z + s < n, downs[s], ups[n - s]) for s in range(1, n)]

    def straight(self, blocks):
        n = self.zs
        rows = []
        for j in range(n):
            row = blocks[j]
            for z in range(1, n):
                row = jnp.where(self.z == z, blocks[(j - z) % n], row)
            rows.append(row)
        return rows

    def line_sum(self, block):
        n = self.zs
        up, down = self.hop(block(n - 1), {0: 1}), self.hop(block(1), {n - 1: n - 2})
        for r in range(2, n):
            up = self.hop(added(block(n - r), up), {i: i + 1 for i in range(r)})
            down = self.hop(added(block(r), down), {i: i - 1 for i in range(n - r, n)})
        return added(block(0), up, down)


LANES = 256
VMEM_BYTES = 48 * 2**20


def shuffle_matrix(x, dps, hidden_width, pieces):
    block, half = hidden_width // dps, hidden_width // 2
    sources, start = [], 0
    for piece in pieces:
        unit = jnp.arange(piece * dps, dtype=jnp.int32)
        sources.append((unit // piece) * block + start + unit % piece)
        start += piece
    low = jnp.concatenate(sources)
    source = jnp.concatenate([low + x * (block // 2), low + (1 - x) * (block // 2)])
    return (jnp.arange(hidden_width, dtype=jnp.int32)[:, None] == source[None, :]).astype(BF)


def pack_kernel(pieces, x_ref, gate_ref, up_ref, down_ref, shuffle_ref, *outs):
    rows, hidden_width = gate_ref.shape
    half, block = hidden_width // 2, down_ref.shape[0]
    shuffle = shuffle_ref[...]
    gate, up = dot(gate_ref[...], shuffle).astype(BF), dot(up_ref[...], shuffle).astype(BF)
    x = x_ref[0]
    done = 0
    for number, piece in enumerate(pieces):
        units = piece * half // sum(pieces)
        count = 2 * units // LANES
        for side, start in ((0, x), (1, 1 - x)):
            ref = outs[2 * number + side]
            at = side * half + done * units // piece
            both = jnp.concatenate([gate[:, at:at + units], up[:, at:at + units]], axis=1)
            for i in range(count):
                ref[i * rows:(i + 1) * rows, :] = both[:, i * LANES:(i + 1) * LANES]
            source = pl.ds(pl.multiple_of(start * (block // 2) + done, 16), piece)
            for j in range(down_ref.shape[1] // LANES):
                to = count * rows + j * piece
                ref[to:to + piece, :] = down_ref[source, j * LANES:(j + 1) * LANES]
        done += piece


def unpack_kernel(pieces, x_ref, *refs):
    packed, (shuffle_ref, gate_ref, up_ref, down_ref) = refs[:-4], refs[-4:]
    rows, hidden_width = gate_ref.shape
    half, block = hidden_width // 2, down_ref.shape[0]
    x = x_ref[0]
    gates, ups = [[], []], [[], []]
    done = 0
    for number, piece in enumerate(pieces):
        units = piece * half // sum(pieces)
        count = 2 * units // LANES
        for side, start in ((0, x), (1, 1 - x)):
            ref = packed[2 * number + side]
            both = jnp.concatenate([ref[i * rows:(i + 1) * rows, :] for i in range(count)], axis=1)
            gates[side].append(both[:, :units])
            ups[side].append(both[:, units:])
            to = pl.ds(pl.multiple_of(start * (block // 2) + done, 16), piece)
            for j in range(down_ref.shape[1] // LANES):
                at = count * rows + j * piece
                down_ref[to, j * LANES:(j + 1) * LANES] = ref[at:at + piece, :].astype(F32)
        done += piece
    shuffle = shuffle_ref[...]
    gate_ref[...] = dot(jnp.concatenate(gates[0] + gates[1], axis=1), shuffle, ((1,), (1,)))
    up_ref[...] = dot(jnp.concatenate(ups[0] + ups[1], axis=1), shuffle, ((1,), (1,)))


def expert_kernel(z_ref, own, up, down, up_2, down_2, last, mine, theirs, *refs):
    weight_outs, (hidden_out, d_both_out, outer_out), outs, refs = refs[:2], refs[2:5], refs[5:9], refs[9:]
    packed, x, grads, gate_up, w_down, pre, d_hidden, hidden, d_both, d_down, terms, load, store = refs
    places, size, _ = packed.shape
    rows, width = x.shape
    slots = rows // 2
    line = width // places
    part_rows = line // 2
    units = w_down.shape[0]
    piece = units // places // 2
    count, columns = 2 * units // LANES, width // LANES
    size_half = size // 2
    z = z_ref[0]

    loads = [
        pltpu.make_async_copy(a, b, load.at[places + n])
        for n, (a, b) in enumerate(
            (
                (mine.at[:, :width], x.at[:slots]),
                (theirs.at[:, :width], x.at[slots:]),
                (mine.at[:, width:], grads.at[:slots]),
                (theirs.at[:, width:], grads.at[slots:]),
            )
        )
    ]
    for copy in loads[:2]:
        copy.start()
    pltpu.make_async_copy(own, packed.at[0], load.at[0]).start()
    for s, is_one, one, other in (
        (1, z == places - 1, last, down),
        (2, z < 2, down_2, up_2),
        (3, z == 0, last, up),
    ):
        @pl.when(is_one)
        def _():
            pltpu.make_async_copy(one, packed.at[s], load.at[s]).start()

        @pl.when(jnp.logical_not(is_one))
        def _():
            pltpu.make_async_copy(other, packed.at[s], load.at[s]).start()

    for copy in loads[2:]:
        copy.start()

    def down_rows(k, h):
        return pl.ds(pl.multiple_of(lax.rem(z + k, places) * (2 * piece) + h * piece, 16), piece)

    for copy in loads[:2]:
        copy.wait()
    for s in range(places):
        pltpu.make_async_copy(own, packed.at[s], load.at[s]).wait()
        for h in range(2):
            for i in range(count):
                at = h * size_half + i * part_rows
                to = s * line + h * part_rows
                gate_up[to:to + part_rows, i * LANES:(i + 1) * LANES] = packed[s, at:at + part_rows, :]
            for j in range(columns):
                at = h * size_half + count * part_rows + j * piece
                w_down[down_rows(s, h), j * LANES:(j + 1) * LANES] = packed[s, at:at + piece, :]
        block = slice(s * line, (s + 1) * line)
        for i in range(count):
            cols = slice(i * LANES, (i + 1) * LANES)
            product = dot(x[:, block], gate_up[block, cols])
            pre[:, cols] = product if s == 0 else pre[:, cols] + product

    stores = []

    def store_to(out, value):
        stores.append(pltpu.make_async_copy(value, out, store.at[len(stores)]))
        stores[-1].start()

    store_to(weight_outs[0], gate_up)
    store_to(weight_outs[1], w_down)
    step = 64 if rows % 64 == 0 else 16

    def activate(r, _):
        at = pl.ds(pl.multiple_of(r * step, 16), step)
        gate_pre, up_pre = pre[at, :units], pre[at, units:]
        sig = 1.0 / (1.0 + jnp.exp(-gate_pre))
        act = gate_pre * sig
        hidden[at, :] = (act * up_pre).astype(BF)
        pre[at, :units] = up_pre * sig * (1.0 + gate_pre * (1.0 - sig))
        pre[at, units:] = act
        return 0

    lax.fori_loop(0, rows // step, activate, 0)
    store_to(hidden_out, hidden)
    for copy in loads[2:]:
        copy.wait()
    d_hidden[...] = dot(grads[...], w_down[...], ((1,), (1,)))

    def differentiate(r, _):
        at = pl.ds(pl.multiple_of(r * step, 16), step)
        d_h = d_hidden[at, :]
        d_both[at, :units] = (d_h * pre[at, :units]).astype(BF)
        d_both[at, units:] = (d_h * pre[at, units:]).astype(BF)
        return 0

    lax.fori_loop(0, rows // step, differentiate, 0)
    store_to(d_both_out, d_both)
    d_down[...] = dot(hidden[...], grads[...], ((0,), (0,))).astype(BF)

    for k in (places - 1, 1, 2, 0):
        for h in range(2):
            from_cols = slice(k * line + h * part_rows, k * line + (h + 1) * part_rows)
            weights = dot(x[:, from_cols], d_both[...], ((0,), (0,))).astype(BF)
            for i in range(count):
                to = h * size_half + i * part_rows
                terms[k, to:to + part_rows, :] = weights[:, i * LANES:(i + 1) * LANES]
            for j in range(columns):
                to = h * size_half + count * part_rows + j * piece
                terms[k, to:to + piece, :] = d_down[down_rows(k, h), j * LANES:(j + 1) * LANES]
        store_to(outs[k], terms.at[k])
        if k == 1:
            store_to(outer_out, terms.at[jnp.where(z == 0, places - 1, 1)])
    for copy in stores:
        copy.wait()


def rows_kernel(chunks, *refs):
    keep, give = refs[-2:]
    slots = keep.shape[0]

    def add(pairs, dims):
        total = sum(dot(a[...], b[...], dims) for a, b in pairs).astype(BF)
        keep[...], give[...] = total[:slots], total[slots:]

    chunked = [refs[4 * n:4 * n + 4] for n in range(chunks)]

    @pl.when(pl.program_id(0) < pl.num_programs(0) // 2)
    def _():
        add([(hidden, w_down) for _, w_down, hidden, _ in chunked], ((1,), (0,)))

    @pl.when(pl.program_id(0) >= pl.num_programs(0) // 2)
    def _():
        add([(d_both, gate_up) for gate_up, _, _, d_both in chunked], ((1,), (1,)))


def in_vmem(count):
    return [pl.BlockSpec(memory_space=pltpu.VMEM)] * count


IN_SMEM = pl.BlockSpec(memory_space=pltpu.SMEM)


def pack(pieces, x, gate, up, down, shuffle):
    rows, hidden_width = gate.shape
    sizes = [(rows * hidden_width + down.size // 2) * piece // sum(pieces) // LANES for piece in pieces]
    return pl.pallas_call(
        functools.partial(pack_kernel, pieces),
        out_shape=[jax.ShapeDtypeStruct((size, LANES), BF) for size in sizes for _ in range(2)],
        in_specs=[IN_SMEM] + in_vmem(4),
        out_specs=in_vmem(2 * len(pieces)),
        compiler_params=pltpu.CompilerParams(vmem_limit_bytes=VMEM_BYTES // 2),
    )(x, gate, up, down, shuffle)


def unpack(pieces, x, packed, shuffle, gate_shape, down_shape):
    return pl.pallas_call(
        functools.partial(unpack_kernel, pieces),
        out_shape=[jax.ShapeDtypeStruct(shape, F32) for shape in (gate_shape, gate_shape, down_shape)],
        in_specs=[IN_SMEM] + in_vmem(len(packed) + 1),
        out_specs=in_vmem(3),
        compiler_params=pltpu.CompilerParams(vmem_limit_bytes=VMEM_BYTES // 2),
    )(x, *packed, shuffle)


def expert(z, places, units, weights, mine, theirs):
    size = weights[0].shape[0]
    slots, width = mine.shape[0], mine.shape[1] // 2
    rows = 2 * slots
    for_rows = [
        jax.ShapeDtypeStruct(shape, BF) for shape in ((width, 2 * units), (units, width), (rows, units), (rows, 2 * units))
    ]
    outs = pl.pallas_call(
        expert_kernel,
        out_shape=for_rows + [jax.ShapeDtypeStruct((size, LANES), BF)] * 5,
        in_specs=[IN_SMEM] + [pl.BlockSpec(memory_space=pl.ANY)] * 8,
        out_specs=[pl.BlockSpec(memory_space=pl.ANY)] * 9,
        scratch_shapes=[
            pltpu.VMEM((places, size, LANES), BF),
            pltpu.VMEM((rows, width), BF),
            pltpu.VMEM((rows, width), BF),
            pltpu.VMEM((width, 2 * units), BF),
            pltpu.VMEM((units, width), BF),
            pltpu.VMEM((rows, 2 * units), F32),
            pltpu.VMEM((rows, units), F32),
            pltpu.VMEM((rows, units), BF),
            pltpu.VMEM((rows, 2 * units), BF),
            pltpu.VMEM((units, width), BF),
            pltpu.VMEM((places, size, LANES), BF),
            pltpu.SemaphoreType.DMA((places + 4,)),
            pltpu.SemaphoreType.DMA((9,)),
        ],
        compiler_params=pltpu.CompilerParams(vmem_limit_bytes=VMEM_BYTES),
        cost_estimate=pl.CostEstimate(
            flops=12 * rows * width * units, bytes_accessed=16 * 2**20, transcendentals=rows * units
        ),
    )(z, *weights, mine, theirs)
    return outs[:4], outs[4], outs[5:]


def token_rows(chunks, slots, width):
    tile = 2 * LANES
    tiles = width // tile
    in_specs = []
    for gate_up, w_down, hidden, d_both in chunks:
        in_specs += [
            pl.BlockSpec((tile, gate_up.shape[1]), lambda n: (jnp.maximum(n - tiles, 0), 0)),
            pl.BlockSpec((w_down.shape[0], tile), lambda n: (0, jnp.minimum(n, tiles - 1))),
            pl.BlockSpec(hidden.shape, lambda n: (0, 0)),
            pl.BlockSpec(d_both.shape, lambda n: (0, 0)),
        ]
    units = sum(chunk[1].shape[0] for chunk in chunks)
    return pl.pallas_call(
        functools.partial(rows_kernel, len(chunks)),
        grid=(2 * tiles,),
        out_shape=[jax.ShapeDtypeStruct((slots, 2 * width), BF)] * 2,
        in_specs=in_specs,
        out_specs=[pl.BlockSpec((slots, tile), lambda n: (0, n))] * 2,
        compiler_params=pltpu.CompilerParams(vmem_limit_bytes=VMEM_BYTES // 2),
        cost_estimate=pl.CostEstimate(
            flops=12 * slots * width * units, bytes_accessed=12 * 2**20, transcendentals=0
        ),
    )(*(array for chunk in chunks for array in chunk))


def local(tokens, expert_ids, gate_probs, w_gate, w_up, w_down, d_out):
    g = Grid()
    rows, topk = expert_ids.shape
    width = tokens.shape[1]
    hidden_width = w_gate.shape[2]
    half = hidden_width // 2
    experts = g.experts
    cap = rows * topk * 9 // (8 * experts)
    slots = experts * cap
    first = g.c == 0
    even = g.x == 0

    block = hidden_width // g.dps
    part = block // 2
    pieces = (2 * part // 3, part // 3)
    in_kernels = g.zs == 4 and slots % 16 == 0 and part % 48 == 0 and all(2 * p * g.dps % LANES == 0 for p in pieces)
    if not in_kernels:
        pieces = (part,)
    shuffle = shuffle_matrix(g.x, g.dps, hidden_width, pieces)

    def out_a(z, x, q, c):
        return z, c, q, x

    def out_b(z, x, q, c):
        return z, c, q, 1 - x

    def back_a(z, x, q, c):
        return z, c, q, x

    def back_b(z, x, q, c):
        return z, 1 - c, q, x

    def spread(part_a, part_b):
        got_a, got_b = g.send(part_a, out_a), g.send(part_b, out_b)
        return jnp.concatenate([jnp.where(first, got_a, got_b), jnp.where(first, got_b, got_a)], axis=0)

    def unspread(both):
        n = both.shape[0] // 2
        low, high = both[:n], both[n:]
        return g.send(jnp.where(first, low, high), back_a), g.send(jnp.where(first, high, low), back_b)

    expert_iota = jnp.arange(experts, dtype=jnp.int32)
    chosen = expert_ids[:, :, None] == expert_iota
    named = jnp.any(chosen, axis=1).astype(BF)
    token_iota = jnp.arange(rows, dtype=jnp.int32)
    earlier = (token_iota[:, None] > token_iota[None, :]).astype(BF)
    before = dot(earlier, named)
    slot = jnp.sum(jnp.where(chosen, before[:, None, :], 0.0), axis=2).astype(jnp.int32)
    relative = ((expert_ids // 2 - g.q + g.qs) % g.qs) * 2 + ((expert_ids % 2) ^ g.x)
    dest = relative * cap + slot
    slot_iota = jnp.arange(slots, dtype=jnp.int32)
    pair = dest[:, :, None] == slot_iota
    placing = jnp.any(pair, axis=1).astype(BF)
    weighted = jnp.sum(jnp.where(pair, gate_probs[:, :, None], 0.0), axis=1)
    slot_probs = jnp.sum(weighted, axis=0)

    def member(r, sign):
        def move(z, x, q, c):
            return z, x ^ (r % 2), (q + sign * (r // 2)) % g.qs, c

        return move

    def other_core(z, x, q, c):
        return z, x, q, 1 - c

    def exchange(value, sign):
        got = [value[:cap]] + [g.send(value[r * cap:(r + 1) * cap], member(r, sign)) for r in range(1, experts)]
        return jnp.concatenate(got, axis=0)

    line_width = width // g.zs
    turned = lax.dynamic_slice(jnp.concatenate([tokens, tokens], axis=1), (0, g.z * line_width), (rows, width))
    sent = jnp.concatenate(
        [
            dot(placing, turned, ((0,), (0,))).astype(BF),
            (slot_probs[:, None] * dot(placing, d_out, ((0,), (0,)))).astype(BF),
        ],
        axis=1,
    )
    shapes = w_gate.shape[1:], w_down.shape[1:]
    together = lax.optimization_barrier
    if in_kernels:
        place_x, place_z = g.x.reshape(1).astype(jnp.int32), g.z.reshape(1).astype(jnp.int32)
        units = [piece * g.dps for piece in pieces]
        a, b, a2, b2 = pack(pieces, place_x, w_gate[0], w_up[0], w_down[0], shuffle)
        ups, downs, passing = {0: 1, 1: 2, 2: 3}, {1: 0, 2: 1, 3: 2}, {2: 3, 1: 0}
        outward, inward_up, inward_down = {0: 1, 3: 2}, {0: 1, 1: 2}, {3: 2, 2: 1}
        to_last = g.z == 2

        shard, a2, b2 = together((spread(a, b), a2, b2))
        up, down = g.hop(shard, ups), g.hop(shard, downs)
        shard2, sent = together((spread(a2, b2), sent))
        up, down = together((up, down))
        up_2, down_2 = g.hop(up, {1: 2, 2: 3}), g.hop(down, {1: 0, 2: 1})
        shard2, mine = together((shard2, exchange(sent, 1)))
        up2, down2 = g.hop(shard2, ups), g.hop(shard2, downs)
        up_2, down_2, up2, down2, mine = together((up_2, down_2, up2, down2, mine))
        last = g.hop(jnp.where(to_last, up_2, down_2), passing)
        theirs = g.send(mine, other_core)
        up2, down2 = tie(up2, last), tie(down2, last)
        up2_2, down2_2 = g.hop(up2, {1: 2, 2: 3}), g.hop(down2, {1: 0, 2: 1})
        chunk, outer, terms = expert(
            place_z, g.zs, units[0], (shard, up, down, up_2, down_2, last), mine, theirs
        )
        up2_2, down2_2 = tie(up2_2, outer), tie(down2_2, outer)
        last2 = g.hop(jnp.where(to_last, up2_2, down2_2), passing)
        begun = g.hop(outer, outward)
        chunk2, outer2, terms2 = expert(
            place_z, g.zs, units[1], (shard2, up2, down2, up2_2, down2_2, last2), mine, theirs
        )
        begun, outer2, chunk2 = together((begun, outer2, chunk2))
        middle, outer2, chunk2 = together((added(terms[2], begun), outer2, chunk2))
        sum_up, sum_down = g.hop(middle, inward_up), g.hop(middle, inward_down)
        begun2 = g.hop(outer2, outward)
        keep, give = token_rows((chunk, chunk2), slots, width)
        sums = added(keep, g.send(give, other_core)).reshape(g.qs, 2, cap, 2 * width)
        sum_up, sum_down, sums = together((sum_up, sum_down, sums))

        def along_x(rows):
            return jnp.stack([rows[:, 0], g.send(rows[:, 1], lambda z, x, q, c: (z, 1 - x, q, c))], axis=1)

        def along_q(rows):
            return jnp.stack(
                [rows[0]] + [g.send(rows[d], lambda z, x, q, c, d=d: (z, x, (q - d) % g.qs, c)) for d in range(1, g.qs)]
            )

        returned, back_rows = along_x(sums[..., :width]), along_q(sums[..., width:])
        sum_up, sum_down = g.hop(added(terms[1], sum_up), ups), g.hop(added(terms[3], sum_down), downs)
        middle2 = added(terms2[2], begun2)
        sum_up2, sum_down2 = g.hop(middle2, inward_up), g.hop(middle2, inward_down)
        returned, back_rows, sum_up, sum_down = together((returned, back_rows, sum_up, sum_down))
        returned, back_rows = along_q(returned), along_x(back_rows)
        grad = added(terms[0], sum_up, sum_down)
        grads = unspread(grad)
        sum_up2, sum_down2 = g.hop(added(terms2[1], sum_up2), ups), g.hop(added(terms2[3], sum_down2), downs)
        sum_up2, sum_down2, grads = together((sum_up2, sum_down2, grads))
        grad2 = added(terms2[0], sum_up2, sum_down2)
        returned, back_rows = tie(returned, grad2), tie(back_rows, grad2)
        returned, back_rows = returned.reshape(slots, width), back_rows.reshape(slots, width)
        grads += unspread(grad2)
        d_w_gate, d_w_up, d_w_down = unpack(pieces, place_x, grads, shuffle, *shapes)
    else:
        gate_cols, up_cols = dot(w_gate[0], shuffle).astype(BF), dot(w_up[0], shuffle).astype(BF)
        gate_up_shard = spread(
            jnp.concatenate([gate_cols[:, :half], up_cols[:, :half]], axis=1),
            jnp.concatenate([gate_cols[:, half:], up_cols[:, half:]], axis=1),
        )
        down_low, down_high = w_down[0, :part], w_down[0, part:]
        down_shard = spread(jnp.where(even, down_low, down_high), jnp.where(even, down_high, down_low))
        gate_up = jnp.concatenate(g.line(gate_up_shard), axis=0)
        down = jnp.concatenate(g.straight(g.line(down_shard)), axis=0)
        mine = exchange(sent, 1)
        inputs = jnp.concatenate([mine, g.send(mine, other_core)], axis=0)
        arrived, d_produced = inputs[:, :width], inputs[:, width:]
        pre = dot(arrived, gate_up)
        gate_pre, up_pre = pre[:, :half], pre[:, half:]
        sig = jax.nn.sigmoid(gate_pre)
        act = gate_pre * sig
        hidden = (act * up_pre).astype(BF)
        d_hidden = dot(d_produced, down, ((1,), (1,)))
        d_gate = (d_hidden * up_pre * sig * (1.0 + gate_pre * (1.0 - sig))).astype(BF)
        d_up = (d_hidden * act).astype(BF)
        d_both = jnp.concatenate([d_gate, d_up], axis=1)
        down_part = dot(hidden, d_produced, ((0,), (0,))).astype(BF)
        both_part = dot(arrived, d_both, ((0,), (0,))).astype(BF)
        partial = jnp.concatenate([dot(hidden, down), dot(d_both, gate_up, ((1,), (1,)))], axis=1).astype(BF)
        got = exchange(added(partial[:slots], g.send(partial[slots:], other_core)), -1)
        down_a, down_b = unspread(
            g.line_sum(
                lambda k: lax.dynamic_slice_in_dim(down_part, ((g.z + k) % g.zs) * (2 * part), 2 * part)
            )
        )
        d_w_down = jnp.where(
            even, jnp.concatenate([down_a, down_b], axis=0), jnp.concatenate([down_b, down_a], axis=0)
        ).astype(F32)
        both_a, both_b = unspread(g.line_sum(lambda k: both_part[k * line_width:(k + 1) * line_width]))
        d_w_gate, d_w_up = (
            dot(jnp.concatenate([both_a[:, cols], both_b[:, cols]], axis=1), shuffle, ((1,), (1,)))
            for cols in (slice(0, half), slice(half, None))
        )
        returned, back_rows = got[:, :width], got[:, width:]

    high = lax.reduce_precision(weighted, 8, 7)
    mixed = (dot(high.astype(BF), returned) + dot((weighted - high).astype(BF), returned)).astype(BF)
    products = dot(d_out, returned, ((1,), (1,)))
    d_probs = jnp.sum(jnp.where(pair, products[:, None, :], 0.0), axis=2)
    d_turned = dot(placing, back_rows).astype(BF)
    d_tokens = lax.dynamic_slice(
        jnp.concatenate([d_turned, d_turned], axis=1), (0, (g.zs - g.z) * line_width), (rows, width)
    )

    return (mixed, d_tokens, d_probs, d_w_gate[None], d_w_up[None], d_w_down[None])


def solution(mesh):
    rows = P(("dp", "expert"), None)
    weight = P("expert", "dp", None)
    return jax.shard_map(
        local,
        mesh=mesh,
        in_specs=(rows, rows, rows, weight, weight, weight, rows),
        out_specs=(rows, rows, rows, weight, weight, weight),
        check_vma=False,
    )
```

```python
import functools

import jax
import jax.numpy as jnp
from jax import lax
from jax.experimental import pallas as pl
from jax.experimental.pallas import tpu as pltpu
from jax.sharding import PartitionSpec as P

BF = jnp.bfloat16
F32 = jnp.float32
BOTH = ("dp", "expert")


def dot(a, b, dims=((1,), (0,))):
    return lax.dot_general(a, b, (dims, ((), ())), preferred_element_type=F32)


def tie(value, *others):
    return lax.optimization_barrier((value,) + others)[0]


def added(*terms):
    return sum(t.astype(F32) for t in terms).astype(BF)


class Grid:
    def __init__(self):
        self.dps, self.experts = lax.axis_size("dp"), lax.axis_size("expert")
        self.zs, self.qs = self.dps // 2, self.experts // 2
        dp, ex = lax.axis_index("dp"), lax.axis_index("expert")
        self.z, self.x, self.q, self.c = dp // 2, dp % 2, ex // 2, ex % 2

    def send(self, value, move):
        pairs = []
        for z in range(self.zs):
            for x in range(2):
                for q in range(self.qs):
                    for c in range(2):
                        to = move(z, x, q, c)
                        if to is not None:
                            pairs.append((self.flat(z, x, q, c), self.flat(*to)))
        return lax.ppermute(value, BOTH, pairs)

    def flat(self, z, x, q, c):
        return (z * 2 + x) * self.experts + q * 2 + c

    def hop(self, value, where):
        return self.send(value, lambda z, x, q, c: (where[z], x, q, c) if z in where else None)

    def line(self, shard):
        n = self.zs
        ups, downs = [shard], [shard]
        for s in range(1, n):
            ups.append(self.hop(ups[-1], {i: i + 1 for i in range(s - 1, n - 1)}))
            downs.append(self.hop(downs[-1], {i: i - 1 for i in range(1, n - s + 1)}))
        return [shard] + [jnp.where(self.z + s < n, downs[s], ups[n - s]) for s in range(1, n)]

    def straight(self, blocks):
        n = self.zs
        rows = []
        for j in range(n):
            row = blocks[j]
            for z in range(1, n):
                row = jnp.where(self.z == z, blocks[(j - z) % n], row)
            rows.append(row)
        return rows

    def line_sum(self, block):
        n = self.zs
        up, down = self.hop(block(n - 1), {0: 1}), self.hop(block(1), {n - 1: n - 2})
        for r in range(2, n):
            up = self.hop(added(block(n - r), up), {i: i + 1 for i in range(r)})
            down = self.hop(added(block(r), down), {i: i - 1 for i in range(n - r, n)})
        return added(block(0), up, down)


LANES = 256
VMEM_BYTES = 48 * 2**20


def shuffle_matrix(x, dps, hidden_width, pieces):
    block, half = hidden_width // dps, hidden_width // 2
    sources, start = [], 0
    for piece in pieces:
        unit = jnp.arange(piece * dps, dtype=jnp.int32)
        sources.append((unit // piece) * block + start + unit % piece)
        start += piece
    low = jnp.concatenate(sources)
    source = jnp.concatenate([low + x * (block // 2), low + (1 - x) * (block // 2)])
    return (jnp.arange(hidden_width, dtype=jnp.int32)[:, None] == source[None, :]).astype(BF)


def pack_kernel(pieces, x_ref, gate_ref, up_ref, down_ref, shuffle_ref, *outs):
    rows, hidden_width = gate_ref.shape
    half, block = hidden_width // 2, down_ref.shape[0]
    shuffle = shuffle_ref[...]
    gate, up = dot(gate_ref[...], shuffle).astype(BF), dot(up_ref[...], shuffle).astype(BF)
    x = x_ref[0]
    done = 0
    for number, piece in enumerate(pieces):
        units = piece * half // sum(pieces)
        count = 2 * units // LANES
        for side, start in ((0, x), (1, 1 - x)):
            ref = outs[2 * number + side]
            at = side * half + done * units // piece
            both = jnp.concatenate([gate[:, at:at + units], up[:, at:at + units]], axis=1)
            for i in range(count):
                ref[i * rows:(i + 1) * rows, :] = both[:, i * LANES:(i + 1) * LANES]
            source = pl.ds(pl.multiple_of(start * (block // 2) + done, 16), piece)
            for j in range(down_ref.shape[1] // LANES):
                to = count * rows + j * piece
                ref[to:to + piece, :] = down_ref[source, j * LANES:(j + 1) * LANES]
        done += piece


def unpack_kernel(pieces, x_ref, *refs):
    packed, (shuffle_ref, gate_ref, up_ref, down_ref) = refs[:-4], refs[-4:]
    rows, hidden_width = gate_ref.shape
    half, block = hidden_width // 2, down_ref.shape[0]
    x = x_ref[0]
    gates, ups = [[], []], [[], []]
    done = 0
    for number, piece in enumerate(pieces):
        units = piece * half // sum(pieces)
        count = 2 * units // LANES
        for side, start in ((0, x), (1, 1 - x)):
            ref = packed[2 * number + side]
            both = jnp.concatenate([ref[i * rows:(i + 1) * rows, :] for i in range(count)], axis=1)
            gates[side].append(both[:, :units])
            ups[side].append(both[:, units:])
            to = pl.ds(pl.multiple_of(start * (block // 2) + done, 16), piece)
            for j in range(down_ref.shape[1] // LANES):
                at = count * rows + j * piece
                down_ref[to, j * LANES:(j + 1) * LANES] = ref[at:at + piece, :].astype(F32)
        done += piece
    shuffle = shuffle_ref[...]
    gate_ref[...] = dot(jnp.concatenate(gates[0] + gates[1], axis=1), shuffle, ((1,), (1,)))
    up_ref[...] = dot(jnp.concatenate(ups[0] + ups[1], axis=1), shuffle, ((1,), (1,)))


def expert_kernel(z_ref, own, up, down, up_2, down_2, last, mine, theirs, *refs):
    weight_outs, (hidden_out, d_both_out, outer_out), outs, refs = refs[:2], refs[2:5], refs[5:9], refs[9:]
    packed, x, grads, gate_up, w_down, pre, d_hidden, hidden, d_both, d_down, terms, load, store = refs
    places, size, _ = packed.shape
    rows, width = x.shape
    slots = rows // 2
    line = width // places
    part_rows = line // 2
    units = w_down.shape[0]
    piece = units // places // 2
    count, columns = 2 * units // LANES, width // LANES
    size_half = size // 2
    z = z_ref[0]

    loads = [
        pltpu.make_async_copy(a, b, load.at[places + n])
        for n, (a, b) in enumerate(
            (
                (mine.at[:, :width], x.at[:slots]),
                (theirs.at[:, :width], x.at[slots:]),
                (mine.at[:, width:], grads.at[:slots]),
                (theirs.at[:, width:], grads.at[slots:]),
            )
        )
    ]
    for copy in loads[:2]:
        copy.start()
    pltpu.make_async_copy(own, packed.at[0], load.at[0]).start()
    for s, is_one, one, other in (
        (1, z == places - 1, last, down),
        (2, z < 2, down_2, up_2),
        (3, z == 0, last, up),
    ):
        @pl.when(is_one)
        def _():
            pltpu.make_async_copy(one, packed.at[s], load.at[s]).start()

        @pl.when(jnp.logical_not(is_one))
        def _():
            pltpu.make_async_copy(other, packed.at[s], load.at[s]).start()

    for copy in loads[2:]:
        copy.start()

    def down_rows(k, h):
        return pl.ds(pl.multiple_of(lax.rem(z + k, places) * (2 * piece) + h * piece, 16), piece)

    for copy in loads[:2]:
        copy.wait()
    for s in range(places):
        pltpu.make_async_copy(own, packed.at[s], load.at[s]).wait()
        for h in range(2):
            for i in range(count):
                at = h * size_half + i * part_rows
                to = s * line + h * part_rows
                gate_up[to:to + part_rows, i * LANES:(i + 1) * LANES] = packed[s, at:at + part_rows, :]
            for j in range(columns):
                at = h * size_half + count * part_rows + j * piece
                w_down[down_rows(s, h), j * LANES:(j + 1) * LANES] = packed[s, at:at + piece, :]
        block = slice(s * line, (s + 1) * line)
        for i in range(count):
            cols = slice(i * LANES, (i + 1) * LANES)
            product = dot(x[:, block], gate_up[block, cols])
            pre[:, cols] = product if s == 0 else pre[:, cols] + product

    stores = []

    def store_to(out, value):
        stores.append(pltpu.make_async_copy(value, out, store.at[len(stores)]))
        stores[-1].start()

    store_to(weight_outs[0], gate_up)
    store_to(weight_outs[1], w_down)
    step = 64 if rows % 64 == 0 else 16

    def activate(r, _):
        at = pl.ds(pl.multiple_of(r * step, 16), step)
        gate_pre, up_pre = pre[at, :units], pre[at, units:]
        sig = 1.0 / (1.0 + jnp.exp(-gate_pre))
        act = gate_pre * sig
        hidden[at, :] = (act * up_pre).astype(BF)
        pre[at, :units] = up_pre * sig * (1.0 + gate_pre * (1.0 - sig))
        pre[at, units:] = act
        return 0

    lax.fori_loop(0, rows // step, activate, 0)
    store_to(hidden_out, hidden)
    for copy in loads[2:]:
        copy.wait()
    d_hidden[...] = dot(grads[...], w_down[...], ((1,), (1,)))

    def differentiate(r, _):
        at = pl.ds(pl.multiple_of(r * step, 16), step)
        d_h = d_hidden[at, :]
        d_both[at, :units] = (d_h * pre[at, :units]).astype(BF)
        d_both[at, units:] = (d_h * pre[at, units:]).astype(BF)
        return 0

    lax.fori_loop(0, rows // step, differentiate, 0)
    store_to(d_both_out, d_both)
    d_down[...] = dot(hidden[...], grads[...], ((0,), (0,))).astype(BF)

    for k in (places - 1, 1, 2, 0):
        for h in range(2):
            from_cols = slice(k * line + h * part_rows, k * line + (h + 1) * part_rows)
            weights = dot(x[:, from_cols], d_both[...], ((0,), (0,))).astype(BF)
            for i in range(count):
                to = h * size_half + i * part_rows
                terms[k, to:to + part_rows, :] = weights[:, i * LANES:(i + 1) * LANES]
            for j in range(columns):
                to = h * size_half + count * part_rows + j * piece
                terms[k, to:to + piece, :] = d_down[down_rows(k, h), j * LANES:(j + 1) * LANES]
        store_to(outs[k], terms.at[k])
        if k == 1:
            store_to(outer_out, terms.at[jnp.where(z == 0, places - 1, 1)])
    for copy in stores:
        copy.wait()


def rows_kernel(chunks, *refs):
    keep, give = refs[-2:]
    slots = keep.shape[0]

    def add(pairs, dims):
        total = sum(dot(a[...], b[...], dims) for a, b in pairs).astype(BF)
        keep[...], give[...] = total[:slots], total[slots:]

    chunked = [refs[4 * n:4 * n + 4] for n in range(chunks)]

    @pl.when(pl.program_id(0) < pl.num_programs(0) // 2)
    def _():
        add([(hidden, w_down) for _, w_down, hidden, _ in chunked], ((1,), (0,)))

    @pl.when(pl.program_id(0) >= pl.num_programs(0) // 2)
    def _():
        add([(d_both, gate_up) for gate_up, _, _, d_both in chunked], ((1,), (1,)))


def in_vmem(count):
    return [pl.BlockSpec(memory_space=pltpu.VMEM)] * count


IN_SMEM = pl.BlockSpec(memory_space=pltpu.SMEM)


def pack(pieces, x, gate, up, down, shuffle):
    rows, hidden_width = gate.shape
    sizes = [(rows * hidden_width + down.size // 2) * piece // sum(pieces) // LANES for piece in pieces]
    return pl.pallas_call(
        functools.partial(pack_kernel, pieces),
        out_shape=[jax.ShapeDtypeStruct((size, LANES), BF) for size in sizes for _ in range(2)],
        in_specs=[IN_SMEM] + in_vmem(4),
        out_specs=in_vmem(2 * len(pieces)),
        compiler_params=pltpu.CompilerParams(vmem_limit_bytes=VMEM_BYTES // 2),
    )(x, gate, up, down, shuffle)


def unpack(pieces, x, packed, shuffle, gate_shape, down_shape):
    return pl.pallas_call(
        functools.partial(unpack_kernel, pieces),
        out_shape=[jax.ShapeDtypeStruct(shape, F32) for shape in (gate_shape, gate_shape, down_shape)],
        in_specs=[IN_SMEM] + in_vmem(len(packed) + 1),
        out_specs=in_vmem(3),
        compiler_params=pltpu.CompilerParams(vmem_limit_bytes=VMEM_BYTES // 2),
    )(x, *packed, shuffle)


def expert(z, places, units, weights, mine, theirs):
    size = weights[0].shape[0]
    slots, width = mine.shape[0], mine.shape[1] // 2
    rows = 2 * slots
    for_rows = [
        jax.ShapeDtypeStruct(shape, BF) for shape in ((width, 2 * units), (units, width), (rows, units), (rows, 2 * units))
    ]
    outs = pl.pallas_call(
        expert_kernel,
        out_shape=for_rows + [jax.ShapeDtypeStruct((size, LANES), BF)] * 5,
        in_specs=[IN_SMEM] + [pl.BlockSpec(memory_space=pl.ANY)] * 8,
        out_specs=[pl.BlockSpec(memory_space=pl.ANY)] * 9,
        scratch_shapes=[
            pltpu.VMEM((places, size, LANES), BF),
            pltpu.VMEM((rows, width), BF),
            pltpu.VMEM((rows, width), BF),
            pltpu.VMEM((width, 2 * units), BF),
            pltpu.VMEM((units, width), BF),
            pltpu.VMEM((rows, 2 * units), F32),
            pltpu.VMEM((rows, units), F32),
            pltpu.VMEM((rows, units), BF),
            pltpu.VMEM((rows, 2 * units), BF),
            pltpu.VMEM((units, width), BF),
            pltpu.VMEM((places, size, LANES), BF),
            pltpu.SemaphoreType.DMA((places + 4,)),
            pltpu.SemaphoreType.DMA((9,)),
        ],
        compiler_params=pltpu.CompilerParams(vmem_limit_bytes=VMEM_BYTES),
        cost_estimate=pl.CostEstimate(
            flops=12 * rows * width * units, bytes_accessed=4 * 2**20, transcendentals=rows * units
        ),
    )(z, *weights, mine, theirs)
    return outs[:4], outs[4], outs[5:]


def token_rows(chunks, slots, width):
    tile = 2 * LANES
    tiles = width // tile
    in_specs = []
    for gate_up, w_down, hidden, d_both in chunks:
        in_specs += [
            pl.BlockSpec((tile, gate_up.shape[1]), lambda n: (jnp.maximum(n - tiles, 0), 0)),
            pl.BlockSpec((w_down.shape[0], tile), lambda n: (0, jnp.minimum(n, tiles - 1))),
            pl.BlockSpec(hidden.shape, lambda n: (0, 0)),
            pl.BlockSpec(d_both.shape, lambda n: (0, 0)),
        ]
    units = sum(chunk[1].shape[0] for chunk in chunks)
    return pl.pallas_call(
        functools.partial(rows_kernel, len(chunks)),
        grid=(2 * tiles,),
        out_shape=[jax.ShapeDtypeStruct((slots, 2 * width), BF)] * 2,
        in_specs=in_specs,
        out_specs=[pl.BlockSpec((slots, tile), lambda n: (0, n))] * 2,
        compiler_params=pltpu.CompilerParams(vmem_limit_bytes=VMEM_BYTES // 2),
        cost_estimate=pl.CostEstimate(
            flops=12 * slots * width * units, bytes_accessed=2 * 2**20, transcendentals=0
        ),
    )(*(array for chunk in chunks for array in chunk))


def local(tokens, expert_ids, gate_probs, w_gate, w_up, w_down, d_out):
    g = Grid()
    rows, topk = expert_ids.shape
    width = tokens.shape[1]
    hidden_width = w_gate.shape[2]
    half = hidden_width // 2
    experts = g.experts
    cap = rows * topk * 9 // (8 * experts)
    slots = experts * cap
    first = g.c == 0
    even = g.x == 0

    block = hidden_width // g.dps
    part = block // 2
    pieces = (2 * part // 3, part // 3)
    in_kernels = g.zs == 4 and slots % 16 == 0 and part % 48 == 0 and all(2 * p * g.dps % LANES == 0 for p in pieces)
    if not in_kernels:
        pieces = (part,)
    shuffle = shuffle_matrix(g.x, g.dps, hidden_width, pieces)

    def out_a(z, x, q, c):
        return z, c, q, x

    def out_b(z, x, q, c):
        return z, c, q, 1 - x

    def back_a(z, x, q, c):
        return z, c, q, x

    def back_b(z, x, q, c):
        return z, 1 - c, q, x

    def spread(part_a, part_b):
        got_a, got_b = g.send(part_a, out_a), g.send(part_b, out_b)
        return jnp.concatenate([jnp.where(first, got_a, got_b), jnp.where(first, got_b, got_a)], axis=0)

    def unspread(both):
        n = both.shape[0] // 2
        low, high = both[:n], both[n:]
        return g.send(jnp.where(first, low, high), back_a), g.send(jnp.where(first, high, low), back_b)

    expert_iota = jnp.arange(experts, dtype=jnp.int32)
    chosen = expert_ids[:, :, None] == expert_iota
    named = jnp.any(chosen, axis=1).astype(BF)
    token_iota = jnp.arange(rows, dtype=jnp.int32)
    earlier = (token_iota[:, None] > token_iota[None, :]).astype(BF)
    before = dot(earlier, named)
    slot = jnp.sum(jnp.where(chosen, before[:, None, :], 0.0), axis=2).astype(jnp.int32)
    relative = ((expert_ids // 2 - g.q + g.qs) % g.qs) * 2 + ((expert_ids % 2) ^ g.x)
    dest = relative * cap + slot
    slot_iota = jnp.arange(slots, dtype=jnp.int32)
    pair = dest[:, :, None] == slot_iota
    placing = jnp.any(pair, axis=1).astype(BF)
    weighted = jnp.sum(jnp.where(pair, gate_probs[:, :, None], 0.0), axis=1)
    slot_probs = jnp.sum(weighted, axis=0)

    def member(r, sign):
        def move(z, x, q, c):
            return z, x ^ (r % 2), (q + sign * (r // 2)) % g.qs, c

        return move

    def other_core(z, x, q, c):
        return z, x, q, 1 - c

    def exchange(value, sign):
        got = [value[:cap]] + [g.send(value[r * cap:(r + 1) * cap], member(r, sign)) for r in range(1, experts)]
        return jnp.concatenate(got, axis=0)

    line_width = width // g.zs
    turned = lax.dynamic_slice(jnp.concatenate([tokens, tokens], axis=1), (0, g.z * line_width), (rows, width))
    sent = jnp.concatenate(
        [
            dot(placing, turned, ((0,), (0,))).astype(BF),
            (slot_probs[:, None] * dot(placing, d_out, ((0,), (0,)))).astype(BF),
        ],
        axis=1,
    )
    def combine(returned, back_rows):
        high = lax.reduce_precision(weighted, 8, 7)
        mixed = (dot(high.astype(BF), returned) + dot((weighted - high).astype(BF), returned)).astype(BF)
        products = dot(d_out, returned, ((1,), (1,)))
        d_probs = jnp.sum(jnp.where(pair, products[:, None, :], 0.0), axis=2)
        d_turned = dot(placing, back_rows).astype(BF)
        d_tokens = lax.dynamic_slice(
            jnp.concatenate([d_turned, d_turned], axis=1), (0, (g.zs - g.z) * line_width), (rows, width)
        )
        return mixed, d_tokens, d_probs

    shapes = w_gate.shape[1:], w_down.shape[1:]
    together = lax.optimization_barrier
    if in_kernels:
        place_x, place_z = g.x.reshape(1).astype(jnp.int32), g.z.reshape(1).astype(jnp.int32)
        units = [piece * g.dps for piece in pieces]
        a, b, a2, b2 = pack(pieces, place_x, w_gate[0], w_up[0], w_down[0], shuffle)
        ups, downs, passing = {0: 1, 1: 2, 2: 3}, {1: 0, 2: 1, 3: 2}, {2: 3, 1: 0}
        outward, inward_up, inward_down = {0: 1, 3: 2}, {0: 1, 1: 2}, {3: 2, 2: 1}
        to_last = g.z == 2

        shard, a2, b2 = together((spread(a, b), a2, b2))
        up, down = g.hop(shard, ups), g.hop(shard, downs)
        shard2, sent = together((spread(a2, b2), sent))
        up, down = together((up, down))
        far = g.hop(jnp.where(g.z == 1, up, down), {1: 3, 2: 0})
        up_2, down_2 = g.hop(up, {1: 2, 2: 3}), g.hop(down, {1: 0, 2: 1})
        mine = tie(exchange(sent, 1), far, up_2, down_2)
        theirs = g.send(mine, other_core)
        shard2 = tie(shard2, mine)
        up2, down2 = g.hop(shard2, ups), g.hop(shard2, downs)
        chunk, outer, terms = expert(place_z, g.zs, units[0], (shard, up, down, up_2, down_2, far), mine, theirs)
        begun = g.hop(outer, outward)
        up2, down2 = tie(up2, outer), tie(down2, outer)
        up2_2, down2_2 = g.hop(up2, {1: 2, 2: 3}), g.hop(down2, {1: 0, 2: 1})
        passed = jnp.where(to_last, up2_2, down2_2)
        last2 = g.hop(passed, passing)
        middle = added(terms[2], tie(begun, passed))
        sum_up, sum_down = g.hop(middle, inward_up), g.hop(middle, inward_down)
        chunk2, outer2, terms2 = expert(
            place_z, g.zs, units[1], (shard2, up2, down2, up2_2, down2_2, tie(last2, middle)), mine, theirs
        )
        keep, give = token_rows((chunk, chunk2), slots, width)
        sum_up, sum_down = tie(sum_up, keep, give), tie(sum_down, keep, give)
        sum_up, sum_down = added(terms[1], sum_up), added(terms[3], sum_down)
        give, outer2 = tie(give, sum_up, sum_down), tie(outer2, sum_up, sum_down)
        sum_up, sum_down = g.hop(sum_up, ups), g.hop(sum_down, downs)
        begun2 = g.hop(outer2, outward)
        sums = added(keep, g.send(give, other_core)).reshape(g.qs, 2, cap, 2 * width)

        def along_x(rows):
            return jnp.stack([rows[:, 0], g.send(rows[:, 1], lambda z, x, q, c: (z, 1 - x, q, c))], axis=1)

        def along_q(rows):
            return jnp.stack(
                [rows[0]] + [g.send(rows[d], lambda z, x, q, c, d=d: (z, x, (q - d) % g.qs, c)) for d in range(1, g.qs)]
            )

        returned, back_rows = along_x(sums[..., :width]), along_q(sums[..., width:])
        grad = added(terms[0], tie(sum_up, sums), tie(sum_down, sums))
        begun2, returned, back_rows, grad = together((begun2, returned, back_rows, grad))
        middle2 = added(terms2[2], begun2)
        sum_up2, sum_down2 = g.hop(middle2, inward_up), g.hop(middle2, inward_down)
        returned, back_rows = along_q(returned), along_x(back_rows)
        sum_up2, sum_down2 = tie(sum_up2, grad), tie(sum_down2, grad)
        sum_up2, sum_down2 = added(terms2[1], sum_up2), added(terms2[3], sum_down2)
        grads = unspread(tie(grad, sum_up2, sum_down2))
        sum_up2, sum_down2 = g.hop(sum_up2, ups), g.hop(sum_down2, downs)
        mixed, d_tokens, d_probs = combine(returned.reshape(slots, width), back_rows.reshape(slots, width))
        sum_up2, sum_down2 = (tie(value, mixed, d_tokens, d_probs, *grads) for value in (sum_up2, sum_down2))
        grads += unspread(added(terms2[0], sum_up2, sum_down2))
        d_w_gate, d_w_up, d_w_down = unpack(pieces, place_x, grads, shuffle, *shapes)
    else:
        gate_cols, up_cols = dot(w_gate[0], shuffle).astype(BF), dot(w_up[0], shuffle).astype(BF)
        gate_up_shard = spread(
            jnp.concatenate([gate_cols[:, :half], up_cols[:, :half]], axis=1),
            jnp.concatenate([gate_cols[:, half:], up_cols[:, half:]], axis=1),
        )
        down_low, down_high = w_down[0, :part], w_down[0, part:]
        down_shard = spread(jnp.where(even, down_low, down_high), jnp.where(even, down_high, down_low))
        gate_up = jnp.concatenate(g.line(gate_up_shard), axis=0)
        down = jnp.concatenate(g.straight(g.line(down_shard)), axis=0)
        mine = exchange(sent, 1)
        inputs = jnp.concatenate([mine, g.send(mine, other_core)], axis=0)
        arrived, d_produced = inputs[:, :width], inputs[:, width:]
        pre = dot(arrived, gate_up)
        gate_pre, up_pre = pre[:, :half], pre[:, half:]
        sig = jax.nn.sigmoid(gate_pre)
        act = gate_pre * sig
        hidden = (act * up_pre).astype(BF)
        d_hidden = dot(d_produced, down, ((1,), (1,)))
        d_gate = (d_hidden * up_pre * sig * (1.0 + gate_pre * (1.0 - sig))).astype(BF)
        d_up = (d_hidden * act).astype(BF)
        d_both = jnp.concatenate([d_gate, d_up], axis=1)
        down_part = dot(hidden, d_produced, ((0,), (0,))).astype(BF)
        both_part = dot(arrived, d_both, ((0,), (0,))).astype(BF)
        partial = jnp.concatenate([dot(hidden, down), dot(d_both, gate_up, ((1,), (1,)))], axis=1).astype(BF)
        got = exchange(added(partial[:slots], g.send(partial[slots:], other_core)), -1)
        down_a, down_b = unspread(
            g.line_sum(
                lambda k: lax.dynamic_slice_in_dim(down_part, ((g.z + k) % g.zs) * (2 * part), 2 * part)
            )
        )
        d_w_down = jnp.where(
            even, jnp.concatenate([down_a, down_b], axis=0), jnp.concatenate([down_b, down_a], axis=0)
        ).astype(F32)
        both_a, both_b = unspread(g.line_sum(lambda k: both_part[k * line_width:(k + 1) * line_width]))
        d_w_gate, d_w_up = (
            dot(jnp.concatenate([both_a[:, cols], both_b[:, cols]], axis=1), shuffle, ((1,), (1,)))
            for cols in (slice(0, half), slice(half, None))
        )
        mixed, d_tokens, d_probs = combine(got[:, :width], got[:, width:])
    return (mixed, d_tokens, d_probs, d_w_gate[None], d_w_up[None], d_w_down[None])


def solution(mesh):
    rows = P(("dp", "expert"), None)
    weight = P("expert", "dp", None)
    return jax.shard_map(
        local,
        mesh=mesh,
        in_specs=(rows, rows, rows, weight, weight, weight, rows),
        out_specs=(rows, rows, rows, weight, weight, weight),
        check_vma=False,
    )
```

```python
import functools

import jax
import jax.numpy as jnp
from jax import lax
from jax.experimental import pallas as pl
from jax.experimental.pallas import tpu as pltpu
from jax.sharding import PartitionSpec as P

BF = jnp.bfloat16
F32 = jnp.float32
BOTH = ("dp", "expert")


def dot(a, b, dims=((1,), (0,))):
    return lax.dot_general(a, b, (dims, ((), ())), preferred_element_type=F32)


def tie(value, *others):
    return lax.optimization_barrier((value,) + others)[0]


def added(*terms):
    return sum(t.astype(F32) for t in terms).astype(BF)


class Grid:
    def __init__(self):
        self.dps, self.experts = lax.axis_size("dp"), lax.axis_size("expert")
        self.zs, self.qs = self.dps // 2, self.experts // 2
        dp, ex = lax.axis_index("dp"), lax.axis_index("expert")
        self.z, self.x, self.q, self.c = dp // 2, dp % 2, ex // 2, ex % 2

    def send(self, value, move):
        pairs = []
        for z in range(self.zs):
            for x in range(2):
                for q in range(self.qs):
                    for c in range(2):
                        to = move(z, x, q, c)
                        if to is not None:
                            pairs.append((self.flat(z, x, q, c), self.flat(*to)))
        return lax.ppermute(value, BOTH, pairs)

    def flat(self, z, x, q, c):
        return (z * 2 + x) * self.experts + q * 2 + c

    def hop(self, value, where):
        return self.send(value, lambda z, x, q, c: (where[z], x, q, c) if z in where else None)

    def line(self, shard):
        n = self.zs
        ups, downs = [shard], [shard]
        for s in range(1, n):
            ups.append(self.hop(ups[-1], {i: i + 1 for i in range(s - 1, n - 1)}))
            downs.append(self.hop(downs[-1], {i: i - 1 for i in range(1, n - s + 1)}))
        return [shard] + [jnp.where(self.z + s < n, downs[s], ups[n - s]) for s in range(1, n)]

    def straight(self, blocks):
        n = self.zs
        rows = []
        for j in range(n):
            row = blocks[j]
            for z in range(1, n):
                row = jnp.where(self.z == z, blocks[(j - z) % n], row)
            rows.append(row)
        return rows

    def line_sum(self, block):
        n = self.zs
        up, down = self.hop(block(n - 1), {0: 1}), self.hop(block(1), {n - 1: n - 2})
        for r in range(2, n):
            up = self.hop(added(block(n - r), up), {i: i + 1 for i in range(r)})
            down = self.hop(added(block(r), down), {i: i - 1 for i in range(n - r, n)})
        return added(block(0), up, down)


LANES = 256
MIB = 2**20


def shuffle_matrix(x, dps, hidden_width, pieces):
    block, half = hidden_width // dps, hidden_width // 2
    sources, start = [], 0
    for piece in pieces:
        unit = jnp.arange(piece * dps, dtype=jnp.int32)
        sources.append((unit // piece) * block + start + unit % piece)
        start += piece
    low = jnp.concatenate(sources)
    source = jnp.concatenate([low + x * (block // 2), low + (1 - x) * (block // 2)])
    return (jnp.arange(hidden_width, dtype=jnp.int32)[:, None] == source[None, :]).astype(BF)


def pack_kernel(pieces, x_ref, gate_ref, up_ref, down_ref, shuffle_ref, *outs):
    rows, hidden_width = gate_ref.shape
    half, block = hidden_width // 2, down_ref.shape[0]
    shuffle = shuffle_ref[...]
    gate, up = dot(gate_ref[...], shuffle).astype(BF), dot(up_ref[...], shuffle).astype(BF)
    x = x_ref[0]
    done = 0
    for number, piece in enumerate(pieces):
        units = piece * half // sum(pieces)
        count = 2 * units // LANES
        for side, start in ((0, x), (1, 1 - x)):
            ref = outs[2 * number + side]
            at = side * half + done * units // piece
            both = jnp.concatenate([gate[:, at:at + units], up[:, at:at + units]], axis=1)
            for i in range(count):
                ref[i * rows:(i + 1) * rows, :] = both[:, i * LANES:(i + 1) * LANES]
            source = pl.ds(pl.multiple_of(start * (block // 2) + done, 16), piece)
            for j in range(down_ref.shape[1] // LANES):
                to = count * rows + j * piece
                ref[to:to + piece, :] = down_ref[source, j * LANES:(j + 1) * LANES]
        done += piece


def unpack_kernel(pieces, x_ref, *refs):
    packed, (shuffle_ref, gate_ref, up_ref, down_ref) = refs[:-4], refs[-4:]
    rows, hidden_width = gate_ref.shape
    half, block = hidden_width // 2, down_ref.shape[0]
    x = x_ref[0]
    gates, ups = [[], []], [[], []]
    done = 0
    for number, piece in enumerate(pieces):
        units = piece * half // sum(pieces)
        count = 2 * units // LANES
        for side, start in ((0, x), (1, 1 - x)):
            ref = packed[2 * number + side]
            both = jnp.concatenate([ref[i * rows:(i + 1) * rows, :] for i in range(count)], axis=1)
            gates[side].append(both[:, :units])
            ups[side].append(both[:, units:])
            to = pl.ds(pl.multiple_of(start * (block // 2) + done, 16), piece)
            for j in range(down_ref.shape[1] // LANES):
                at = count * rows + j * piece
                down_ref[to, j * LANES:(j + 1) * LANES] = ref[at:at + piece, :].astype(F32)
        done += piece
    shuffle = shuffle_ref[...]
    gate_ref[...] = dot(jnp.concatenate(gates[0] + gates[1], axis=1), shuffle, ((1,), (1,)))
    up_ref[...] = dot(jnp.concatenate(ups[0] + ups[1], axis=1), shuffle, ((1,), (1,)))


def expert_kernel(z_ref, own, up, down, up_2, down_2, last, mine, theirs, *refs):
    weight_outs, (hidden_out, d_both_out, outer_out), outs, refs = refs[:2], refs[2:5], refs[5:9], refs[9:]
    packed, x, grads, gate_up, w_down, pre, d_hidden, hidden, d_both, d_down, terms, load, store = refs
    places, size, _ = packed.shape
    rows, width = x.shape
    slots = rows // 2
    line = width // places
    part_rows = line // 2
    units = w_down.shape[0]
    piece = units // places // 2
    count, columns = 2 * units // LANES, width // LANES
    size_half = size // 2
    z = z_ref[0]

    loads = [
        pltpu.make_async_copy(a, b, load.at[places + n])
        for n, (a, b) in enumerate(
            (
                (mine.at[:, :width], x.at[:slots]),
                (theirs.at[:, :width], x.at[slots:]),
                (mine.at[:, width:], grads.at[:slots]),
                (theirs.at[:, width:], grads.at[slots:]),
            )
        )
    ]
    for copy in loads[:2]:
        copy.start()
    pltpu.make_async_copy(own, packed.at[0], load.at[0]).start()
    for s, is_one, one, other in (
        (1, z == places - 1, last, down),
        (2, z < 2, down_2, up_2),
        (3, z == 0, last, up),
    ):
        @pl.when(is_one)
        def _():
            pltpu.make_async_copy(one, packed.at[s], load.at[s]).start()

        @pl.when(jnp.logical_not(is_one))
        def _():
            pltpu.make_async_copy(other, packed.at[s], load.at[s]).start()

    for copy in loads[2:]:
        copy.start()

    def down_rows(k, h):
        return pl.ds(pl.multiple_of(lax.rem(z + k, places) * (2 * piece) + h * piece, 16), piece)

    for copy in loads[:2]:
        copy.wait()
    for s in range(places):
        pltpu.make_async_copy(own, packed.at[s], load.at[s]).wait()
        for h in range(2):
            for i in range(count):
                at = h * size_half + i * part_rows
                to = s * line + h * part_rows
                gate_up[to:to + part_rows, i * LANES:(i + 1) * LANES] = packed[s, at:at + part_rows, :]
            for j in range(columns):
                at = h * size_half + count * part_rows + j * piece
                w_down[down_rows(s, h), j * LANES:(j + 1) * LANES] = packed[s, at:at + piece, :]
        block = slice(s * line, (s + 1) * line)
        for i in range(count):
            cols = slice(i * LANES, (i + 1) * LANES)
            product = dot(x[:, block], gate_up[block, cols])
            pre[:, cols] = product if s == 0 else pre[:, cols] + product

    stores = []

    def store_to(out, value):
        stores.append(pltpu.make_async_copy(value, out, store.at[len(stores)]))
        stores[-1].start()

    store_to(weight_outs[0], gate_up)
    store_to(weight_outs[1], w_down)
    step = 64 if rows % 64 == 0 else 16

    def activate(r, _):
        at = pl.ds(pl.multiple_of(r * step, 16), step)
        gate_pre, up_pre = pre[at, :units], pre[at, units:]
        sig = 1.0 / (1.0 + jnp.exp(-gate_pre))
        act = gate_pre * sig
        hidden[at, :] = (act * up_pre).astype(BF)
        pre[at, :units] = up_pre * sig * (1.0 + gate_pre * (1.0 - sig))
        pre[at, units:] = act
        return 0

    lax.fori_loop(0, rows // step, activate, 0)
    store_to(hidden_out, hidden)
    for copy in loads[2:]:
        copy.wait()
    d_hidden[...] = dot(grads[...], w_down[...], ((1,), (1,)))

    def differentiate(r, _):
        at = pl.ds(pl.multiple_of(r * step, 16), step)
        d_h = d_hidden[at, :]
        d_both[at, :units] = (d_h * pre[at, :units]).astype(BF)
        d_both[at, units:] = (d_h * pre[at, units:]).astype(BF)
        return 0

    lax.fori_loop(0, rows // step, differentiate, 0)
    store_to(d_both_out, d_both)
    d_down[...] = dot(hidden[...], grads[...], ((0,), (0,))).astype(BF)

    for k in (places - 1, 1, 2, 0):
        for h in range(2):
            from_cols = slice(k * line + h * part_rows, k * line + (h + 1) * part_rows)
            weights = dot(x[:, from_cols], d_both[...], ((0,), (0,))).astype(BF)
            for i in range(count):
                to = h * size_half + i * part_rows
                terms[k, to:to + part_rows, :] = weights[:, i * LANES:(i + 1) * LANES]
            for j in range(columns):
                to = h * size_half + count * part_rows + j * piece
                terms[k, to:to + piece, :] = d_down[down_rows(k, h), j * LANES:(j + 1) * LANES]
        store_to(outs[k], terms.at[k])
        if k == 1:
            store_to(outer_out, terms.at[jnp.where(z == 0, places - 1, 1)])
    for copy in stores:
        copy.wait()


def rows_kernel(chunks, *refs):
    keep, give = refs[-2:]
    slots = keep.shape[0]

    def add(pairs, dims):
        total = sum(dot(a[...], b[...], dims) for a, b in pairs).astype(BF)
        keep[...], give[...] = total[:slots], total[slots:]

    chunked = [refs[4 * n:4 * n + 4] for n in range(chunks)]

    @pl.when(pl.program_id(0) < pl.num_programs(0) // 2)
    def _():
        add([(hidden, w_down) for _, w_down, hidden, _ in chunked], ((1,), (0,)))

    @pl.when(pl.program_id(0) >= pl.num_programs(0) // 2)
    def _():
        add([(d_both, gate_up) for gate_up, _, _, d_both in chunked], ((1,), (1,)))


def in_vmem(count):
    return [pl.BlockSpec(memory_space=pltpu.VMEM)] * count


IN_SMEM = pl.BlockSpec(memory_space=pltpu.SMEM)


def pack(pieces, x, gate, up, down, shuffle):
    rows, hidden_width = gate.shape
    sizes = [(rows * hidden_width + down.size // 2) * piece // sum(pieces) // LANES for piece in pieces]
    return pl.pallas_call(
        functools.partial(pack_kernel, pieces),
        out_shape=[jax.ShapeDtypeStruct((size, LANES), BF) for size in sizes for _ in range(2)],
        in_specs=[IN_SMEM] + in_vmem(4),
        out_specs=in_vmem(2 * len(pieces)),
        compiler_params=pltpu.CompilerParams(vmem_limit_bytes=58 * MIB),
    )(x, gate, up, down, shuffle)


def unpack(pieces, x, packed, shuffle, gate_shape, down_shape):
    return pl.pallas_call(
        functools.partial(unpack_kernel, pieces),
        out_shape=[jax.ShapeDtypeStruct(shape, F32) for shape in (gate_shape, gate_shape, down_shape)],
        in_specs=[IN_SMEM] + in_vmem(len(packed) + 1),
        out_specs=in_vmem(3),
        compiler_params=pltpu.CompilerParams(vmem_limit_bytes=24 * MIB),
    )(x, *packed, shuffle)


def expert(z, places, units, weights, mine, theirs):
    size = weights[0].shape[0]
    slots, width = mine.shape[0], mine.shape[1] // 2
    rows = 2 * slots
    for_rows = [
        jax.ShapeDtypeStruct(shape, BF) for shape in ((width, 2 * units), (units, width), (rows, units), (rows, 2 * units))
    ]
    outs = pl.pallas_call(
        expert_kernel,
        out_shape=for_rows + [jax.ShapeDtypeStruct((size, LANES), BF)] * 5,
        in_specs=[IN_SMEM] + [pl.BlockSpec(memory_space=pl.ANY)] * 8,
        out_specs=[pl.BlockSpec(memory_space=pl.ANY)] * 9,
        scratch_shapes=[
            pltpu.VMEM((places, size, LANES), BF),
            pltpu.VMEM((rows, width), BF),
            pltpu.VMEM((rows, width), BF),
            pltpu.VMEM((width, 2 * units), BF),
            pltpu.VMEM((units, width), BF),
            pltpu.VMEM((rows, 2 * units), F32),
            pltpu.VMEM((rows, units), F32),
            pltpu.VMEM((rows, units), BF),
            pltpu.VMEM((rows, 2 * units), BF),
            pltpu.VMEM((units, width), BF),
            pltpu.VMEM((places, size, LANES), BF),
            pltpu.SemaphoreType.DMA((places + 4,)),
            pltpu.SemaphoreType.DMA((9,)),
        ],
        compiler_params=pltpu.CompilerParams(vmem_limit_bytes=24 * MIB),
        cost_estimate=pl.CostEstimate(
            flops=12 * rows * width * units, bytes_accessed=4 * 2**20, transcendentals=rows * units
        ),
    )(z, *weights, mine, theirs)
    return outs[:4], outs[4], outs[5:]


def token_rows(chunks, slots, width):
    tile = 2 * LANES
    tiles = width // tile
    in_specs = []
    for gate_up, w_down, hidden, d_both in chunks:
        in_specs += [
            pl.BlockSpec((tile, gate_up.shape[1]), lambda n: (jnp.maximum(n - tiles, 0), 0)),
            pl.BlockSpec((w_down.shape[0], tile), lambda n: (0, jnp.minimum(n, tiles - 1))),
            pl.BlockSpec(hidden.shape, lambda n: (0, 0)),
            pl.BlockSpec(d_both.shape, lambda n: (0, 0)),
        ]
    units = sum(chunk[1].shape[0] for chunk in chunks)
    return pl.pallas_call(
        functools.partial(rows_kernel, len(chunks)),
        grid=(2 * tiles,),
        out_shape=[jax.ShapeDtypeStruct((slots, 2 * width), BF)] * 2,
        in_specs=in_specs,
        out_specs=[pl.BlockSpec((slots, tile), lambda n: (0, n))] * 2,
        compiler_params=pltpu.CompilerParams(vmem_limit_bytes=24 * MIB),
        cost_estimate=pl.CostEstimate(
            flops=12 * slots * width * units, bytes_accessed=2 * 2**20, transcendentals=0
        ),
    )(*(array for chunk in chunks for array in chunk))


def local(tokens, expert_ids, gate_probs, w_gate, w_up, w_down, d_out):
    g = Grid()
    rows, topk = expert_ids.shape
    width = tokens.shape[1]
    hidden_width = w_gate.shape[2]
    half = hidden_width // 2
    experts = g.experts
    cap = rows * topk * 9 // (8 * experts)
    slots = experts * cap
    first = g.c == 0
    even = g.x == 0

    block = hidden_width // g.dps
    part = block // 2
    pieces = (2 * part // 3, part // 3)
    in_kernels = g.zs == 4 and slots % 16 == 0 and part % 48 == 0 and all(2 * p * g.dps % LANES == 0 for p in pieces)
    if not in_kernels:
        pieces = (part,)
    shuffle = shuffle_matrix(g.x, g.dps, hidden_width, pieces)

    def out_a(z, x, q, c):
        return z, c, q, x

    def out_b(z, x, q, c):
        return z, c, q, 1 - x

    def back_a(z, x, q, c):
        return z, c, q, x

    def back_b(z, x, q, c):
        return z, 1 - c, q, x

    def spread(part_a, part_b):
        got_a, got_b = g.send(part_a, out_a), g.send(part_b, out_b)
        return jnp.concatenate([jnp.where(first, got_a, got_b), jnp.where(first, got_b, got_a)], axis=0)

    def unspread(both):
        n = both.shape[0] // 2
        low, high = both[:n], both[n:]
        return g.send(jnp.where(first, low, high), back_a), g.send(jnp.where(first, high, low), back_b)

    expert_iota = jnp.arange(experts, dtype=jnp.int32)
    chosen = expert_ids[:, :, None] == expert_iota
    named = jnp.any(chosen, axis=1).astype(BF)
    token_iota = jnp.arange(rows, dtype=jnp.int32)
    earlier = (token_iota[:, None] > token_iota[None, :]).astype(BF)
    before = dot(earlier, named)
    slot = jnp.sum(jnp.where(chosen, before[:, None, :], 0.0), axis=2).astype(jnp.int32)
    relative = ((expert_ids // 2 - g.q + g.qs) % g.qs) * 2 + ((expert_ids % 2) ^ g.x)
    dest = relative * cap + slot
    slot_iota = jnp.arange(slots, dtype=jnp.int32)
    pair = dest[:, :, None] == slot_iota
    placing = jnp.any(pair, axis=1).astype(BF)
    weighted = jnp.sum(jnp.where(pair, gate_probs[:, :, None], 0.0), axis=1)
    slot_probs = jnp.sum(weighted, axis=0)

    def member(r, sign):
        def move(z, x, q, c):
            return z, x ^ (r % 2), (q + sign * (r // 2)) % g.qs, c

        return move

    def other_core(z, x, q, c):
        return z, x, q, 1 - c

    def exchange(value, sign):
        got = [value[:cap]] + [g.send(value[r * cap:(r + 1) * cap], member(r, sign)) for r in range(1, experts)]
        return jnp.concatenate(got, axis=0)

    line_width = width // g.zs
    turned = lax.dynamic_slice(jnp.concatenate([tokens, tokens], axis=1), (0, g.z * line_width), (rows, width))
    sent = jnp.concatenate(
        [
            dot(placing, turned, ((0,), (0,))).astype(BF),
            (slot_probs[:, None] * dot(placing, d_out, ((0,), (0,)))).astype(BF),
        ],
        axis=1,
    )
    def combine(returned, back_rows):
        high = lax.reduce_precision(weighted, 8, 7)
        mixed = (dot(high.astype(BF), returned) + dot((weighted - high).astype(BF), returned)).astype(BF)
        products = dot(d_out, returned, ((1,), (1,)))
        d_probs = jnp.sum(jnp.where(pair, products[:, None, :], 0.0), axis=2)
        d_turned = dot(placing, back_rows).astype(BF)
        d_tokens = lax.dynamic_slice(
            jnp.concatenate([d_turned, d_turned], axis=1), (0, (g.zs - g.z) * line_width), (rows, width)
        )
        return mixed, d_tokens, d_probs

    shapes = w_gate.shape[1:], w_down.shape[1:]
    together = lax.optimization_barrier
    if in_kernels:
        place_x, place_z = g.x.reshape(1).astype(jnp.int32), g.z.reshape(1).astype(jnp.int32)
        units = [piece * g.dps for piece in pieces]
        a, b, a2, b2 = pack(pieces, place_x, w_gate[0], w_up[0], w_down[0], shuffle)
        ups, downs, passing = {0: 1, 1: 2, 2: 3}, {1: 0, 2: 1, 3: 2}, {2: 3, 1: 0}
        outward, inward_up, inward_down = {0: 1, 3: 2}, {0: 1, 1: 2}, {3: 2, 2: 1}
        to_last = g.z == 2

        shard, a2, b2 = together((spread(a, b), a2, b2))
        up, down = g.hop(shard, ups), g.hop(shard, downs)
        shard2, sent = together((spread(a2, b2), sent))
        up, down = together((up, down))
        far = g.hop(jnp.where(g.z == 1, up, down), {1: 3, 2: 0})
        up_2, down_2 = g.hop(up, {1: 2, 2: 3}), g.hop(down, {1: 0, 2: 1})
        mine = tie(exchange(sent, 1), far, up_2, down_2)
        theirs = g.send(mine, other_core)
        shard2 = tie(shard2, mine)
        up2, down2 = g.hop(shard2, ups), g.hop(shard2, downs)
        chunk, outer, terms = expert(place_z, g.zs, units[0], (shard, up, down, up_2, down_2, far), mine, theirs)
        begun = g.hop(outer, outward)
        up2, down2 = tie(up2, outer), tie(down2, outer)
        up2_2, down2_2 = g.hop(up2, {1: 2, 2: 3}), g.hop(down2, {1: 0, 2: 1})
        passed = jnp.where(to_last, up2_2, down2_2)
        last2 = g.hop(passed, passing)
        middle = added(terms[2], tie(begun, passed))
        sum_up, sum_down = g.hop(middle, inward_up), g.hop(middle, inward_down)
        chunk2, outer2, terms2 = expert(
            place_z, g.zs, units[1], (shard2, up2, down2, up2_2, down2_2, tie(last2, middle)), mine, theirs
        )
        keep, give = token_rows((chunk, chunk2), slots, width)
        sum_up, sum_down = tie(sum_up, keep, give), tie(sum_down, keep, give)
        sum_up, sum_down = added(terms[1], sum_up), added(terms[3], sum_down)
        give, outer2 = tie(give, sum_up, sum_down), tie(outer2, sum_up, sum_down)
        sum_up, sum_down = g.hop(sum_up, ups), g.hop(sum_down, downs)
        begun2 = g.hop(outer2, outward)
        sums = added(keep, g.send(give, other_core)).reshape(g.qs, 2, cap, 2 * width)

        def along_x(rows):
            return jnp.stack([rows[:, 0], g.send(rows[:, 1], lambda z, x, q, c: (z, 1 - x, q, c))], axis=1)

        def along_q(rows):
            return jnp.stack(
                [rows[0]] + [g.send(rows[d], lambda z, x, q, c, d=d: (z, x, (q - d) % g.qs, c)) for d in range(1, g.qs)]
            )

        returned, back_rows = along_x(sums[..., :width]), along_q(sums[..., width:])
        grad = added(terms[0], tie(sum_up, sums), tie(sum_down, sums))
        begun2, grad = together((begun2, grad))
        middle2 = added(terms2[2], begun2)
        sum_up2, sum_down2 = g.hop(middle2, inward_up), g.hop(middle2, inward_down)
        returned, back_rows = along_q(returned), along_x(back_rows)
        sum_up2, sum_down2 = tie(sum_up2, grad), tie(sum_down2, grad)
        sum_up2, sum_down2 = added(terms2[1], sum_up2), added(terms2[3], sum_down2)
        grads = unspread(tie(grad, sum_up2, sum_down2))
        sum_up2, sum_down2 = g.hop(sum_up2, ups), g.hop(sum_down2, downs)
        mixed, d_tokens, d_probs = combine(returned.reshape(slots, width), back_rows.reshape(slots, width))
        sum_up2, sum_down2 = (tie(value, mixed, d_tokens, d_probs, *grads) for value in (sum_up2, sum_down2))
        grads += unspread(added(terms2[0], sum_up2, sum_down2))
        d_w_gate, d_w_up, d_w_down = unpack(pieces, place_x, grads, shuffle, *shapes)
    else:
        gate_cols, up_cols = dot(w_gate[0], shuffle).astype(BF), dot(w_up[0], shuffle).astype(BF)
        gate_up_shard = spread(
            jnp.concatenate([gate_cols[:, :half], up_cols[:, :half]], axis=1),
            jnp.concatenate([gate_cols[:, half:], up_cols[:, half:]], axis=1),
        )
        down_low, down_high = w_down[0, :part], w_down[0, part:]
        down_shard = spread(jnp.where(even, down_low, down_high), jnp.where(even, down_high, down_low))
        gate_up = jnp.concatenate(g.line(gate_up_shard), axis=0)
        down = jnp.concatenate(g.straight(g.line(down_shard)), axis=0)
        mine = exchange(sent, 1)
        inputs = jnp.concatenate([mine, g.send(mine, other_core)], axis=0)
        arrived, d_produced = inputs[:, :width], inputs[:, width:]
        pre = dot(arrived, gate_up)
        gate_pre, up_pre = pre[:, :half], pre[:, half:]
        sig = jax.nn.sigmoid(gate_pre)
        act = gate_pre * sig
        hidden = (act * up_pre).astype(BF)
        d_hidden = dot(d_produced, down, ((1,), (1,)))
        d_gate = (d_hidden * up_pre * sig * (1.0 + gate_pre * (1.0 - sig))).astype(BF)
        d_up = (d_hidden * act).astype(BF)
        d_both = jnp.concatenate([d_gate, d_up], axis=1)
        down_part = dot(hidden, d_produced, ((0,), (0,))).astype(BF)
        both_part = dot(arrived, d_both, ((0,), (0,))).astype(BF)
        partial = jnp.concatenate([dot(hidden, down), dot(d_both, gate_up, ((1,), (1,)))], axis=1).astype(BF)
        got = exchange(added(partial[:slots], g.send(partial[slots:], other_core)), -1)
        down_a, down_b = unspread(
            g.line_sum(
                lambda k: lax.dynamic_slice_in_dim(down_part, ((g.z + k) % g.zs) * (2 * part), 2 * part)
            )
        )
        d_w_down = jnp.where(
            even, jnp.concatenate([down_a, down_b], axis=0), jnp.concatenate([down_b, down_a], axis=0)
        ).astype(F32)
        both_a, both_b = unspread(g.line_sum(lambda k: both_part[k * line_width:(k + 1) * line_width]))
        d_w_gate, d_w_up = (
            dot(jnp.concatenate([both_a[:, cols], both_b[:, cols]], axis=1), shuffle, ((1,), (1,)))
            for cols in (slice(0, half), slice(half, None))
        )
        mixed, d_tokens, d_probs = combine(got[:, :width], got[:, width:])
    return (mixed, d_tokens, d_probs, d_w_gate[None], d_w_up[None], d_w_down[None])


def solution(mesh):
    rows = P(("dp", "expert"), None)
    weight = P("expert", "dp", None)
    return jax.shard_map(
        local,
        mesh=mesh,
        in_specs=(rows, rows, rows, weight, weight, weight, rows),
        out_specs=(rows, rows, rows, weight, weight, weight),
        check_vma=False,
    )
```

```python
import functools

import jax
import jax.numpy as jnp
from jax import lax
from jax.experimental import pallas as pl
from jax.experimental.pallas import tpu as pltpu
from jax.sharding import PartitionSpec as P

BF = jnp.bfloat16
F32 = jnp.float32
BOTH = ("dp", "expert")


def dot(a, b, dims=((1,), (0,))):
    return lax.dot_general(a, b, (dims, ((), ())), preferred_element_type=F32)


def tie(value, *others):
    return lax.optimization_barrier((value,) + others)[0]


def added(*terms):
    return sum(t.astype(F32) for t in terms).astype(BF)


class Grid:
    def __init__(self):
        self.dps, self.experts = lax.axis_size("dp"), lax.axis_size("expert")
        self.zs, self.qs = self.dps // 2, self.experts // 2
        dp, ex = lax.axis_index("dp"), lax.axis_index("expert")
        self.z, self.x, self.q, self.c = dp // 2, dp % 2, ex // 2, ex % 2

    def send(self, value, move):
        pairs = []
        for z in range(self.zs):
            for x in range(2):
                for q in range(self.qs):
                    for c in range(2):
                        to = move(z, x, q, c)
                        if to is not None:
                            pairs.append((self.flat(z, x, q, c), self.flat(*to)))
        return lax.ppermute(value, BOTH, pairs)

    def flat(self, z, x, q, c):
        return (z * 2 + x) * self.experts + q * 2 + c

    def hop(self, value, where):
        return self.send(value, lambda z, x, q, c: (where[z], x, q, c) if z in where else None)

    def line(self, shard):
        n = self.zs
        ups, downs = [shard], [shard]
        for s in range(1, n):
            ups.append(self.hop(ups[-1], {i: i + 1 for i in range(s - 1, n - 1)}))
            downs.append(self.hop(downs[-1], {i: i - 1 for i in range(1, n - s + 1)}))
        return [shard] + [jnp.where(self.z + s < n, downs[s], ups[n - s]) for s in range(1, n)]

    def straight(self, blocks):
        n = self.zs
        rows = []
        for j in range(n):
            row = blocks[j]
            for z in range(1, n):
                row = jnp.where(self.z == z, blocks[(j - z) % n], row)
            rows.append(row)
        return rows

    def line_sum(self, block):
        n = self.zs
        up, down = self.hop(block(n - 1), {0: 1}), self.hop(block(1), {n - 1: n - 2})
        for r in range(2, n):
            up = self.hop(added(block(n - r), up), {i: i + 1 for i in range(r)})
            down = self.hop(added(block(r), down), {i: i - 1 for i in range(n - r, n)})
        return added(block(0), up, down)


LANES = 256
MIB = 2**20


def shuffle_matrix(x, dps, hidden_width, pieces):
    block, half = hidden_width // dps, hidden_width // 2
    sources, start = [], 0
    for piece in pieces:
        unit = jnp.arange(piece * dps, dtype=jnp.int32)
        sources.append((unit // piece) * block + start + unit % piece)
        start += piece
    low = jnp.concatenate(sources)
    source = jnp.concatenate([low + x * (block // 2), low + (1 - x) * (block // 2)])
    return (jnp.arange(hidden_width, dtype=jnp.int32)[:, None] == source[None, :]).astype(BF)


def pack_kernel(pieces, x_ref, gate_ref, up_ref, down_ref, shuffle_ref, *outs):
    rows, hidden_width = gate_ref.shape
    half, block = hidden_width // 2, down_ref.shape[0]
    shuffle = shuffle_ref[...]
    gate, up = dot(gate_ref[...], shuffle).astype(BF), dot(up_ref[...], shuffle).astype(BF)
    x = x_ref[0]
    done = 0
    for number, piece in enumerate(pieces):
        units = piece * half // sum(pieces)
        count = 2 * units // LANES
        for side, start in ((0, x), (1, 1 - x)):
            ref = outs[2 * number + side]
            at = side * half + done * units // piece
            both = jnp.concatenate([gate[:, at:at + units], up[:, at:at + units]], axis=1)
            for i in range(count):
                ref[i * rows:(i + 1) * rows, :] = both[:, i * LANES:(i + 1) * LANES]
            source = pl.ds(pl.multiple_of(start * (block // 2) + done, 16), piece)
            for j in range(down_ref.shape[1] // LANES):
                to = count * rows + j * piece
                ref[to:to + piece, :] = down_ref[source, j * LANES:(j + 1) * LANES]
        done += piece


def unpack_kernel(pieces, x_ref, *refs):
    packed, (shuffle_ref, gate_ref, up_ref, down_ref) = refs[:-4], refs[-4:]
    rows, hidden_width = gate_ref.shape
    half, block = hidden_width // 2, down_ref.shape[0]
    x = x_ref[0]
    gates, ups = [[], []], [[], []]
    done = 0
    for number, piece in enumerate(pieces):
        units = piece * half // sum(pieces)
        count = 2 * units // LANES
        for side, start in ((0, x), (1, 1 - x)):
            ref = packed[2 * number + side]
            both = jnp.concatenate([ref[i * rows:(i + 1) * rows, :] for i in range(count)], axis=1)
            gates[side].append(both[:, :units])
            ups[side].append(both[:, units:])
            to = pl.ds(pl.multiple_of(start * (block // 2) + done, 16), piece)
            for j in range(down_ref.shape[1] // LANES):
                at = count * rows + j * piece
                down_ref[to, j * LANES:(j + 1) * LANES] = ref[at:at + piece, :].astype(F32)
        done += piece
    shuffle = shuffle_ref[...]
    gate_ref[...] = dot(jnp.concatenate(gates[0] + gates[1], axis=1), shuffle, ((1,), (1,)))
    up_ref[...] = dot(jnp.concatenate(ups[0] + ups[1], axis=1), shuffle, ((1,), (1,)))


def expert_kernel(z_ref, own, up, down, up_2, down_2, last, mine, theirs, *refs):
    gate_up, w_down, hidden, d_both, outer = refs[:5]
    terms, refs = refs[5:9], refs[9:]
    packed, x, grads, pre, d_hidden, d_down, load = refs
    places, size, _ = packed.shape
    rows, width = x.shape
    slots = rows // 2
    line = width // places
    part_rows = line // 2
    units = w_down.shape[0]
    piece = units // places // 2
    count, columns = 2 * units // LANES, width // LANES
    size_half = size // 2
    z = z_ref[0]

    loads = [
        pltpu.make_async_copy(a, b, load.at[places + n])
        for n, (a, b) in enumerate(
            (
                (mine.at[:, :width], x.at[:slots]),
                (theirs.at[:, :width], x.at[slots:]),
                (mine.at[:, width:], grads.at[:slots]),
                (theirs.at[:, width:], grads.at[slots:]),
            )
        )
    ]
    for copy in loads[:2]:
        copy.start()
    pltpu.make_async_copy(own, packed.at[0], load.at[0]).start()
    for s, is_one, one, other in (
        (1, z == places - 1, last, down),
        (2, z < 2, down_2, up_2),
        (3, z == 0, last, up),
    ):
        @pl.when(is_one)
        def _():
            pltpu.make_async_copy(one, packed.at[s], load.at[s]).start()

        @pl.when(jnp.logical_not(is_one))
        def _():
            pltpu.make_async_copy(other, packed.at[s], load.at[s]).start()

    for copy in loads[2:]:
        copy.start()

    def down_rows(k, h):
        return pl.ds(pl.multiple_of(lax.rem(z + k, places) * (2 * piece) + h * piece, 16), piece)

    for copy in loads[:2]:
        copy.wait()
    for s in range(places):
        pltpu.make_async_copy(own, packed.at[s], load.at[s]).wait()
        for h in range(2):
            for i in range(count):
                at = h * size_half + i * part_rows
                to = s * line + h * part_rows
                gate_up[to:to + part_rows, i * LANES:(i + 1) * LANES] = packed[s, at:at + part_rows, :]
            for j in range(columns):
                at = h * size_half + count * part_rows + j * piece
                w_down[down_rows(s, h), j * LANES:(j + 1) * LANES] = packed[s, at:at + piece, :]
        block = slice(s * line, (s + 1) * line)
        for i in range(count):
            cols = slice(i * LANES, (i + 1) * LANES)
            product = dot(x[:, block], gate_up[block, cols])
            pre[:, cols] = product if s == 0 else pre[:, cols] + product

    step = 64 if rows % 64 == 0 else 16

    def activate(r, _):
        at = pl.ds(pl.multiple_of(r * step, 16), step)
        gate_pre, up_pre = pre[at, :units], pre[at, units:]
        sig = 1.0 / (1.0 + jnp.exp(-gate_pre))
        act = gate_pre * sig
        hidden[at, :] = (act * up_pre).astype(BF)
        pre[at, :units] = up_pre * sig * (1.0 + gate_pre * (1.0 - sig))
        pre[at, units:] = act
        return 0

    lax.fori_loop(0, rows // step, activate, 0)
    for copy in loads[2:]:
        copy.wait()
    d_hidden[...] = dot(grads[...], w_down[...], ((1,), (1,)))

    def differentiate(r, _):
        at = pl.ds(pl.multiple_of(r * step, 16), step)
        d_h = d_hidden[at, :]
        d_both[at, :units] = (d_h * pre[at, :units]).astype(BF)
        d_both[at, units:] = (d_h * pre[at, units:]).astype(BF)
        return 0

    lax.fori_loop(0, rows // step, differentiate, 0)
    d_down[...] = dot(hidden[...], grads[...], ((0,), (0,))).astype(BF)

    for k, term in enumerate(terms):
        for h in range(2):
            from_cols = slice(k * line + h * part_rows, k * line + (h + 1) * part_rows)
            weights = dot(x[:, from_cols], d_both[...], ((0,), (0,))).astype(BF)
            for i in range(count):
                to = h * size_half + i * part_rows
                term[to:to + part_rows, :] = weights[:, i * LANES:(i + 1) * LANES]
            for j in range(columns):
                to = h * size_half + count * part_rows + j * piece
                term[to:to + piece, :] = d_down[down_rows(k, h), j * LANES:(j + 1) * LANES]

    @pl.when(z == 0)
    def _():
        outer[...] = terms[places - 1][...]

    @pl.when(z != 0)
    def _():
        outer[...] = terms[1][...]


def rows_kernel(chunks, *refs):
    keep, give = refs[-2:]
    slots = keep.shape[0]

    def add(pairs, dims):
        total = sum(dot(a[...], b[...], dims) for a, b in pairs).astype(BF)
        keep[...], give[...] = total[:slots], total[slots:]

    chunked = [refs[4 * n:4 * n + 4] for n in range(chunks)]

    @pl.when(pl.program_id(0) < pl.num_programs(0) // 2)
    def _():
        add([(hidden, w_down) for _, w_down, hidden, _ in chunked], ((1,), (0,)))

    @pl.when(pl.program_id(0) >= pl.num_programs(0) // 2)
    def _():
        add([(d_both, gate_up) for gate_up, _, _, d_both in chunked], ((1,), (1,)))


def in_vmem(count):
    return [pl.BlockSpec(memory_space=pltpu.VMEM)] * count


IN_SMEM = pl.BlockSpec(memory_space=pltpu.SMEM)


def pack(pieces, x, gate, up, down, shuffle):
    rows, hidden_width = gate.shape
    sizes = [(rows * hidden_width + down.size // 2) * piece // sum(pieces) // LANES for piece in pieces]
    return pl.pallas_call(
        functools.partial(pack_kernel, pieces),
        out_shape=[jax.ShapeDtypeStruct((size, LANES), BF) for size in sizes for _ in range(2)],
        in_specs=[IN_SMEM] + in_vmem(4),
        out_specs=in_vmem(2 * len(pieces)),
        compiler_params=pltpu.CompilerParams(vmem_limit_bytes=58 * MIB),
    )(x, gate, up, down, shuffle)


def unpack(pieces, x, packed, shuffle, gate_shape, down_shape):
    return pl.pallas_call(
        functools.partial(unpack_kernel, pieces),
        out_shape=[jax.ShapeDtypeStruct(shape, F32) for shape in (gate_shape, gate_shape, down_shape)],
        in_specs=[IN_SMEM] + in_vmem(len(packed) + 1),
        out_specs=in_vmem(3),
        compiler_params=pltpu.CompilerParams(vmem_limit_bytes=24 * MIB),
    )(x, *packed, shuffle)


def expert(z, places, units, weights, mine, theirs):
    size = weights[0].shape[0]
    slots, width = mine.shape[0], mine.shape[1] // 2
    rows = 2 * slots
    for_rows = [
        jax.ShapeDtypeStruct(shape, BF) for shape in ((width, 2 * units), (units, width), (rows, units), (rows, 2 * units))
    ]
    outs = pl.pallas_call(
        expert_kernel,
        out_shape=for_rows + [jax.ShapeDtypeStruct((size, LANES), BF)] * 5,
        in_specs=[IN_SMEM] + [pl.BlockSpec(memory_space=pl.ANY)] * 8,
        out_specs=in_vmem(9),
        scratch_shapes=[
            pltpu.VMEM((places, size, LANES), BF),
            pltpu.VMEM((rows, width), BF),
            pltpu.VMEM((rows, width), BF),
            pltpu.VMEM((rows, 2 * units), F32),
            pltpu.VMEM((rows, units), F32),
            pltpu.VMEM((units, width), BF),
            pltpu.SemaphoreType.DMA((places + 4,)),
        ],
        compiler_params=pltpu.CompilerParams(vmem_limit_bytes=24 * MIB),
        cost_estimate=pl.CostEstimate(
            flops=12 * rows * width * units, bytes_accessed=4 * 2**20, transcendentals=rows * units
        ),
    )(z, *weights, mine, theirs)
    return outs[:4], outs[4], outs[5:]


def token_rows(chunks, slots, width):
    tile = 2 * LANES
    tiles = width // tile
    in_specs = []
    for gate_up, w_down, hidden, d_both in chunks:
        in_specs += [
            pl.BlockSpec((tile, gate_up.shape[1]), lambda n: (jnp.maximum(n - tiles, 0), 0)),
            pl.BlockSpec((w_down.shape[0], tile), lambda n: (0, jnp.minimum(n, tiles - 1))),
            pl.BlockSpec(hidden.shape, lambda n: (0, 0)),
            pl.BlockSpec(d_both.shape, lambda n: (0, 0)),
        ]
    units = sum(chunk[1].shape[0] for chunk in chunks)
    return pl.pallas_call(
        functools.partial(rows_kernel, len(chunks)),
        grid=(2 * tiles,),
        out_shape=[jax.ShapeDtypeStruct((slots, 2 * width), BF)] * 2,
        in_specs=in_specs,
        out_specs=[pl.BlockSpec((slots, tile), lambda n: (0, n))] * 2,
        compiler_params=pltpu.CompilerParams(vmem_limit_bytes=24 * MIB),
        cost_estimate=pl.CostEstimate(
            flops=12 * slots * width * units, bytes_accessed=2 * 2**20, transcendentals=0
        ),
    )(*(array for chunk in chunks for array in chunk))


def local(tokens, expert_ids, gate_probs, w_gate, w_up, w_down, d_out):
    g = Grid()
    rows, topk = expert_ids.shape
    width = tokens.shape[1]
    hidden_width = w_gate.shape[2]
    half = hidden_width // 2
    experts = g.experts
    cap = rows * topk * 9 // (8 * experts)
    slots = experts * cap
    first = g.c == 0
    even = g.x == 0

    block = hidden_width // g.dps
    part = block // 2
    pieces = (2 * part // 3, part // 3)
    in_kernels = g.zs == 4 and slots % 16 == 0 and part % 48 == 0 and all(2 * p * g.dps % LANES == 0 for p in pieces)
    if not in_kernels:
        pieces = (part,)
    shuffle = shuffle_matrix(g.x, g.dps, hidden_width, pieces)

    def out_a(z, x, q, c):
        return z, c, q, x

    def out_b(z, x, q, c):
        return z, c, q, 1 - x

    def back_a(z, x, q, c):
        return z, c, q, x

    def back_b(z, x, q, c):
        return z, 1 - c, q, x

    def spread(part_a, part_b):
        got_a, got_b = g.send(part_a, out_a), g.send(part_b, out_b)
        return jnp.concatenate([jnp.where(first, got_a, got_b), jnp.where(first, got_b, got_a)], axis=0)

    def unspread(both):
        n = both.shape[0] // 2
        low, high = both[:n], both[n:]
        return g.send(jnp.where(first, low, high), back_a), g.send(jnp.where(first, high, low), back_b)

    expert_iota = jnp.arange(experts, dtype=jnp.int32)
    chosen = expert_ids[:, :, None] == expert_iota
    named = jnp.any(chosen, axis=1).astype(BF)
    token_iota = jnp.arange(rows, dtype=jnp.int32)
    earlier = (token_iota[:, None] > token_iota[None, :]).astype(BF)
    before = dot(earlier, named)
    slot = jnp.sum(jnp.where(chosen, before[:, None, :], 0.0), axis=2).astype(jnp.int32)
    relative = ((expert_ids // 2 - g.q + g.qs) % g.qs) * 2 + ((expert_ids % 2) ^ g.x)
    dest = relative * cap + slot
    slot_iota = jnp.arange(slots, dtype=jnp.int32)
    pair = dest[:, :, None] == slot_iota
    placing = jnp.any(pair, axis=1).astype(BF)
    weighted = jnp.sum(jnp.where(pair, gate_probs[:, :, None], 0.0), axis=1)
    slot_probs = jnp.sum(weighted, axis=0)

    def member(r, sign):
        def move(z, x, q, c):
            return z, x ^ (r % 2), (q + sign * (r // 2)) % g.qs, c

        return move

    def other_core(z, x, q, c):
        return z, x, q, 1 - c

    def exchange(value, sign):
        got = [value[:cap]] + [g.send(value[r * cap:(r + 1) * cap], member(r, sign)) for r in range(1, experts)]
        return jnp.concatenate(got, axis=0)

    line_width = width // g.zs
    turned = lax.dynamic_slice(jnp.concatenate([tokens, tokens], axis=1), (0, g.z * line_width), (rows, width))
    sent = jnp.concatenate(
        [
            dot(placing, turned, ((0,), (0,))).astype(BF),
            (slot_probs[:, None] * dot(placing, d_out, ((0,), (0,)))).astype(BF),
        ],
        axis=1,
    )
    def combine(returned, back_rows):
        high = lax.reduce_precision(weighted, 8, 7)
        mixed = (dot(high.astype(BF), returned) + dot((weighted - high).astype(BF), returned)).astype(BF)
        products = dot(d_out, returned, ((1,), (1,)))
        d_probs = jnp.sum(jnp.where(pair, products[:, None, :], 0.0), axis=2)
        d_turned = dot(placing, back_rows).astype(BF)
        d_tokens = lax.dynamic_slice(
            jnp.concatenate([d_turned, d_turned], axis=1), (0, (g.zs - g.z) * line_width), (rows, width)
        )
        return mixed, d_tokens, d_probs

    shapes = w_gate.shape[1:], w_down.shape[1:]
    together = lax.optimization_barrier
    if in_kernels:
        place_x, place_z = g.x.reshape(1).astype(jnp.int32), g.z.reshape(1).astype(jnp.int32)
        units = [piece * g.dps for piece in pieces]
        a, b, a2, b2 = pack(pieces, place_x, w_gate[0], w_up[0], w_down[0], shuffle)
        ups, downs, passing = {0: 1, 1: 2, 2: 3}, {1: 0, 2: 1, 3: 2}, {2: 3, 1: 0}
        outward, inward_up, inward_down = {0: 1, 3: 2}, {0: 1, 1: 2}, {3: 2, 2: 1}
        to_last = g.z == 2

        shard, a2, b2 = together((spread(a, b), a2, b2))
        up, down = g.hop(shard, ups), g.hop(shard, downs)
        shard2, sent = together((spread(a2, b2), sent))
        up, down = together((up, down))
        far = g.hop(jnp.where(g.z == 1, up, down), {1: 3, 2: 0})
        up_2, down_2 = g.hop(up, {1: 2, 2: 3}), g.hop(down, {1: 0, 2: 1})
        mine = tie(exchange(sent, 1), far, up_2, down_2)
        theirs = g.send(mine, other_core)
        shard2 = tie(shard2, mine)
        up2, down2 = g.hop(shard2, ups), g.hop(shard2, downs)
        chunk, outer, terms = expert(place_z, g.zs, units[0], (shard, up, down, up_2, down_2, far), mine, theirs)
        begun = g.hop(outer, outward)
        up2, down2 = tie(up2, outer), tie(down2, outer)
        up2_2, down2_2 = g.hop(up2, {1: 2, 2: 3}), g.hop(down2, {1: 0, 2: 1})
        passed = jnp.where(to_last, up2_2, down2_2)
        last2 = g.hop(passed, passing)
        middle = added(terms[2], tie(begun, passed))
        sum_up, sum_down = g.hop(middle, inward_up), g.hop(middle, inward_down)
        chunk2, outer2, terms2 = expert(
            place_z, g.zs, units[1], (shard2, up2, down2, up2_2, down2_2, tie(last2, middle)), mine, theirs
        )
        keep, give = token_rows((chunk, chunk2), slots, width)
        sum_up, sum_down = tie(sum_up, keep, give), tie(sum_down, keep, give)
        sum_up, sum_down = added(terms[1], sum_up), added(terms[3], sum_down)
        give, outer2 = tie(give, sum_up, sum_down), tie(outer2, sum_up, sum_down)
        sums = added(keep, g.send(give, other_core)).reshape(g.qs, 2, cap, 2 * width)
        sum_up, sum_down, sums = together((sum_up, sum_down, sums))
        sum_up, sum_down = g.hop(sum_up, ups), g.hop(sum_down, downs)
        begun2 = g.hop(outer2, outward)
        far_rows = g.send(sums[:, 1], lambda z, x, q, c: (z, 1 - x, q, c))
        grad = added(terms[0], sum_up, sum_down)
        begun2, grad = together((begun2, grad))
        middle2 = added(terms2[2], begun2)
        sum_up2, sum_down2 = g.hop(middle2, inward_up), g.hop(middle2, inward_down)
        near = jnp.stack([sums[:, 0], far_rows], axis=1)
        got = jnp.concatenate(
            [near[0]] + [g.send(near[d], lambda z, x, q, c, d=d: (z, x, (q - d) % g.qs, c)) for d in range(1, g.qs)]
        ).reshape(slots, 2 * width)
        sum_up2, sum_down2 = tie(sum_up2, grad), tie(sum_down2, grad)
        sum_up2, sum_down2 = added(terms2[1], sum_up2), added(terms2[3], sum_down2)
        grads = unspread(tie(grad, sum_up2, sum_down2))
        sum_up2, sum_down2 = g.hop(sum_up2, ups), g.hop(sum_down2, downs)
        mixed, d_tokens, d_probs = combine(got[:, :width], got[:, width:])
        sum_up2, sum_down2 = (tie(value, *grads) for value in (sum_up2, sum_down2))
        grads += unspread(added(terms2[0], sum_up2, sum_down2))
        d_w_gate, d_w_up, d_w_down = unpack(pieces, place_x, grads, shuffle, *shapes)
    else:
        gate_cols, up_cols = dot(w_gate[0], shuffle).astype(BF), dot(w_up[0], shuffle).astype(BF)
        gate_up_shard = spread(
            jnp.concatenate([gate_cols[:, :half], up_cols[:, :half]], axis=1),
            jnp.concatenate([gate_cols[:, half:], up_cols[:, half:]], axis=1),
        )
        down_low, down_high = w_down[0, :part], w_down[0, part:]
        down_shard = spread(jnp.where(even, down_low, down_high), jnp.where(even, down_high, down_low))
        gate_up = jnp.concatenate(g.line(gate_up_shard), axis=0)
        down = jnp.concatenate(g.straight(g.line(down_shard)), axis=0)
        mine = exchange(sent, 1)
        inputs = jnp.concatenate([mine, g.send(mine, other_core)], axis=0)
        arrived, d_produced = inputs[:, :width], inputs[:, width:]
        pre = dot(arrived, gate_up)
        gate_pre, up_pre = pre[:, :half], pre[:, half:]
        sig = jax.nn.sigmoid(gate_pre)
        act = gate_pre * sig
        hidden = (act * up_pre).astype(BF)
        d_hidden = dot(d_produced, down, ((1,), (1,)))
        d_gate = (d_hidden * up_pre * sig * (1.0 + gate_pre * (1.0 - sig))).astype(BF)
        d_up = (d_hidden * act).astype(BF)
        d_both = jnp.concatenate([d_gate, d_up], axis=1)
        down_part = dot(hidden, d_produced, ((0,), (0,))).astype(BF)
        both_part = dot(arrived, d_both, ((0,), (0,))).astype(BF)
        partial = jnp.concatenate([dot(hidden, down), dot(d_both, gate_up, ((1,), (1,)))], axis=1).astype(BF)
        got = exchange(added(partial[:slots], g.send(partial[slots:], other_core)), -1)
        down_a, down_b = unspread(
            g.line_sum(
                lambda k: lax.dynamic_slice_in_dim(down_part, ((g.z + k) % g.zs) * (2 * part), 2 * part)
            )
        )
        d_w_down = jnp.where(
            even, jnp.concatenate([down_a, down_b], axis=0), jnp.concatenate([down_b, down_a], axis=0)
        ).astype(F32)
        both_a, both_b = unspread(g.line_sum(lambda k: both_part[k * line_width:(k + 1) * line_width]))
        d_w_gate, d_w_up = (
            dot(jnp.concatenate([both_a[:, cols], both_b[:, cols]], axis=1), shuffle, ((1,), (1,)))
            for cols in (slice(0, half), slice(half, None))
        )
        mixed, d_tokens, d_probs = combine(got[:, :width], got[:, width:])
    return (mixed, d_tokens, d_probs, d_w_gate[None], d_w_up[None], d_w_down[None])


def solution(mesh):
    rows = P(("dp", "expert"), None)
    weight = P("expert", "dp", None)
    return jax.shard_map(
        local,
        mesh=mesh,
        in_specs=(rows, rows, rows, weight, weight, weight, rows),
        out_specs=(rows, rows, rows, weight, weight, weight),
        check_vma=False,
    )
```

```python
import functools

import jax
import jax.numpy as jnp
from jax import lax
from jax.experimental import pallas as pl
from jax.experimental.pallas import tpu as pltpu
from jax.sharding import PartitionSpec as P

BF = jnp.bfloat16
F32 = jnp.float32
BOTH = ("dp", "expert")


def dot(a, b, dims=((1,), (0,))):
    return lax.dot_general(a, b, (dims, ((), ())), preferred_element_type=F32)


def tie(value, *others):
    return lax.optimization_barrier((value,) + others)[0]


def tie_all(values, *others):
    return [tie(value, *others) for value in values]


def added(*terms):
    return sum(t.astype(F32) for t in terms).astype(BF)


class Grid:
    def __init__(self):
        self.dps, self.experts = lax.axis_size("dp"), lax.axis_size("expert")
        self.zs, self.qs = self.dps // 2, self.experts // 2
        dp, ex = lax.axis_index("dp"), lax.axis_index("expert")
        self.z, self.x, self.q, self.c = dp // 2, dp % 2, ex // 2, ex % 2

    def send(self, value, move):
        pairs = []
        for z in range(self.zs):
            for x in range(2):
                for q in range(self.qs):
                    for c in range(2):
                        to = move(z, x, q, c)
                        if to is not None:
                            pairs.append((self.flat(z, x, q, c), self.flat(*to)))
        return lax.ppermute(value, BOTH, pairs)

    def flat(self, z, x, q, c):
        return (z * 2 + x) * self.experts + q * 2 + c

    def hop(self, value, where):
        return self.send(value, lambda z, x, q, c: (where[z], x, q, c) if z in where else None)

    def line(self, shard):
        n = self.zs
        ups, downs = [shard], [shard]
        for s in range(1, n):
            ups.append(self.hop(ups[-1], {i: i + 1 for i in range(s - 1, n - 1)}))
            downs.append(self.hop(downs[-1], {i: i - 1 for i in range(1, n - s + 1)}))
        return [shard] + [jnp.where(self.z + s < n, downs[s], ups[n - s]) for s in range(1, n)]

    def straight(self, blocks):
        n = self.zs
        rows = []
        for j in range(n):
            row = blocks[j]
            for z in range(1, n):
                row = jnp.where(self.z == z, blocks[(j - z) % n], row)
            rows.append(row)
        return rows

    def line_sum(self, block):
        n = self.zs
        up, down = self.hop(block(n - 1), {0: 1}), self.hop(block(1), {n - 1: n - 2})
        for r in range(2, n):
            up = self.hop(added(block(n - r), up), {i: i + 1 for i in range(r)})
            down = self.hop(added(block(r), down), {i: i - 1 for i in range(n - r, n)})
        return added(block(0), up, down)


LANES = 256
MIB = 2**20


def shuffle_matrix(x, dps, hidden_width, pieces):
    block, half = hidden_width // dps, hidden_width // 2
    sources, start = [], 0
    for piece in pieces:
        unit = jnp.arange(piece * dps, dtype=jnp.int32)
        sources.append((unit // piece) * block + start + unit % piece)
        start += piece
    low = jnp.concatenate(sources)
    source = jnp.concatenate([low + x * (block // 2), low + (1 - x) * (block // 2)])
    return (jnp.arange(hidden_width, dtype=jnp.int32)[:, None] == source[None, :]).astype(BF)


def pack_kernel(pieces, x_ref, gate_ref, up_ref, down_ref, shuffle_ref, *outs):
    rows, hidden_width = gate_ref.shape
    half, block = hidden_width // 2, down_ref.shape[0]
    shuffle = shuffle_ref[...]
    gate, up = dot(gate_ref[...], shuffle).astype(BF), dot(up_ref[...], shuffle).astype(BF)
    x = x_ref[0]
    done = 0
    for number, piece in enumerate(pieces):
        units = piece * half // sum(pieces)
        count = 2 * units // LANES
        for side, start in ((0, x), (1, 1 - x)):
            ref = outs[2 * number + side]
            at = side * half + done * units // piece
            both = jnp.concatenate([gate[:, at:at + units], up[:, at:at + units]], axis=1)
            for i in range(count):
                ref[i * rows:(i + 1) * rows, :] = both[:, i * LANES:(i + 1) * LANES]
            source = pl.ds(pl.multiple_of(start * (block // 2) + done, 16), piece)
            for j in range(down_ref.shape[1] // LANES):
                to = count * rows + j * piece
                ref[to:to + piece, :] = down_ref[source, j * LANES:(j + 1) * LANES]
        done += piece


def unpack_kernel(pieces, x_ref, *refs):
    packed, (shuffle_ref, gate_ref, up_ref, down_ref) = refs[:-4], refs[-4:]
    rows, hidden_width = gate_ref.shape
    half, block = hidden_width // 2, down_ref.shape[0]
    x = x_ref[0]
    gates, ups = [[], []], [[], []]
    done = 0
    for number, piece in enumerate(pieces):
        units = piece * half // sum(pieces)
        count = 2 * units // LANES
        for side, start in ((0, x), (1, 1 - x)):
            ref = packed[2 * number + side]
            both = jnp.concatenate([ref[i * rows:(i + 1) * rows, :] for i in range(count)], axis=1)
            gates[side].append(both[:, :units])
            ups[side].append(both[:, units:])
            to = pl.ds(pl.multiple_of(start * (block // 2) + done, 16), piece)
            for j in range(down_ref.shape[1] // LANES):
                at = count * rows + j * piece
                down_ref[to, j * LANES:(j + 1) * LANES] = ref[at:at + piece, :].astype(F32)
        done += piece
    shuffle = shuffle_ref[...]
    gate_ref[...] = dot(jnp.concatenate(gates[0] + gates[1], axis=1), shuffle, ((1,), (1,)))
    up_ref[...] = dot(jnp.concatenate(ups[0] + ups[1], axis=1), shuffle, ((1,), (1,)))


def expert_kernel(z_ref, own, up, down, up_2, down_2, last, mine, theirs, *refs):
    weight_outs, (hidden_out, d_both_out, outer_out), outs, refs = refs[:2], refs[2:5], refs[5:9], refs[9:]
    packed, x, grads, gate_up, w_down, pre, d_hidden, hidden, d_both, d_down, terms, load, store = refs
    places, size, _ = packed.shape
    rows, width = x.shape
    slots = rows // 2
    line = width // places
    part_rows = line // 2
    units = w_down.shape[0]
    piece = units // places // 2
    count, columns = 2 * units // LANES, width // LANES
    size_half = size // 2
    z = z_ref[0]

    loads = [
        pltpu.make_async_copy(a, b, load.at[places + n])
        for n, (a, b) in enumerate(
            (
                (mine.at[:, :width], x.at[:slots]),
                (theirs.at[:, :width], x.at[slots:]),
                (mine.at[:, width:], grads.at[:slots]),
                (theirs.at[:, width:], grads.at[slots:]),
            )
        )
    ]
    for copy in loads[:2]:
        copy.start()
    pltpu.make_async_copy(own, packed.at[0], load.at[0]).start()
    for s, is_one, one, other in (
        (1, z == places - 1, last, down),
        (2, z < 2, down_2, up_2),
        (3, z == 0, last, up),
    ):
        @pl.when(is_one)
        def _():
            pltpu.make_async_copy(one, packed.at[s], load.at[s]).start()

        @pl.when(jnp.logical_not(is_one))
        def _():
            pltpu.make_async_copy(other, packed.at[s], load.at[s]).start()

    for copy in loads[2:]:
        copy.start()

    def down_rows(k, h):
        return pl.ds(pl.multiple_of(lax.rem(z + k, places) * (2 * piece) + h * piece, 16), piece)

    for copy in loads[:2]:
        copy.wait()
    for s in range(places):
        pltpu.make_async_copy(own, packed.at[s], load.at[s]).wait()
        for h in range(2):
            for i in range(count):
                at = h * size_half + i * part_rows
                to = s * line + h * part_rows
                gate_up[to:to + part_rows, i * LANES:(i + 1) * LANES] = packed[s, at:at + part_rows, :]
            for j in range(columns):
                at = h * size_half + count * part_rows + j * piece
                w_down[down_rows(s, h), j * LANES:(j + 1) * LANES] = packed[s, at:at + piece, :]
        block = slice(s * line, (s + 1) * line)
        for i in range(count):
            cols = slice(i * LANES, (i + 1) * LANES)
            product = dot(x[:, block], gate_up[block, cols])
            pre[:, cols] = product if s == 0 else pre[:, cols] + product

    stores = []

    def store_to(out, value):
        stores.append(pltpu.make_async_copy(value, out, store.at[len(stores)]))
        stores[-1].start()

    store_to(weight_outs[0], gate_up)
    store_to(weight_outs[1], w_down)
    step = 64 if rows % 64 == 0 else 16

    def activate(r, _):
        at = pl.ds(pl.multiple_of(r * step, 16), step)
        gate_pre, up_pre = pre[at, :units], pre[at, units:]
        sig = 1.0 / (1.0 + jnp.exp(-gate_pre))
        act = gate_pre * sig
        hidden[at, :] = (act * up_pre).astype(BF)
        pre[at, :units] = up_pre * sig * (1.0 + gate_pre * (1.0 - sig))
        pre[at, units:] = act
        return 0

    lax.fori_loop(0, rows // step, activate, 0)
    store_to(hidden_out, hidden)
    for copy in loads[2:]:
        copy.wait()
    d_hidden[...] = dot(grads[...], w_down[...], ((1,), (1,)))

    def differentiate(r, _):
        at = pl.ds(pl.multiple_of(r * step, 16), step)
        d_h = d_hidden[at, :]
        d_both[at, :units] = (d_h * pre[at, :units]).astype(BF)
        d_both[at, units:] = (d_h * pre[at, units:]).astype(BF)
        return 0

    lax.fori_loop(0, rows // step, differentiate, 0)
    store_to(d_both_out, d_both)
    d_down[...] = dot(hidden[...], grads[...], ((0,), (0,))).astype(BF)

    for k in (places - 1, 1, 2, 0):
        for h in range(2):
            from_cols = slice(k * line + h * part_rows, k * line + (h + 1) * part_rows)
            weights = dot(x[:, from_cols], d_both[...], ((0,), (0,))).astype(BF)
            for i in range(count):
                to = h * size_half + i * part_rows
                terms[k, to:to + part_rows, :] = weights[:, i * LANES:(i + 1) * LANES]
            for j in range(columns):
                to = h * size_half + count * part_rows + j * piece
                terms[k, to:to + piece, :] = d_down[down_rows(k, h), j * LANES:(j + 1) * LANES]
        store_to(outs[k], terms.at[k])
        if k == 1:
            store_to(outer_out, terms.at[jnp.where(z == 0, places - 1, 1)])
    for copy in stores:
        copy.wait()


def rows_kernel(chunks, *refs):
    keep, give = refs[-2:]
    slots = keep.shape[0]

    def add(pairs, dims):
        total = sum(dot(a[...], b[...], dims) for a, b in pairs).astype(BF)
        keep[...], give[...] = total[:slots], total[slots:]

    chunked = [refs[4 * n:4 * n + 4] for n in range(chunks)]

    @pl.when(pl.program_id(0) < pl.num_programs(0) // 2)
    def _():
        add([(hidden, w_down) for _, w_down, hidden, _ in chunked], ((1,), (0,)))

    @pl.when(pl.program_id(0) >= pl.num_programs(0) // 2)
    def _():
        add([(d_both, gate_up) for gate_up, _, _, d_both in chunked], ((1,), (1,)))


def in_vmem(count):
    return [pl.BlockSpec(memory_space=pltpu.VMEM)] * count


IN_SMEM = pl.BlockSpec(memory_space=pltpu.SMEM)


def pack(pieces, x, gate, up, down, shuffle):
    rows, hidden_width = gate.shape
    sizes = [(rows * hidden_width + down.size // 2) * piece // sum(pieces) // LANES for piece in pieces]
    return pl.pallas_call(
        functools.partial(pack_kernel, pieces),
        out_shape=[jax.ShapeDtypeStruct((size, LANES), BF) for size in sizes for _ in range(2)],
        in_specs=[IN_SMEM] + in_vmem(4),
        out_specs=in_vmem(2 * len(pieces)),
        compiler_params=pltpu.CompilerParams(vmem_limit_bytes=58 * MIB),
    )(x, gate, up, down, shuffle)


def unpack(pieces, x, packed, shuffle, gate_shape, down_shape):
    return pl.pallas_call(
        functools.partial(unpack_kernel, pieces),
        out_shape=[jax.ShapeDtypeStruct(shape, F32) for shape in (gate_shape, gate_shape, down_shape)],
        in_specs=[IN_SMEM] + in_vmem(len(packed) + 1),
        out_specs=in_vmem(3),
        compiler_params=pltpu.CompilerParams(vmem_limit_bytes=24 * MIB),
    )(x, *packed, shuffle)


def expert(z, places, units, weights, mine, theirs):
    size = weights[0].shape[0]
    slots, width = mine.shape[0], mine.shape[1] // 2
    rows = 2 * slots
    for_rows = [
        jax.ShapeDtypeStruct(shape, BF) for shape in ((width, 2 * units), (units, width), (rows, units), (rows, 2 * units))
    ]
    outs = pl.pallas_call(
        expert_kernel,
        out_shape=for_rows + [jax.ShapeDtypeStruct((size, LANES), BF)] * 5,
        in_specs=[IN_SMEM] + [pl.BlockSpec(memory_space=pl.ANY)] * 8,
        out_specs=[pl.BlockSpec(memory_space=pltpu.HBM)] * 9,
        scratch_shapes=[
            pltpu.VMEM((places, size, LANES), BF),
            pltpu.VMEM((rows, width), BF),
            pltpu.VMEM((rows, width), BF),
            pltpu.VMEM((width, 2 * units), BF),
            pltpu.VMEM((units, width), BF),
            pltpu.VMEM((rows, 2 * units), F32),
            pltpu.VMEM((rows, units), F32),
            pltpu.VMEM((rows, units), BF),
            pltpu.VMEM((rows, 2 * units), BF),
            pltpu.VMEM((units, width), BF),
            pltpu.VMEM((places, size, LANES), BF),
            pltpu.SemaphoreType.DMA((places + 4,)),
            pltpu.SemaphoreType.DMA((9,)),
        ],
        compiler_params=pltpu.CompilerParams(vmem_limit_bytes=24 * MIB),
        cost_estimate=pl.CostEstimate(
            flops=12 * rows * width * units, bytes_accessed=4 * 2**20, transcendentals=rows * units
        ),
    )(z, *weights, mine, theirs)
    return outs[:4], outs[4], outs[5:]


def token_rows(chunks, slots, width):
    tile = 2 * LANES
    tiles = width // tile
    in_specs = []
    for gate_up, w_down, hidden, d_both in chunks:
        in_specs += [
            pl.BlockSpec((tile, gate_up.shape[1]), lambda n: (jnp.maximum(n - tiles, 0), 0)),
            pl.BlockSpec((w_down.shape[0], tile), lambda n: (0, jnp.minimum(n, tiles - 1))),
            pl.BlockSpec(hidden.shape, lambda n: (0, 0)),
            pl.BlockSpec(d_both.shape, lambda n: (0, 0)),
        ]
    units = sum(chunk[1].shape[0] for chunk in chunks)
    return pl.pallas_call(
        functools.partial(rows_kernel, len(chunks)),
        grid=(2 * tiles,),
        out_shape=[jax.ShapeDtypeStruct((slots, 2 * width), BF)] * 2,
        in_specs=in_specs,
        out_specs=[pl.BlockSpec((slots, tile), lambda n: (0, n))] * 2,
        compiler_params=pltpu.CompilerParams(vmem_limit_bytes=24 * MIB),
        cost_estimate=pl.CostEstimate(
            flops=12 * slots * width * units, bytes_accessed=2 * 2**20, transcendentals=0
        ),
    )(*(array for chunk in chunks for array in chunk))


def local(tokens, expert_ids, gate_probs, w_gate, w_up, w_down, d_out):
    g = Grid()
    rows, topk = expert_ids.shape
    width = tokens.shape[1]
    hidden_width = w_gate.shape[2]
    half = hidden_width // 2
    experts = g.experts
    cap = rows * topk * 9 // (8 * experts)
    slots = experts * cap
    first = g.c == 0
    even = g.x == 0

    block = hidden_width // g.dps
    part = block // 2
    pieces = (2 * part // 3, part // 3)
    in_kernels = g.zs == 4 and slots % 16 == 0 and part % 48 == 0 and all(2 * p * g.dps % LANES == 0 for p in pieces)
    if not in_kernels:
        pieces = (part,)
    shuffle = shuffle_matrix(g.x, g.dps, hidden_width, pieces)

    def out_a(z, x, q, c):
        return z, c, q, x

    def out_b(z, x, q, c):
        return z, c, q, 1 - x

    def back_a(z, x, q, c):
        return z, c, q, x

    def back_b(z, x, q, c):
        return z, 1 - c, q, x

    def spread(part_a, part_b):
        got_a, got_b = g.send(part_a, out_a), g.send(part_b, out_b)
        return jnp.concatenate([jnp.where(first, got_a, got_b), jnp.where(first, got_b, got_a)], axis=0)

    def unspread(both):
        n = both.shape[0] // 2
        low, high = both[:n], both[n:]
        return g.send(jnp.where(first, low, high), back_a), g.send(jnp.where(first, high, low), back_b)

    expert_iota = jnp.arange(experts, dtype=jnp.int32)
    chosen = expert_ids[:, :, None] == expert_iota
    named = jnp.any(chosen, axis=1).astype(BF)
    token_iota = jnp.arange(rows, dtype=jnp.int32)
    earlier = (token_iota[:, None] > token_iota[None, :]).astype(BF)
    before = dot(earlier, named)
    slot = jnp.sum(jnp.where(chosen, before[:, None, :], 0.0), axis=2).astype(jnp.int32)
    relative = ((expert_ids // 2 - g.q + g.qs) % g.qs) * 2 + ((expert_ids % 2) ^ g.x)
    dest = relative * cap + slot
    slot_iota = jnp.arange(slots, dtype=jnp.int32)
    pair = dest[:, :, None] == slot_iota
    placing = jnp.any(pair, axis=1).astype(BF)
    weighted = jnp.sum(jnp.where(pair, gate_probs[:, :, None], 0.0), axis=1)
    slot_probs = jnp.sum(weighted, axis=0)

    def member(r, sign):
        def move(z, x, q, c):
            return z, x ^ (r % 2), (q + sign * (r // 2)) % g.qs, c

        return move

    def other_core(z, x, q, c):
        return z, x, q, 1 - c

    def exchange(value, sign):
        got = [value[:cap]] + [g.send(value[r * cap:(r + 1) * cap], member(r, sign)) for r in range(1, experts)]
        return jnp.concatenate(got, axis=0)

    line_width = width // g.zs
    turned = lax.dynamic_slice(jnp.concatenate([tokens, tokens], axis=1), (0, g.z * line_width), (rows, width))
    sent = jnp.concatenate(
        [
            dot(placing, turned, ((0,), (0,))).astype(BF),
            (slot_probs[:, None] * dot(placing, d_out, ((0,), (0,)))).astype(BF),
        ],
        axis=1,
    )
    def combine(returned, back_rows):
        high = lax.reduce_precision(weighted, 8, 7)
        mixed = (dot(high.astype(BF), returned) + dot((weighted - high).astype(BF), returned)).astype(BF)
        products = dot(d_out, returned, ((1,), (1,)))
        d_probs = jnp.sum(jnp.where(pair, products[:, None, :], 0.0), axis=2)
        d_turned = dot(placing, back_rows).astype(BF)
        d_tokens = lax.dynamic_slice(
            jnp.concatenate([d_turned, d_turned], axis=1), (0, (g.zs - g.z) * line_width), (rows, width)
        )
        return mixed, d_tokens, d_probs

    shapes = w_gate.shape[1:], w_down.shape[1:]
    together = lax.optimization_barrier
    if in_kernels:
        place_x, place_z = g.x.reshape(1).astype(jnp.int32), g.z.reshape(1).astype(jnp.int32)
        units = [piece * g.dps for piece in pieces]
        a, b, a2, b2 = pack(pieces, place_x, w_gate[0], w_up[0], w_down[0], shuffle)
        ups, downs, passing = {0: 1, 1: 2, 2: 3}, {1: 0, 2: 1, 3: 2}, {2: 3, 1: 0}
        outward, inward_up, inward_down = {0: 1, 3: 2}, {0: 1, 1: 2}, {3: 2, 2: 1}
        to_last = g.z == 2

        shard, a2, b2 = together((spread(a, b), a2, b2))
        up, down = g.hop(shard, ups), g.hop(shard, downs)
        shard2, sent = together((spread(a2, b2), sent))
        up, down = together((up, down))
        far = g.hop(jnp.where(g.z == 1, up, down), {1: 3, 2: 0})
        up_2, down_2 = g.hop(up, {1: 2, 2: 3}), g.hop(down, {1: 0, 2: 1})
        mine = tie(exchange(sent, 1), far, up_2, down_2)
        theirs = g.send(mine, other_core)
        shard2 = tie(shard2, mine)
        up2, down2 = g.hop(shard2, ups), g.hop(shard2, downs)
        chunk, outer, terms = expert(place_z, g.zs, units[0], (shard, up, down, up_2, down_2, far), mine, theirs)
        begun = g.hop(outer, outward)
        up2, down2 = tie(up2, outer), tie(down2, outer)
        up2_2, down2_2 = g.hop(up2, {1: 2, 2: 3}), g.hop(down2, {1: 0, 2: 1})
        passed = jnp.where(to_last, up2_2, down2_2)
        last2 = g.hop(passed, passing)
        middle = added(terms[2], tie(begun, passed))
        sum_up, sum_down = g.hop(middle, inward_up), g.hop(middle, inward_down)
        chunk2, outer2, terms2 = expert(
            place_z, g.zs, units[1], (shard2, up2, down2, up2_2, down2_2, tie(last2, middle)), mine, theirs
        )
        keep, give = token_rows((chunk, chunk2), slots, width)
        sum_up, sum_down = tie(sum_up, keep, give), tie(sum_down, keep, give)
        sum_up, sum_down = added(terms[1], sum_up), added(terms[3], sum_down)
        give, outer2 = tie(give, sum_up, sum_down), tie(outer2, sum_up, sum_down)
        sums = added(keep, g.send(give, other_core)).reshape(g.qs, 2, cap, 2 * width)
        sum_up, sum_down, sums = together((sum_up, sum_down, sums))
        sum_up, sum_down = g.hop(sum_up, ups), g.hop(sum_down, downs)
        begun2 = g.hop(outer2, outward)
        far_rows = g.send(sums[:, 1], lambda z, x, q, c: (z, 1 - x, q, c))
        grad = added(terms[0], sum_up, sum_down)
        begun2, grad = together((begun2, grad))
        middle2 = added(terms2[2], begun2)
        sum_up2, sum_down2 = g.hop(middle2, inward_up), g.hop(middle2, inward_down)
        near = jnp.stack([sums[:, 0], far_rows], axis=1)
        got = jnp.concatenate(
            [near[0]] + [g.send(near[d], lambda z, x, q, c, d=d: (z, x, (q - d) % g.qs, c)) for d in range(1, g.qs)]
        ).reshape(slots, 2 * width)
        sum_up2, sum_down2 = tie(sum_up2, grad), tie(sum_down2, grad)
        sum_up2, sum_down2 = added(terms2[1], sum_up2), added(terms2[3], sum_down2)
        grads = unspread(tie(grad, sum_up2, sum_down2))
        sum_up2, sum_down2 = g.hop(sum_up2, ups), g.hop(sum_down2, downs)
        mixed, d_tokens, d_probs = combine(got[:, :width], got[:, width:])
        grads = tie_all(grads, sum_up2, sum_down2)
        grads += tie_all(unspread(added(terms2[0], sum_up2, sum_down2)), mixed, d_tokens, d_probs)
        d_w_gate, d_w_up, d_w_down = unpack(pieces, place_x, grads, shuffle, *shapes)
    else:
        gate_cols, up_cols = dot(w_gate[0], shuffle).astype(BF), dot(w_up[0], shuffle).astype(BF)
        gate_up_shard = spread(
            jnp.concatenate([gate_cols[:, :half], up_cols[:, :half]], axis=1),
            jnp.concatenate([gate_cols[:, half:], up_cols[:, half:]], axis=1),
        )
        down_low, down_high = w_down[0, :part], w_down[0, part:]
        down_shard = spread(jnp.where(even, down_low, down_high), jnp.where(even, down_high, down_low))
        gate_up = jnp.concatenate(g.line(gate_up_shard), axis=0)
        down = jnp.concatenate(g.straight(g.line(down_shard)), axis=0)
        mine = exchange(sent, 1)
        inputs = jnp.concatenate([mine, g.send(mine, other_core)], axis=0)
        arrived, d_produced = inputs[:, :width], inputs[:, width:]
        pre = dot(arrived, gate_up)
        gate_pre, up_pre = pre[:, :half], pre[:, half:]
        sig = jax.nn.sigmoid(gate_pre)
        act = gate_pre * sig
        hidden = (act * up_pre).astype(BF)
        d_hidden = dot(d_produced, down, ((1,), (1,)))
        d_gate = (d_hidden * up_pre * sig * (1.0 + gate_pre * (1.0 - sig))).astype(BF)
        d_up = (d_hidden * act).astype(BF)
        d_both = jnp.concatenate([d_gate, d_up], axis=1)
        down_part = dot(hidden, d_produced, ((0,), (0,))).astype(BF)
        both_part = dot(arrived, d_both, ((0,), (0,))).astype(BF)
        partial = jnp.concatenate([dot(hidden, down), dot(d_both, gate_up, ((1,), (1,)))], axis=1).astype(BF)
        got = exchange(added(partial[:slots], g.send(partial[slots:], other_core)), -1)
        down_a, down_b = unspread(
            g.line_sum(
                lambda k: lax.dynamic_slice_in_dim(down_part, ((g.z + k) % g.zs) * (2 * part), 2 * part)
            )
        )
        d_w_down = jnp.where(
            even, jnp.concatenate([down_a, down_b], axis=0), jnp.concatenate([down_b, down_a], axis=0)
        ).astype(F32)
        both_a, both_b = unspread(g.line_sum(lambda k: both_part[k * line_width:(k + 1) * line_width]))
        d_w_gate, d_w_up = (
            dot(jnp.concatenate([both_a[:, cols], both_b[:, cols]], axis=1), shuffle, ((1,), (1,)))
            for cols in (slice(0, half), slice(half, None))
        )
        mixed, d_tokens, d_probs = combine(got[:, :width], got[:, width:])
    return (mixed, d_tokens, d_probs, d_w_gate[None], d_w_up[None], d_w_down[None])


def solution(mesh):
    rows = P(("dp", "expert"), None)
    weight = P("expert", "dp", None)
    return jax.shard_map(
        local,
        mesh=mesh,
        in_specs=(rows, rows, rows, weight, weight, weight, rows),
        out_specs=(rows, rows, rows, weight, weight, weight),
        check_vma=False,
    )
```

```python
import functools

import jax
import jax.numpy as jnp
from jax import lax
from jax.experimental import pallas as pl
from jax.experimental.pallas import tpu as pltpu
from jax.sharding import PartitionSpec as P

BF = jnp.bfloat16
F32 = jnp.float32
BOTH = ("dp", "expert")


def dot(a, b, dims=((1,), (0,))):
    return lax.dot_general(a, b, (dims, ((), ())), preferred_element_type=F32)


def tie(value, *others):
    return lax.optimization_barrier((value,) + others)[0]


def tie_all(values, *others):
    return [tie(value, *others) for value in values]


def added(*terms):
    return sum(t.astype(F32) for t in terms).astype(BF)


class Grid:
    def __init__(self):
        self.dps, self.experts = lax.axis_size("dp"), lax.axis_size("expert")
        self.zs, self.qs = self.dps // 2, self.experts // 2
        dp, ex = lax.axis_index("dp"), lax.axis_index("expert")
        self.z, self.x, self.q, self.c = dp // 2, dp % 2, ex // 2, ex % 2

    def send(self, value, move):
        pairs = []
        for z in range(self.zs):
            for x in range(2):
                for q in range(self.qs):
                    for c in range(2):
                        to = move(z, x, q, c)
                        if to is not None:
                            pairs.append((self.flat(z, x, q, c), self.flat(*to)))
        return lax.ppermute(value, BOTH, pairs)

    def flat(self, z, x, q, c):
        return (z * 2 + x) * self.experts + q * 2 + c

    def hop(self, value, where):
        return self.send(value, lambda z, x, q, c: (where[z], x, q, c) if z in where else None)

    def line(self, shard):
        n = self.zs
        ups, downs = [shard], [shard]
        for s in range(1, n):
            ups.append(self.hop(ups[-1], {i: i + 1 for i in range(s - 1, n - 1)}))
            downs.append(self.hop(downs[-1], {i: i - 1 for i in range(1, n - s + 1)}))
        return [shard] + [jnp.where(self.z + s < n, downs[s], ups[n - s]) for s in range(1, n)]

    def straight(self, blocks):
        n = self.zs
        rows = []
        for j in range(n):
            row = blocks[j]
            for z in range(1, n):
                row = jnp.where(self.z == z, blocks[(j - z) % n], row)
            rows.append(row)
        return rows

    def line_sum(self, block):
        n = self.zs
        up, down = self.hop(block(n - 1), {0: 1}), self.hop(block(1), {n - 1: n - 2})
        for r in range(2, n):
            up = self.hop(added(block(n - r), up), {i: i + 1 for i in range(r)})
            down = self.hop(added(block(r), down), {i: i - 1 for i in range(n - r, n)})
        return added(block(0), up, down)


LANES = 256
MIB = 2**20


def shuffle_matrix(x, dps, hidden_width, pieces):
    block, half = hidden_width // dps, hidden_width // 2
    sources, start = [], 0
    for piece in pieces:
        unit = jnp.arange(piece * dps, dtype=jnp.int32)
        sources.append((unit // piece) * block + start + unit % piece)
        start += piece
    low = jnp.concatenate(sources)
    source = jnp.concatenate([low + x * (block // 2), low + (1 - x) * (block // 2)])
    return (jnp.arange(hidden_width, dtype=jnp.int32)[:, None] == source[None, :]).astype(BF)


def pack_kernel(pieces, x_ref, gate_ref, up_ref, down_ref, shuffle_ref, *outs):
    rows, hidden_width = gate_ref.shape
    half, block = hidden_width // 2, down_ref.shape[0]
    shuffle = shuffle_ref[...]
    gate, up = dot(gate_ref[...], shuffle).astype(BF), dot(up_ref[...], shuffle).astype(BF)
    x = x_ref[0]
    done = 0
    for number, piece in enumerate(pieces):
        units = piece * half // sum(pieces)
        count = 2 * units // LANES
        for side, start in ((0, x), (1, 1 - x)):
            ref = outs[2 * number + side]
            at = side * half + done * units // piece
            both = jnp.concatenate([gate[:, at:at + units], up[:, at:at + units]], axis=1)
            for i in range(count):
                ref[i * rows:(i + 1) * rows, :] = both[:, i * LANES:(i + 1) * LANES]
            source = pl.ds(pl.multiple_of(start * (block // 2) + done, 16), piece)
            for j in range(down_ref.shape[1] // LANES):
                to = count * rows + j * piece
                ref[to:to + piece, :] = down_ref[source, j * LANES:(j + 1) * LANES]
        done += piece


def unpack_kernel(pieces, x_ref, *refs):
    packed, (shuffle_ref, gate_ref, up_ref, down_ref) = refs[:-4], refs[-4:]
    rows, hidden_width = gate_ref.shape
    half, block = hidden_width // 2, down_ref.shape[0]
    x = x_ref[0]
    gates, ups = [[], []], [[], []]
    done = 0
    for number, piece in enumerate(pieces):
        units = piece * half // sum(pieces)
        count = 2 * units // LANES
        for side, start in ((0, x), (1, 1 - x)):
            ref = packed[2 * number + side]
            both = jnp.concatenate([ref[i * rows:(i + 1) * rows, :] for i in range(count)], axis=1)
            gates[side].append(both[:, :units])
            ups[side].append(both[:, units:])
            to = pl.ds(pl.multiple_of(start * (block // 2) + done, 16), piece)
            for j in range(down_ref.shape[1] // LANES):
                at = count * rows + j * piece
                down_ref[to, j * LANES:(j + 1) * LANES] = ref[at:at + piece, :].astype(F32)
        done += piece
    shuffle = shuffle_ref[...]
    gate_ref[...] = dot(jnp.concatenate(gates[0] + gates[1], axis=1), shuffle, ((1,), (1,)))
    up_ref[...] = dot(jnp.concatenate(ups[0] + ups[1], axis=1), shuffle, ((1,), (1,)))


def expert_kernel(z_ref, own, up, down, up_2, down_2, last, mine, theirs, *refs):
    weight_outs, (hidden_out, d_both_out, outer_out), outs, refs = refs[:2], refs[2:5], refs[5:9], refs[9:]
    packed, x, grads, gate_up, w_down, pre, d_hidden, hidden, d_both, d_down, terms, load, store = refs
    places, size, _ = packed.shape
    rows, width = x.shape
    slots = rows // 2
    line = width // places
    part_rows = line // 2
    units = w_down.shape[0]
    piece = units // places // 2
    count, columns = 2 * units // LANES, width // LANES
    size_half = size // 2
    z = z_ref[0]

    loads = [
        pltpu.make_async_copy(a, b, load.at[places + n])
        for n, (a, b) in enumerate(
            (
                (mine.at[:, :width], x.at[:slots]),
                (theirs.at[:, :width], x.at[slots:]),
                (mine.at[:, width:], grads.at[:slots]),
                (theirs.at[:, width:], grads.at[slots:]),
            )
        )
    ]
    for copy in loads[:2]:
        copy.start()
    pltpu.make_async_copy(own, packed.at[0], load.at[0]).start()
    for s, is_one, one, other in (
        (1, z == places - 1, last, down),
        (2, z < 2, down_2, up_2),
        (3, z == 0, last, up),
    ):
        @pl.when(is_one)
        def _():
            pltpu.make_async_copy(one, packed.at[s], load.at[s]).start()

        @pl.when(jnp.logical_not(is_one))
        def _():
            pltpu.make_async_copy(other, packed.at[s], load.at[s]).start()

    for copy in loads[2:]:
        copy.start()

    def down_rows(k, h):
        return pl.ds(pl.multiple_of(lax.rem(z + k, places) * (2 * piece) + h * piece, 16), piece)

    for copy in loads[:2]:
        copy.wait()
    for s in range(places):
        pltpu.make_async_copy(own, packed.at[s], load.at[s]).wait()
        for h in range(2):
            for i in range(count):
                at = h * size_half + i * part_rows
                to = s * line + h * part_rows
                gate_up[to:to + part_rows, i * LANES:(i + 1) * LANES] = packed[s, at:at + part_rows, :]
            for j in range(columns):
                at = h * size_half + count * part_rows + j * piece
                w_down[down_rows(s, h), j * LANES:(j + 1) * LANES] = packed[s, at:at + piece, :]
        block = slice(s * line, (s + 1) * line)
        for i in range(count):
            cols = slice(i * LANES, (i + 1) * LANES)
            product = dot(x[:, block], gate_up[block, cols])
            pre[:, cols] = product if s == 0 else pre[:, cols] + product

    stores = []

    def store_to(out, value):
        stores.append(pltpu.make_async_copy(value, out, store.at[len(stores)]))
        stores[-1].start()

    store_to(weight_outs[0], gate_up)
    store_to(weight_outs[1], w_down)
    step = 64 if rows % 64 == 0 else 16

    def activate(r, _):
        at = pl.ds(pl.multiple_of(r * step, 16), step)
        gate_pre, up_pre = pre[at, :units], pre[at, units:]
        sig = 1.0 / (1.0 + jnp.exp(-gate_pre))
        act = gate_pre * sig
        hidden[at, :] = (act * up_pre).astype(BF)
        pre[at, :units] = up_pre * sig * (1.0 + gate_pre * (1.0 - sig))
        pre[at, units:] = act
        return 0

    lax.fori_loop(0, rows // step, activate, 0)
    store_to(hidden_out, hidden)
    for copy in loads[2:]:
        copy.wait()
    d_hidden[...] = dot(grads[...], w_down[...], ((1,), (1,)))

    def differentiate(r, _):
        at = pl.ds(pl.multiple_of(r * step, 16), step)
        d_h = d_hidden[at, :]
        d_both[at, :units] = (d_h * pre[at, :units]).astype(BF)
        d_both[at, units:] = (d_h * pre[at, units:]).astype(BF)
        return 0

    lax.fori_loop(0, rows // step, differentiate, 0)
    store_to(d_both_out, d_both)
    d_down[...] = dot(hidden[...], grads[...], ((0,), (0,))).astype(BF)

    for k in (places - 1, 1, 2, 0):
        for h in range(2):
            from_cols = slice(k * line + h * part_rows, k * line + (h + 1) * part_rows)
            weights = dot(x[:, from_cols], d_both[...], ((0,), (0,))).astype(BF)
            for i in range(count):
                to = h * size_half + i * part_rows
                terms[k, to:to + part_rows, :] = weights[:, i * LANES:(i + 1) * LANES]
            for j in range(columns):
                to = h * size_half + count * part_rows + j * piece
                terms[k, to:to + piece, :] = d_down[down_rows(k, h), j * LANES:(j + 1) * LANES]
        store_to(outs[k], terms.at[k])
        if k == 1:
            store_to(outer_out, terms.at[jnp.where(z == 0, places - 1, 1)])
    for copy in stores:
        copy.wait()


def rows_kernel(chunks, *refs):
    keep, give = refs[-2:]
    slots = keep.shape[0]

    def add(pairs, dims):
        total = sum(dot(a[...], b[...], dims) for a, b in pairs).astype(BF)
        keep[...], give[...] = total[:slots], total[slots:]

    chunked = [refs[4 * n:4 * n + 4] for n in range(chunks)]

    @pl.when(pl.program_id(0) < pl.num_programs(0) // 2)
    def _():
        add([(hidden, w_down) for _, w_down, hidden, _ in chunked], ((1,), (0,)))

    @pl.when(pl.program_id(0) >= pl.num_programs(0) // 2)
    def _():
        add([(d_both, gate_up) for gate_up, _, _, d_both in chunked], ((1,), (1,)))


def in_vmem(count):
    return [pl.BlockSpec(memory_space=pltpu.VMEM)] * count


IN_SMEM = pl.BlockSpec(memory_space=pltpu.SMEM)


def pack(pieces, x, gate, up, down, shuffle):
    rows, hidden_width = gate.shape
    sizes = [(rows * hidden_width + down.size // 2) * piece // sum(pieces) // LANES for piece in pieces]
    return pl.pallas_call(
        functools.partial(pack_kernel, pieces),
        out_shape=[jax.ShapeDtypeStruct((size, LANES), BF) for size in sizes for _ in range(2)],
        in_specs=[IN_SMEM] + in_vmem(4),
        out_specs=in_vmem(2 * len(pieces)),
        compiler_params=pltpu.CompilerParams(vmem_limit_bytes=58 * MIB),
    )(x, gate, up, down, shuffle)


def unpack(pieces, x, packed, shuffle, gate_shape, down_shape):
    return pl.pallas_call(
        functools.partial(unpack_kernel, pieces),
        out_shape=[jax.ShapeDtypeStruct(shape, F32) for shape in (gate_shape, gate_shape, down_shape)],
        in_specs=[IN_SMEM] + in_vmem(len(packed) + 1),
        out_specs=in_vmem(3),
        compiler_params=pltpu.CompilerParams(vmem_limit_bytes=24 * MIB),
    )(x, *packed, shuffle)


def expert(z, places, units, weights, mine, theirs, vmem):
    size = weights[0].shape[0]
    slots, width = mine.shape[0], mine.shape[1] // 2
    rows = 2 * slots
    for_rows = [
        jax.ShapeDtypeStruct(shape, BF) for shape in ((width, 2 * units), (units, width), (rows, units), (rows, 2 * units))
    ]
    outs = pl.pallas_call(
        expert_kernel,
        out_shape=for_rows + [jax.ShapeDtypeStruct((size, LANES), BF)] * 5,
        in_specs=[IN_SMEM] + [pl.BlockSpec(memory_space=pl.ANY)] * 8,
        out_specs=[pl.BlockSpec(memory_space=pltpu.HBM)] * 9,
        scratch_shapes=[
            pltpu.VMEM((places, size, LANES), BF),
            pltpu.VMEM((rows, width), BF),
            pltpu.VMEM((rows, width), BF),
            pltpu.VMEM((width, 2 * units), BF),
            pltpu.VMEM((units, width), BF),
            pltpu.VMEM((rows, 2 * units), F32),
            pltpu.VMEM((rows, units), F32),
            pltpu.VMEM((rows, units), BF),
            pltpu.VMEM((rows, 2 * units), BF),
            pltpu.VMEM((units, width), BF),
            pltpu.VMEM((places, size, LANES), BF),
            pltpu.SemaphoreType.DMA((places + 4,)),
            pltpu.SemaphoreType.DMA((9,)),
        ],
        compiler_params=pltpu.CompilerParams(vmem_limit_bytes=vmem),
        cost_estimate=pl.CostEstimate(
            flops=12 * rows * width * units, bytes_accessed=4 * 2**20, transcendentals=rows * units
        ),
    )(z, *weights, mine, theirs)
    return outs[:4], outs[4], outs[5:]


def token_rows(chunks, slots, width):
    tile = 2 * LANES
    tiles = width // tile
    in_specs = []
    for gate_up, w_down, hidden, d_both in chunks:
        in_specs += [
            pl.BlockSpec((tile, gate_up.shape[1]), lambda n: (jnp.maximum(n - tiles, 0), 0)),
            pl.BlockSpec((w_down.shape[0], tile), lambda n: (0, jnp.minimum(n, tiles - 1))),
            pl.BlockSpec(hidden.shape, lambda n: (0, 0)),
            pl.BlockSpec(d_both.shape, lambda n: (0, 0)),
        ]
    units = sum(chunk[1].shape[0] for chunk in chunks)
    return pl.pallas_call(
        functools.partial(rows_kernel, len(chunks)),
        grid=(2 * tiles,),
        out_shape=[jax.ShapeDtypeStruct((slots, 2 * width), BF)] * 2,
        in_specs=in_specs,
        out_specs=[pl.BlockSpec((slots, tile), lambda n: (0, n))] * 2,
        compiler_params=pltpu.CompilerParams(vmem_limit_bytes=24 * MIB),
        cost_estimate=pl.CostEstimate(
            flops=12 * slots * width * units, bytes_accessed=2 * 2**20, transcendentals=0
        ),
    )(*(array for chunk in chunks for array in chunk))


def local(tokens, expert_ids, gate_probs, w_gate, w_up, w_down, d_out):
    g = Grid()
    rows, topk = expert_ids.shape
    width = tokens.shape[1]
    hidden_width = w_gate.shape[2]
    half = hidden_width // 2
    experts = g.experts
    cap = rows * topk * 9 // (8 * experts)
    slots = experts * cap
    first = g.c == 0
    even = g.x == 0

    block = hidden_width // g.dps
    part = block // 2
    pieces = (2 * part // 3, part // 3)
    in_kernels = g.zs == 4 and slots % 16 == 0 and part % 48 == 0 and all(2 * p * g.dps % LANES == 0 for p in pieces)
    if not in_kernels:
        pieces = (part,)
    shuffle = shuffle_matrix(g.x, g.dps, hidden_width, pieces)

    def out_a(z, x, q, c):
        return z, c, q, x

    def out_b(z, x, q, c):
        return z, c, q, 1 - x

    def back_a(z, x, q, c):
        return z, c, q, x

    def back_b(z, x, q, c):
        return z, 1 - c, q, x

    def spread(part_a, part_b):
        got_a, got_b = g.send(part_a, out_a), g.send(part_b, out_b)
        return jnp.concatenate([jnp.where(first, got_a, got_b), jnp.where(first, got_b, got_a)], axis=0)

    def unspread(both):
        n = both.shape[0] // 2
        low, high = both[:n], both[n:]
        return g.send(jnp.where(first, low, high), back_a), g.send(jnp.where(first, high, low), back_b)

    expert_iota = jnp.arange(experts, dtype=jnp.int32)
    chosen = expert_ids[:, :, None] == expert_iota
    named = jnp.any(chosen, axis=1).astype(BF)
    token_iota = jnp.arange(rows, dtype=jnp.int32)
    earlier = (token_iota[:, None] > token_iota[None, :]).astype(BF)
    before = dot(earlier, named)
    slot = jnp.sum(jnp.where(chosen, before[:, None, :], 0.0), axis=2).astype(jnp.int32)
    relative = ((expert_ids // 2 - g.q + g.qs) % g.qs) * 2 + ((expert_ids % 2) ^ g.x)
    dest = relative * cap + slot
    slot_iota = jnp.arange(slots, dtype=jnp.int32)
    pair = dest[:, :, None] == slot_iota
    placing = jnp.any(pair, axis=1).astype(BF)
    weighted = jnp.sum(jnp.where(pair, gate_probs[:, :, None], 0.0), axis=1)
    slot_probs = jnp.sum(weighted, axis=0)

    def member(r, sign):
        def move(z, x, q, c):
            return z, x ^ (r % 2), (q + sign * (r // 2)) % g.qs, c

        return move

    def other_core(z, x, q, c):
        return z, x, q, 1 - c

    def exchange(value, sign):
        got = [value[:cap]] + [g.send(value[r * cap:(r + 1) * cap], member(r, sign)) for r in range(1, experts)]
        return jnp.concatenate(got, axis=0)

    line_width = width // g.zs
    turned = lax.dynamic_slice(jnp.concatenate([tokens, tokens], axis=1), (0, g.z * line_width), (rows, width))
    sent = jnp.concatenate(
        [
            dot(placing, turned, ((0,), (0,))).astype(BF),
            (slot_probs[:, None] * dot(placing, d_out, ((0,), (0,)))).astype(BF),
        ],
        axis=1,
    )
    def combine(returned, back_rows):
        high = lax.reduce_precision(weighted, 8, 7)
        mixed = (dot(high.astype(BF), returned) + dot((weighted - high).astype(BF), returned)).astype(BF)
        products = dot(d_out, returned, ((1,), (1,)))
        d_probs = jnp.sum(jnp.where(pair, products[:, None, :], 0.0), axis=2)
        d_turned = dot(placing, back_rows).astype(BF)
        d_tokens = lax.dynamic_slice(
            jnp.concatenate([d_turned, d_turned], axis=1), (0, (g.zs - g.z) * line_width), (rows, width)
        )
        return mixed, d_tokens, d_probs

    shapes = w_gate.shape[1:], w_down.shape[1:]
    together = lax.optimization_barrier
    if in_kernels:
        place_x, place_z = g.x.reshape(1).astype(jnp.int32), g.z.reshape(1).astype(jnp.int32)
        units = [piece * g.dps for piece in pieces]
        a, b, a2, b2 = pack(pieces, place_x, w_gate[0], w_up[0], w_down[0], shuffle)
        ups, downs, passing = {0: 1, 1: 2, 2: 3}, {1: 0, 2: 1, 3: 2}, {2: 3, 1: 0}
        outward, inward_up, inward_down = {0: 1, 3: 2}, {0: 1, 1: 2}, {3: 2, 2: 1}
        to_last = g.z == 2

        shard, a2, b2 = together((spread(a, b), a2, b2))
        up, down = g.hop(shard, ups), g.hop(shard, downs)
        shard2, sent = together((spread(a2, b2), sent))
        up, down = together((up, down))
        far = g.hop(jnp.where(g.z == 1, up, down), {1: 3, 2: 0})
        up_2, down_2 = g.hop(up, {1: 2, 2: 3}), g.hop(down, {1: 0, 2: 1})
        mine = tie(exchange(sent, 1), far, up_2, down_2)
        theirs = g.send(mine, other_core)
        shard2 = tie(shard2, mine)
        up2, down2 = g.hop(shard2, ups), g.hop(shard2, downs)
        chunk, outer, terms = expert(place_z, g.zs, units[0], (shard, up, down, up_2, down_2, far), mine, theirs, 52 * MIB)
        begun = g.hop(outer, outward)
        up2, down2 = tie(up2, outer), tie(down2, outer)
        up2_2, down2_2 = g.hop(up2, {1: 2, 2: 3}), g.hop(down2, {1: 0, 2: 1})
        passed = jnp.where(to_last, up2_2, down2_2)
        last2 = g.hop(passed, passing)
        middle = added(terms[2], tie(begun, passed))
        sum_up, sum_down = g.hop(middle, inward_up), g.hop(middle, inward_down)
        chunk2, outer2, terms2 = expert(
            place_z, g.zs, units[1], (shard2, up2, down2, up2_2, down2_2, tie(last2, middle)), mine, theirs, 24 * MIB
        )
        keep, give = token_rows((chunk, chunk2), slots, width)
        sum_up, sum_down = tie(sum_up, keep, give), tie(sum_down, keep, give)
        sum_up, sum_down = added(terms[1], sum_up), added(terms[3], sum_down)
        give, outer2 = tie(give, sum_up, sum_down), tie(outer2, sum_up, sum_down)
        sums = added(keep, g.send(give, other_core)).reshape(g.qs, 2, cap, 2 * width)
        sum_up, sum_down, sums = together((sum_up, sum_down, sums))
        sum_up, sum_down = g.hop(sum_up, ups), g.hop(sum_down, downs)
        begun2 = g.hop(outer2, outward)
        far_rows = g.send(sums[:, 1], lambda z, x, q, c: (z, 1 - x, q, c))
        grad = added(terms[0], sum_up, sum_down)
        begun2, grad = together((begun2, grad))
        middle2 = added(terms2[2], begun2)
        sum_up2, sum_down2 = g.hop(middle2, inward_up), g.hop(middle2, inward_down)
        near = jnp.stack([sums[:, 0], far_rows], axis=1)
        got = jnp.concatenate(
            [near[0]] + [g.send(near[d], lambda z, x, q, c, d=d: (z, x, (q - d) % g.qs, c)) for d in range(1, g.qs)]
        ).reshape(slots, 2 * width)
        sum_up2, sum_down2 = tie(sum_up2, grad), tie(sum_down2, grad)
        sum_up2, sum_down2 = added(terms2[1], sum_up2), added(terms2[3], sum_down2)
        grads = unspread(tie(grad, sum_up2, sum_down2))
        sum_up2, sum_down2 = g.hop(sum_up2, ups), g.hop(sum_down2, downs)
        mixed, d_tokens, d_probs = combine(got[:, :width], got[:, width:])
        grads = tie_all(grads, sum_up2, sum_down2)
        grads += tie_all(unspread(added(terms2[0], sum_up2, sum_down2)), mixed, d_tokens, d_probs)
        d_w_gate, d_w_up, d_w_down = unpack(pieces, place_x, grads, shuffle, *shapes)
    else:
        gate_cols, up_cols = dot(w_gate[0], shuffle).astype(BF), dot(w_up[0], shuffle).astype(BF)
        gate_up_shard = spread(
            jnp.concatenate([gate_cols[:, :half], up_cols[:, :half]], axis=1),
            jnp.concatenate([gate_cols[:, half:], up_cols[:, half:]], axis=1),
        )
        down_low, down_high = w_down[0, :part], w_down[0, part:]
        down_shard = spread(jnp.where(even, down_low, down_high), jnp.where(even, down_high, down_low))
        gate_up = jnp.concatenate(g.line(gate_up_shard), axis=0)
        down = jnp.concatenate(g.straight(g.line(down_shard)), axis=0)
        mine = exchange(sent, 1)
        inputs = jnp.concatenate([mine, g.send(mine, other_core)], axis=0)
        arrived, d_produced = inputs[:, :width], inputs[:, width:]
        pre = dot(arrived, gate_up)
        gate_pre, up_pre = pre[:, :half], pre[:, half:]
        sig = jax.nn.sigmoid(gate_pre)
        act = gate_pre * sig
        hidden = (act * up_pre).astype(BF)
        d_hidden = dot(d_produced, down, ((1,), (1,)))
        d_gate = (d_hidden * up_pre * sig * (1.0 + gate_pre * (1.0 - sig))).astype(BF)
        d_up = (d_hidden * act).astype(BF)
        d_both = jnp.concatenate([d_gate, d_up], axis=1)
        down_part = dot(hidden, d_produced, ((0,), (0,))).astype(BF)
        both_part = dot(arrived, d_both, ((0,), (0,))).astype(BF)
        partial = jnp.concatenate([dot(hidden, down), dot(d_both, gate_up, ((1,), (1,)))], axis=1).astype(BF)
        got = exchange(added(partial[:slots], g.send(partial[slots:], other_core)), -1)
        down_a, down_b = unspread(
            g.line_sum(
                lambda k: lax.dynamic_slice_in_dim(down_part, ((g.z + k) % g.zs) * (2 * part), 2 * part)
            )
        )
        d_w_down = jnp.where(
            even, jnp.concatenate([down_a, down_b], axis=0), jnp.concatenate([down_b, down_a], axis=0)
        ).astype(F32)
        both_a, both_b = unspread(g.line_sum(lambda k: both_part[k * line_width:(k + 1) * line_width]))
        d_w_gate, d_w_up = (
            dot(jnp.concatenate([both_a[:, cols], both_b[:, cols]], axis=1), shuffle, ((1,), (1,)))
            for cols in (slice(0, half), slice(half, None))
        )
        mixed, d_tokens, d_probs = combine(got[:, :width], got[:, width:])
    return (mixed, d_tokens, d_probs, d_w_gate[None], d_w_up[None], d_w_down[None])


def solution(mesh):
    rows = P(("dp", "expert"), None)
    weight = P("expert", "dp", None)
    return jax.shard_map(
        local,
        mesh=mesh,
        in_specs=(rows, rows, rows, weight, weight, weight, rows),
        out_specs=(rows, rows, rows, weight, weight, weight),
        check_vma=False,
    )
```

```python
import functools

import jax
import jax.numpy as jnp
from jax import lax
from jax.experimental import pallas as pl
from jax.experimental.pallas import tpu as pltpu
from jax.sharding import PartitionSpec as P

BF = jnp.bfloat16
F32 = jnp.float32
BOTH = ("dp", "expert")


def dot(a, b, dims=((1,), (0,))):
    return lax.dot_general(a, b, (dims, ((), ())), preferred_element_type=F32)


def tie(value, *others):
    return lax.optimization_barrier((value,) + others)[0]


def tie_all(values, *others):
    return [tie(value, *others) for value in values]


def added(*terms):
    return sum(t.astype(F32) for t in terms).astype(BF)


class Grid:
    def __init__(self):
        self.dps, self.experts = lax.axis_size("dp"), lax.axis_size("expert")
        self.zs, self.qs = self.dps // 2, self.experts // 2
        dp, ex = lax.axis_index("dp"), lax.axis_index("expert")
        self.z, self.x, self.q, self.c = dp // 2, dp % 2, ex // 2, ex % 2

    def send(self, value, move):
        pairs = []
        for z in range(self.zs):
            for x in range(2):
                for q in range(self.qs):
                    for c in range(2):
                        to = move(z, x, q, c)
                        if to is not None:
                            pairs.append((self.flat(z, x, q, c), self.flat(*to)))
        return lax.ppermute(value, BOTH, pairs)

    def flat(self, z, x, q, c):
        return (z * 2 + x) * self.experts + q * 2 + c

    def hop(self, value, where):
        return self.send(value, lambda z, x, q, c: (where[z], x, q, c) if z in where else None)

    def line(self, shard):
        n = self.zs
        ups, downs = [shard], [shard]
        for s in range(1, n):
            ups.append(self.hop(ups[-1], {i: i + 1 for i in range(s - 1, n - 1)}))
            downs.append(self.hop(downs[-1], {i: i - 1 for i in range(1, n - s + 1)}))
        return [shard] + [jnp.where(self.z + s < n, downs[s], ups[n - s]) for s in range(1, n)]

    def straight(self, blocks):
        n = self.zs
        rows = []
        for j in range(n):
            row = blocks[j]
            for z in range(1, n):
                row = jnp.where(self.z == z, blocks[(j - z) % n], row)
            rows.append(row)
        return rows

    def line_sum(self, block):
        n = self.zs
        up, down = self.hop(block(n - 1), {0: 1}), self.hop(block(1), {n - 1: n - 2})
        for r in range(2, n):
            up = self.hop(added(block(n - r), up), {i: i + 1 for i in range(r)})
            down = self.hop(added(block(r), down), {i: i - 1 for i in range(n - r, n)})
        return added(block(0), up, down)


LANES = 256
MIB = 2**20


def shuffle_matrix(x, dps, hidden_width, pieces):
    block, half = hidden_width // dps, hidden_width // 2
    sources, start = [], 0
    for piece in pieces:
        unit = jnp.arange(piece * dps, dtype=jnp.int32)
        sources.append((unit // piece) * block + start + unit % piece)
        start += piece
    low = jnp.concatenate(sources)
    source = jnp.concatenate([low + x * (block // 2), low + (1 - x) * (block // 2)])
    return (jnp.arange(hidden_width, dtype=jnp.int32)[:, None] == source[None, :]).astype(BF)


def pack_kernel(pieces, x_ref, gate_ref, up_ref, down_ref, shuffle_ref, *outs):
    rows, hidden_width = gate_ref.shape
    half, block = hidden_width // 2, down_ref.shape[0]
    shuffle = shuffle_ref[...]
    gate, up = dot(gate_ref[...], shuffle).astype(BF), dot(up_ref[...], shuffle).astype(BF)
    x = x_ref[0]
    done = 0
    for number, piece in enumerate(pieces):
        units = piece * half // sum(pieces)
        count = 2 * units // LANES
        for side, start in ((0, x), (1, 1 - x)):
            ref = outs[2 * number + side]
            at = side * half + done * units // piece
            both = jnp.concatenate([gate[:, at:at + units], up[:, at:at + units]], axis=1)
            for i in range(count):
                ref[i * rows:(i + 1) * rows, :] = both[:, i * LANES:(i + 1) * LANES]
            source = pl.ds(pl.multiple_of(start * (block // 2) + done, 16), piece)
            for j in range(down_ref.shape[1] // LANES):
                to = count * rows + j * piece
                ref[to:to + piece, :] = down_ref[source, j * LANES:(j + 1) * LANES]
        done += piece


def unpack_kernel(pieces, x_ref, *refs):
    packed, (shuffle_ref, gate_ref, up_ref, down_ref) = refs[:-4], refs[-4:]
    rows, hidden_width = gate_ref.shape
    half, block = hidden_width // 2, down_ref.shape[0]
    x = x_ref[0]
    gates, ups = [[], []], [[], []]
    done = 0
    for number, piece in enumerate(pieces):
        units = piece * half // sum(pieces)
        count = 2 * units // LANES
        for side, start in ((0, x), (1, 1 - x)):
            ref = packed[2 * number + side]
            both = jnp.concatenate([ref[i * rows:(i + 1) * rows, :] for i in range(count)], axis=1)
            gates[side].append(both[:, :units])
            ups[side].append(both[:, units:])
            to = pl.ds(pl.multiple_of(start * (block // 2) + done, 16), piece)
            for j in range(down_ref.shape[1] // LANES):
                at = count * rows + j * piece
                down_ref[to, j * LANES:(j + 1) * LANES] = ref[at:at + piece, :].astype(F32)
        done += piece
    shuffle = shuffle_ref[...]
    gate_ref[...] = dot(jnp.concatenate(gates[0] + gates[1], axis=1), shuffle, ((1,), (1,)))
    up_ref[...] = dot(jnp.concatenate(ups[0] + ups[1], axis=1), shuffle, ((1,), (1,)))


def expert_kernel(z_ref, own, up, down, up_2, down_2, last, mine, theirs, *refs):
    weight_outs, (hidden_out, d_both_out, outer_out), outs, refs = refs[:2], refs[2:5], refs[5:9], refs[9:]
    packed, x, grads, gate_up, w_down, pre, d_hidden, hidden, d_both, d_down, terms, load, store = refs
    places, size, _ = packed.shape
    rows, width = x.shape
    slots = rows // 2
    line = width // places
    part_rows = line // 2
    units = w_down.shape[0]
    piece = units // places // 2
    count, columns = 2 * units // LANES, width // LANES
    size_half = size // 2
    z = z_ref[0]

    loads = [
        pltpu.make_async_copy(a, b, load.at[places + n])
        for n, (a, b) in enumerate(
            (
                (mine.at[:, :width], x.at[:slots]),
                (theirs.at[:, :width], x.at[slots:]),
                (mine.at[:, width:], grads.at[:slots]),
                (theirs.at[:, width:], grads.at[slots:]),
            )
        )
    ]
    for copy in loads[:2]:
        copy.start()
    pltpu.make_async_copy(own, packed.at[0], load.at[0]).start()
    for s, is_one, one, other in (
        (1, z == places - 1, last, down),
        (2, z < 2, down_2, up_2),
        (3, z == 0, last, up),
    ):
        @pl.when(is_one)
        def _():
            pltpu.make_async_copy(one, packed.at[s], load.at[s]).start()

        @pl.when(jnp.logical_not(is_one))
        def _():
            pltpu.make_async_copy(other, packed.at[s], load.at[s]).start()

    for copy in loads[2:]:
        copy.start()

    def down_rows(k, h):
        return pl.ds(pl.multiple_of(lax.rem(z + k, places) * (2 * piece) + h * piece, 16), piece)

    for copy in loads[:2]:
        copy.wait()
    for s in range(places):
        pltpu.make_async_copy(own, packed.at[s], load.at[s]).wait()
        for h in range(2):
            for i in range(count):
                at = h * size_half + i * part_rows
                to = s * line + h * part_rows
                gate_up[to:to + part_rows, i * LANES:(i + 1) * LANES] = packed[s, at:at + part_rows, :]
            for j in range(columns):
                at = h * size_half + count * part_rows + j * piece
                w_down[down_rows(s, h), j * LANES:(j + 1) * LANES] = packed[s, at:at + piece, :]
        block = slice(s * line, (s + 1) * line)
        for i in range(count):
            cols = slice(i * LANES, (i + 1) * LANES)
            product = dot(x[:, block], gate_up[block, cols])
            pre[:, cols] = product if s == 0 else pre[:, cols] + product

    stores = []

    def store_to(out, value):
        stores.append(pltpu.make_async_copy(value, out, store.at[len(stores)]))
        stores[-1].start()

    store_to(weight_outs[0], gate_up)
    store_to(weight_outs[1], w_down)
    step = 64 if rows % 64 == 0 else 16

    def activate(r, _):
        at = pl.ds(pl.multiple_of(r * step, 16), step)
        gate_pre, up_pre = pre[at, :units], pre[at, units:]
        sig = 1.0 / (1.0 + jnp.exp(-gate_pre))
        act = gate_pre * sig
        hidden[at, :] = (act * up_pre).astype(BF)
        pre[at, :units] = up_pre * sig * (1.0 + gate_pre * (1.0 - sig))
        pre[at, units:] = act
        return 0

    lax.fori_loop(0, rows // step, activate, 0)
    store_to(hidden_out, hidden)
    for copy in loads[2:]:
        copy.wait()
    d_hidden[...] = dot(grads[...], w_down[...], ((1,), (1,)))

    def differentiate(r, _):
        at = pl.ds(pl.multiple_of(r * step, 16), step)
        d_h = d_hidden[at, :]
        d_both[at, :units] = (d_h * pre[at, :units]).astype(BF)
        d_both[at, units:] = (d_h * pre[at, units:]).astype(BF)
        return 0

    lax.fori_loop(0, rows // step, differentiate, 0)
    store_to(d_both_out, d_both)
    d_down[...] = dot(hidden[...], grads[...], ((0,), (0,))).astype(BF)

    for k in (places - 1, 1, 2, 0):
        for h in range(2):
            from_cols = slice(k * line + h * part_rows, k * line + (h + 1) * part_rows)
            weights = dot(x[:, from_cols], d_both[...], ((0,), (0,))).astype(BF)
            for i in range(count):
                to = h * size_half + i * part_rows
                terms[k, to:to + part_rows, :] = weights[:, i * LANES:(i + 1) * LANES]
            for j in range(columns):
                to = h * size_half + count * part_rows + j * piece
                terms[k, to:to + piece, :] = d_down[down_rows(k, h), j * LANES:(j + 1) * LANES]
        store_to(outs[k], terms.at[k])
        if k == 1:
            store_to(outer_out, terms.at[jnp.where(z == 0, places - 1, 1)])
    for copy in stores:
        copy.wait()


def rows_kernel(chunks, *refs):
    keep, give = refs[-2:]
    slots = keep.shape[0]

    def add(pairs, dims):
        total = sum(dot(a[...], b[...], dims) for a, b in pairs).astype(BF)
        keep[...], give[...] = total[:slots], total[slots:]

    chunked = [refs[4 * n:4 * n + 4] for n in range(chunks)]

    @pl.when(pl.program_id(0) < pl.num_programs(0) // 2)
    def _():
        add([(hidden, w_down) for _, w_down, hidden, _ in chunked], ((1,), (0,)))

    @pl.when(pl.program_id(0) >= pl.num_programs(0) // 2)
    def _():
        add([(d_both, gate_up) for gate_up, _, _, d_both in chunked], ((1,), (1,)))


def in_vmem(count):
    return [pl.BlockSpec(memory_space=pltpu.VMEM)] * count


IN_SMEM = pl.BlockSpec(memory_space=pltpu.SMEM)


def pack(pieces, x, gate, up, down, shuffle):
    rows, hidden_width = gate.shape
    sizes = [(rows * hidden_width + down.size // 2) * piece // sum(pieces) // LANES for piece in pieces]
    return pl.pallas_call(
        functools.partial(pack_kernel, pieces),
        out_shape=[jax.ShapeDtypeStruct((size, LANES), BF) for size in sizes for _ in range(2)],
        in_specs=[IN_SMEM] + in_vmem(4),
        out_specs=in_vmem(2 * len(pieces)),
        compiler_params=pltpu.CompilerParams(vmem_limit_bytes=58 * MIB),
    )(x, gate, up, down, shuffle)


def unpack(pieces, x, packed, shuffle, gate_shape, down_shape):
    return pl.pallas_call(
        functools.partial(unpack_kernel, pieces),
        out_shape=[jax.ShapeDtypeStruct(shape, F32) for shape in (gate_shape, gate_shape, down_shape)],
        in_specs=[IN_SMEM] + in_vmem(len(packed) + 1),
        out_specs=in_vmem(3),
        compiler_params=pltpu.CompilerParams(vmem_limit_bytes=24 * MIB),
    )(x, *packed, shuffle)


def expert(z, places, units, weights, mine, theirs, vmem):
    size = weights[0].shape[0]
    slots, width = mine.shape[0], mine.shape[1] // 2
    rows = 2 * slots
    for_rows = [
        jax.ShapeDtypeStruct(shape, BF) for shape in ((width, 2 * units), (units, width), (rows, units), (rows, 2 * units))
    ]
    outs = pl.pallas_call(
        expert_kernel,
        out_shape=for_rows + [jax.ShapeDtypeStruct((size, LANES), BF)] * 5,
        in_specs=[IN_SMEM] + [pl.BlockSpec(memory_space=pl.ANY)] * 8,
        out_specs=[pl.BlockSpec(memory_space=pltpu.HBM)] * 9,
        scratch_shapes=[
            pltpu.VMEM((places, size, LANES), BF),
            pltpu.VMEM((rows, width), BF),
            pltpu.VMEM((rows, width), BF),
            pltpu.VMEM((width, 2 * units), BF),
            pltpu.VMEM((units, width), BF),
            pltpu.VMEM((rows, 2 * units), F32),
            pltpu.VMEM((rows, units), F32),
            pltpu.VMEM((rows, units), BF),
            pltpu.VMEM((rows, 2 * units), BF),
            pltpu.VMEM((units, width), BF),
            pltpu.VMEM((places, size, LANES), BF),
            pltpu.SemaphoreType.DMA((places + 4,)),
            pltpu.SemaphoreType.DMA((9,)),
        ],
        compiler_params=pltpu.CompilerParams(vmem_limit_bytes=vmem),
        cost_estimate=pl.CostEstimate(
            flops=12 * rows * width * units, bytes_accessed=4 * 2**20, transcendentals=rows * units
        ),
    )(z, *weights, mine, theirs)
    return outs[:4], outs[4], outs[5:]


def token_rows(chunks, slots, width):
    tile = 2 * LANES
    tiles = width // tile
    in_specs = []
    for gate_up, w_down, hidden, d_both in chunks:
        in_specs += [
            pl.BlockSpec((tile, gate_up.shape[1]), lambda n: (jnp.maximum(n - tiles, 0), 0)),
            pl.BlockSpec((w_down.shape[0], tile), lambda n: (0, jnp.minimum(n, tiles - 1))),
            pl.BlockSpec(hidden.shape, lambda n: (0, 0)),
            pl.BlockSpec(d_both.shape, lambda n: (0, 0)),
        ]
    units = sum(chunk[1].shape[0] for chunk in chunks)
    return pl.pallas_call(
        functools.partial(rows_kernel, len(chunks)),
        grid=(2 * tiles,),
        out_shape=[jax.ShapeDtypeStruct((slots, 2 * width), BF)] * 2,
        in_specs=in_specs,
        out_specs=[pl.BlockSpec((slots, tile), lambda n: (0, n))] * 2,
        compiler_params=pltpu.CompilerParams(vmem_limit_bytes=24 * MIB),
        cost_estimate=pl.CostEstimate(
            flops=12 * slots * width * units, bytes_accessed=2 * 2**20, transcendentals=0
        ),
    )(*(array for chunk in chunks for array in chunk))


def local(tokens, expert_ids, gate_probs, w_gate, w_up, w_down, d_out):
    g = Grid()
    rows, topk = expert_ids.shape
    width = tokens.shape[1]
    hidden_width = w_gate.shape[2]
    half = hidden_width // 2
    experts = g.experts
    cap = rows * topk * 9 // (8 * experts)
    slots = experts * cap
    first = g.c == 0
    even = g.x == 0

    block = hidden_width // g.dps
    part = block // 2
    pieces = (2 * part // 3, part // 3)
    in_kernels = g.zs == 4 and slots % 16 == 0 and part % 48 == 0 and all(2 * p * g.dps % LANES == 0 for p in pieces)
    if not in_kernels:
        pieces = (part,)
    shuffle = shuffle_matrix(g.x, g.dps, hidden_width, pieces)

    def out_a(z, x, q, c):
        return z, c, q, x

    def out_b(z, x, q, c):
        return z, c, q, 1 - x

    def back_a(z, x, q, c):
        return z, c, q, x

    def back_b(z, x, q, c):
        return z, 1 - c, q, x

    def spread(part_a, part_b):
        got_a, got_b = g.send(part_a, out_a), g.send(part_b, out_b)
        return jnp.concatenate([jnp.where(first, got_a, got_b), jnp.where(first, got_b, got_a)], axis=0)

    def unspread(both):
        n = both.shape[0] // 2
        low, high = both[:n], both[n:]
        return g.send(jnp.where(first, low, high), back_a), g.send(jnp.where(first, high, low), back_b)

    expert_iota = jnp.arange(experts, dtype=jnp.int32)
    chosen = expert_ids[:, :, None] == expert_iota
    named = jnp.any(chosen, axis=1).astype(BF)
    token_iota = jnp.arange(rows, dtype=jnp.int32)
    earlier = (token_iota[:, None] > token_iota[None, :]).astype(BF)
    before = dot(earlier, named)
    slot = jnp.sum(jnp.where(chosen, before[:, None, :], 0.0), axis=2).astype(jnp.int32)
    relative = ((expert_ids // 2 - g.q + g.qs) % g.qs) * 2 + ((expert_ids % 2) ^ g.x)
    dest = relative * cap + slot
    slot_iota = jnp.arange(slots, dtype=jnp.int32)
    pair = dest[:, :, None] == slot_iota
    placing = jnp.any(pair, axis=1).astype(BF)
    weighted = jnp.sum(jnp.where(pair, gate_probs[:, :, None], 0.0), axis=1)
    slot_probs = jnp.sum(weighted, axis=0)

    def member(r, sign):
        def move(z, x, q, c):
            return z, x ^ (r % 2), (q + sign * (r // 2)) % g.qs, c

        return move

    def other_core(z, x, q, c):
        return z, x, q, 1 - c

    def exchange(value, sign):
        got = [value[:cap]] + [g.send(value[r * cap:(r + 1) * cap], member(r, sign)) for r in range(1, experts)]
        return jnp.concatenate(got, axis=0)

    line_width = width // g.zs
    turned = lax.dynamic_slice(jnp.concatenate([tokens, tokens], axis=1), (0, g.z * line_width), (rows, width))
    sent = jnp.concatenate(
        [
            dot(placing, turned, ((0,), (0,))).astype(BF),
            (slot_probs[:, None] * dot(placing, d_out, ((0,), (0,)))).astype(BF),
        ],
        axis=1,
    )
    def combine(returned, back_rows):
        high = lax.reduce_precision(weighted, 8, 7)
        mixed = (dot(high.astype(BF), returned) + dot((weighted - high).astype(BF), returned)).astype(BF)
        products = dot(d_out, returned, ((1,), (1,)))
        d_probs = jnp.sum(jnp.where(pair, products[:, None, :], 0.0), axis=2)
        d_turned = dot(placing, back_rows).astype(BF)
        d_tokens = lax.dynamic_slice(
            jnp.concatenate([d_turned, d_turned], axis=1), (0, (g.zs - g.z) * line_width), (rows, width)
        )
        return mixed, d_tokens, d_probs

    shapes = w_gate.shape[1:], w_down.shape[1:]
    together = lax.optimization_barrier
    if in_kernels:
        place_x, place_z = g.x.reshape(1).astype(jnp.int32), g.z.reshape(1).astype(jnp.int32)
        units = [piece * g.dps for piece in pieces]
        a, b, a2, b2 = pack(pieces, place_x, w_gate[0], w_up[0], w_down[0], shuffle)
        ups, downs, passing = {0: 1, 1: 2, 2: 3}, {1: 0, 2: 1, 3: 2}, {2: 3, 1: 0}
        outward, inward_up, inward_down = {0: 1, 3: 2}, {0: 1, 1: 2}, {3: 2, 2: 1}
        to_last = g.z == 2

        shard, a2, b2 = together((spread(a, b), a2, b2))
        up, down = g.hop(shard, ups), g.hop(shard, downs)
        shard2, sent = together((spread(a2, b2), sent))
        up, down = together((up, down))
        far = g.hop(jnp.where(g.z == 1, up, down), {1: 3, 2: 0})
        up_2, down_2 = g.hop(up, {1: 2, 2: 3}), g.hop(down, {1: 0, 2: 1})
        mine = tie(exchange(sent, 1), far, up_2, down_2)
        theirs = g.send(mine, other_core)
        shard2 = tie(shard2, mine)
        up2, down2 = g.hop(shard2, ups), g.hop(shard2, downs)
        chunk, outer, terms = expert(place_z, g.zs, units[0], (shard, up, down, up_2, down_2, far), mine, theirs, 52 * MIB)
        begun = g.hop(outer, outward)
        up2, down2 = tie(up2, outer), tie(down2, outer)
        up2_2, down2_2 = g.hop(up2, {1: 2, 2: 3}), g.hop(down2, {1: 0, 2: 1})
        passed = jnp.where(to_last, up2_2, down2_2)
        last2 = g.hop(passed, passing)
        middle = added(terms[2], tie(begun, passed))
        sum_up, sum_down = g.hop(middle, inward_up), g.hop(middle, inward_down)
        chunk2, outer2, terms2 = expert(
            place_z, g.zs, units[1], (shard2, up2, down2, up2_2, down2_2, tie(last2, middle)), mine, theirs, 24 * MIB
        )
        keep, give = token_rows((chunk, chunk2), slots, width)
        sum_up, sum_down = tie(sum_up, keep, give), tie(sum_down, keep, give)
        sum_up, sum_down = added(terms[1], sum_up), added(terms[3], sum_down)
        give, outer2 = tie(give, sum_up, sum_down), tie(outer2, sum_up, sum_down)
        sums = added(keep, g.send(give, other_core)).reshape(g.qs, 2, cap, 2 * width)
        sum_up, sum_down = g.hop(sum_up, ups), g.hop(sum_down, downs)
        begun2 = g.hop(outer2, outward)
        far_rows = g.send(sums[:, 1], lambda z, x, q, c: (z, 1 - x, q, c))
        sum_up, sum_down, far_rows = together((sum_up, sum_down, far_rows))
        grad = added(terms[0], sum_up, sum_down)
        middle2 = added(terms2[2], begun2)
        sum_up2, sum_down2 = g.hop(middle2, inward_up), g.hop(middle2, inward_down)
        near = jnp.stack([sums[:, 0], far_rows], axis=1)
        got = jnp.concatenate(
            [near[0]] + [g.send(near[d], lambda z, x, q, c, d=d: (z, x, (q - d) % g.qs, c)) for d in range(1, g.qs)]
        ).reshape(slots, 2 * width)
        sum_up2, sum_down2 = tie(sum_up2, grad), tie(sum_down2, grad)
        sum_up2, sum_down2 = added(terms2[1], sum_up2), added(terms2[3], sum_down2)
        grads = unspread(tie(grad, sum_up2, sum_down2))
        sum_up2, sum_down2 = g.hop(sum_up2, ups), g.hop(sum_down2, downs)
        mixed, d_tokens, d_probs = combine(got[:, :width], got[:, width:])
        grads = tie_all(grads, sum_up2, sum_down2)
        grads += tie_all(unspread(added(terms2[0], sum_up2, sum_down2)), mixed, d_tokens, d_probs)
        d_w_gate, d_w_up, d_w_down = unpack(pieces, place_x, grads, shuffle, *shapes)
    else:
        gate_cols, up_cols = dot(w_gate[0], shuffle).astype(BF), dot(w_up[0], shuffle).astype(BF)
        gate_up_shard = spread(
            jnp.concatenate([gate_cols[:, :half], up_cols[:, :half]], axis=1),
            jnp.concatenate([gate_cols[:, half:], up_cols[:, half:]], axis=1),
        )
        down_low, down_high = w_down[0, :part], w_down[0, part:]
        down_shard = spread(jnp.where(even, down_low, down_high), jnp.where(even, down_high, down_low))
        gate_up = jnp.concatenate(g.line(gate_up_shard), axis=0)
        down = jnp.concatenate(g.straight(g.line(down_shard)), axis=0)
        mine = exchange(sent, 1)
        inputs = jnp.concatenate([mine, g.send(mine, other_core)], axis=0)
        arrived, d_produced = inputs[:, :width], inputs[:, width:]
        pre = dot(arrived, gate_up)
        gate_pre, up_pre = pre[:, :half], pre[:, half:]
        sig = jax.nn.sigmoid(gate_pre)
        act = gate_pre * sig
        hidden = (act * up_pre).astype(BF)
        d_hidden = dot(d_produced, down, ((1,), (1,)))
        d_gate = (d_hidden * up_pre * sig * (1.0 + gate_pre * (1.0 - sig))).astype(BF)
        d_up = (d_hidden * act).astype(BF)
        d_both = jnp.concatenate([d_gate, d_up], axis=1)
        down_part = dot(hidden, d_produced, ((0,), (0,))).astype(BF)
        both_part = dot(arrived, d_both, ((0,), (0,))).astype(BF)
        partial = jnp.concatenate([dot(hidden, down), dot(d_both, gate_up, ((1,), (1,)))], axis=1).astype(BF)
        got = exchange(added(partial[:slots], g.send(partial[slots:], other_core)), -1)
        down_a, down_b = unspread(
            g.line_sum(
                lambda k: lax.dynamic_slice_in_dim(down_part, ((g.z + k) % g.zs) * (2 * part), 2 * part)
            )
        )
        d_w_down = jnp.where(
            even, jnp.concatenate([down_a, down_b], axis=0), jnp.concatenate([down_b, down_a], axis=0)
        ).astype(F32)
        both_a, both_b = unspread(g.line_sum(lambda k: both_part[k * line_width:(k + 1) * line_width]))
        d_w_gate, d_w_up = (
            dot(jnp.concatenate([both_a[:, cols], both_b[:, cols]], axis=1), shuffle, ((1,), (1,)))
            for cols in (slice(0, half), slice(half, None))
        )
        mixed, d_tokens, d_probs = combine(got[:, :width], got[:, width:])
    return (mixed, d_tokens, d_probs, d_w_gate[None], d_w_up[None], d_w_down[None])


def solution(mesh):
    rows = P(("dp", "expert"), None)
    weight = P("expert", "dp", None)
    return jax.shard_map(
        local,
        mesh=mesh,
        in_specs=(rows, rows, rows, weight, weight, weight, rows),
        out_specs=(rows, rows, rows, weight, weight, weight),
        check_vma=False,
    )
```
